512 devices in a mesh: dp: 32 (over z_hi, x, core), space: 16 (over y, z_lo).
Axes of the slice: x: 4, y: 8, z: 8 (z_hi: 4, z_lo: 2; z = z_hi * 2 + z_lo), core: 2. Of those that a mesh axis runs over, the one named last changes fastest.
Arguments:
- wake_field: bfloat16 [32, 1, 48, 20, 2304], P('dp', None, 'space'), may hold values from -6 to 6
- spec_weight: bfloat16 [2, 20, 20, 6912], P(None, None, None, 'space'), may hold values from -1.25 to 1.25
- point_weight: bfloat16 [20, 20], replicated, may hold values from -1.25 to 1.25
- bias_term: float32 [20], replicated, may hold values from -3 to 3
- cotangent: bfloat16 [32, 1, 48, 20, 2304], P('dp', None, 'space'), may hold values from -6 to 6
Outputs:
- output_field: bfloat16 [32, 1, 48, 20, 2304], P('dp', None, 'space')
- grad_field: bfloat16 [32, 1, 48, 20, 2304], P('dp', None, 'space')
- grad_spec: float32 [2, 20, 20, 6912], P(None, None, None, 'space')
- grad_point: float32 [20, 20], replicated
- grad_bias: float32 [20], replicated
The draws below stay inside these ranges and needn't reach their ends.
All inputs are finite; a program needn't handle non-finite values.
Results may differ from the reference program's by a relative error of at most 0.001.
Values sent between devices are 32-bit elements; how exact they have to be, the bound alone decides.
A program may use at most 128 MiB of HBM per device.

```python
import jax
import jax.numpy as jnp
from jax import lax

C = 20
NX = 48
NY = 48
NZ = 48
MX = 12
MY = 12
MZ = 12
FRAMES = 1
CONFIGS = 32
MODES = 6912


def block_scale(rng, shape, pieces, least, largest):
    level = 1.0
    for dim, parts in pieces:
        steps = jax.random.uniform(jax.random.fold_in(jax.random.fold_in(rng, 6), dim), (parts,), jnp.float32, least / len(pieces), largest / len(pieces))
        level = level * jnp.repeat(jnp.exp(steps), shape[dim] // parts).reshape((-1,) + (1,) * (len(shape) - 1 - dim))
    return level


def noise(key, dims, spread, reach, split=(), kind=jnp.bfloat16):
    entries = jax.random.normal(key, dims, jnp.float32) * spread
    if len(split) > 0:
        entries = block_scale(key, dims, split, -0.22, 0.18) * entries
    return jnp.clip(entries, min=-reach, max=reach).astype(kind)


def setup_inputs(seed: int = 0) -> dict:
    keys = jax.random.split(jax.random.key(seed), 6)
    wake_field = noise(keys[0], (CONFIGS, FRAMES, NX, C, NY * NZ), 1.0, 6.0, ((0, 32), (2, 16)))
    spec_weight = noise(keys[1], (2, C, C, MODES), C ** -0.5, 1.25, ((3, 16),))
    point_weight = noise(keys[2], (C, C), C ** -0.5, 1.25)
    bias_term = noise(keys[3], (C,), 0.5, 3.0, (), jnp.float32)
    cotangent = noise(keys[4], (CONFIGS, FRAMES, NX, C, NY * NZ), 1.0, 6.0, ((0, 32), (2, 16)))
    return dict(wake_field=wake_field, spec_weight=spec_weight, point_weight=point_weight, bias_term=bias_term, cotangent=cotangent)


def spectral_part(values, weight_real, weight_imag):
    spectra = jnp.fft.rfft(values, axis=4, norm='ortho')[..., :MZ]
    spectra = jnp.fft.fft(spectra, axis=3, norm='ortho')
    spectra = jnp.concatenate([spectra[:, :, :, :MY], spectra[:, :, :, NY - MY:]], axis=3)
    spectra = jnp.fft.fft(spectra, axis=1, norm='ortho')
    spectra = jnp.concatenate([spectra[:, :MX], spectra[:, NX - MX:]], axis=1)
    modes = jnp.transpose(spectra, (0, 2, 3, 4, 1)).reshape(FRAMES, C, 2 * MY * MZ * 2 * MX)
    weight = weight_real + 1j * weight_imag
    mixed = jnp.einsum('tcm,com->tom', modes, weight)
    mixed = mixed.reshape(FRAMES, C, 2 * MY, MZ, 2 * MX).transpose(0, 4, 1, 2, 3)
    zeros_x = jnp.zeros((FRAMES, NX - 2 * MX, C, 2 * MY, MZ), mixed.dtype)
    full = jnp.concatenate([mixed[:, :MX], zeros_x, mixed[:, MX:]], axis=1)
    full = jnp.fft.ifft(full, axis=1, norm='ortho')
    zeros_y = jnp.zeros((FRAMES, NX, C, NY - 2 * MY, MZ), full.dtype)
    full = jnp.concatenate([full[:, :, :, :MY], zeros_y, full[:, :, :, MY:]], axis=3)
    full = jnp.fft.ifft(full, axis=3, norm='ortho')
    zeros_z = jnp.zeros((FRAMES, NX, C, NY, NZ // 2 + 1 - MZ), full.dtype)
    full = jnp.concatenate([full, zeros_z], axis=4)
    return jnp.fft.irfft(full, n=NZ, axis=4, norm='ortho')

def reference(wake_field, spec_weight, point_weight, bias_term, cotangent):
    weight_real = spec_weight[0].astype(jnp.float32)
    weight_imag = spec_weight[1].astype(jnp.float32)
    weight_point = point_weight.astype(jnp.float32)

    def pre_layer(values, wreal, wimag, wpoint, offsets):
        spatial = spectral_part(values, wreal, wimag)
        pointwise = jnp.einsum('txcyz,co->txoyz', values, wpoint, precision=lax.Precision.HIGHEST)
        return spatial + pointwise + offsets[None, None, :, None, None]

    def one_config(carry, inputs):
        field_one, cot_one = inputs
        values = field_one.astype(jnp.float32).reshape(FRAMES, NX, C, NY, NZ)
        pre, pre_back = jax.vjp(pre_layer, values, weight_real, weight_imag, weight_point, bias_term)
        activated, gelu_back = jax.vjp(jax.nn.gelu, pre)
        grad_pre = gelu_back(cot_one.astype(jnp.float32).reshape(pre.shape))[0]
        grad_values, grad_real, grad_imag, grad_wpoint, grad_offsets = pre_back(grad_pre)
        spec_acc, point_acc, bias_acc = carry
        carry = (spec_acc + jnp.stack([grad_real, grad_imag]), point_acc + grad_wpoint, bias_acc + grad_offsets)
        outputs = (activated.astype(jnp.bfloat16).reshape(field_one.shape), grad_values.astype(jnp.bfloat16).reshape(field_one.shape))
        return (carry, outputs)
    start = (jnp.zeros((2, C, C, MODES), jnp.float32), jnp.zeros((C, C), jnp.float32), jnp.zeros((C,), jnp.float32))
    totals, outputs = lax.scan(one_config, start, (wake_field, cotangent))
    return (outputs[0], outputs[1], totals[0], totals[1], totals[2])
```

```python
import functools
import math

import jax
import jax.numpy as jnp
import numpy as np
from jax import lax
from jax.experimental import pallas as pl
from jax.experimental.pallas import tpu as pltpu
from jax.sharding import PartitionSpec as P

MESH = pl.DeviceIdType.MESH
F32 = jnp.float32
BF16 = jnp.bfloat16

C = 20
N = 48
MZ = 12
CELLS = N * N
KX = 24
SLABS = 16
PLANES = 3
OWN = 18
MODES = OWN * KX
ROWS = 24
TALL = PLANES * ROWS
TILES = 6
WIDE = TILES * 128


def wave(i):
    return np.where(i < 12, i, i - 24)


def halves(table):
    high = table.astype(np.float32).astype(BF16)
    low = (table - high.astype(np.float64)).astype(np.float32).astype(BF16)
    return np.stack([high, low])


def yz_table():
    lane = np.arange(128)
    g, k, part, q6 = lane // 36, lane % 36 // 12, lane % 12 // 6, lane % 6
    owner = 3 * np.arange(TILES)[:, None] + k[None, :]
    used = (lane < 108)[None, :] & (owner < SLABS)
    q = OWN * owner + 6 * g[None, :] + q6[None, :]
    ky, kz = wave(q // MZ), q % MZ
    cell = np.arange(CELLS)
    y, z = cell // N, cell % N
    phase = (y[:, None, None] * ky[None] + z[:, None, None] * kz[None]) % N
    angle = 2.0 * np.pi * phase / N
    table = np.where(part == 0, np.cos(angle), -np.sin(angle)) / N
    return np.where(used[None], table, 0.0).reshape(CELLS, WIDE)


def x_table():
    lane = np.arange(128)
    k, p, part, q6 = lane // 36, lane % 36 // 12, lane % 12 // 6, lane % 6
    slab = 3 * np.arange(TILES)[:, None] + k[None, :]
    used = ((lane < 108)[None, :] & (slab < SLABS)).reshape(-1)
    x = (PLANES * slab + p[None, :]).reshape(-1)
    part, q6 = np.tile(part, TILES), np.tile(q6, TILES)
    column = np.arange(512)
    part_out, rest = column // 256, column % 256
    q6_out, i = rest // KX, rest % KX
    angle = 2.0 * np.pi * (x[:, None] * wave(i)[None, :] % N) / N
    cosine, sine = np.cos(angle), np.sin(angle)
    same = part[:, None] == part_out[None, :]
    table = np.where(same, cosine, np.where(part[:, None] == 1, sine, -sine)) / math.sqrt(N)
    keep = used[:, None] & (rest < 6 * KX)[None, :] & (q6[:, None] == q6_out[None, :])
    return np.where(keep, table, 0.0)


@functools.cache
def tables():
    yz, x = yz_table(), x_table()
    yz_two, x_two = halves(yz), halves(x)
    forward = np.ascontiguousarray(yz_two.reshape(2, CELLS, 3, 256).transpose(2, 0, 1, 3))
    inverse = np.ascontiguousarray(yz_two.transpose(0, 2, 1).reshape(2, WIDE, 9, 256).transpose(2, 0, 1, 3))
    x_inverse = np.ascontiguousarray(x_two.transpose(0, 2, 1))
    own = np.arange(512) // KX
    weight = np.stack([np.where((6 * parity + own) % MZ == 0, 1.0, 2.0) for parity in range(2)])
    weight = np.broadcast_to(weight[:, None, :], (2, 8, 512)).astype(np.float32)
    return forward, inverse, x_two, x_inverse, np.ascontiguousarray(weight)


def times(value, high, low):
    rows = value.shape[0]
    top = value.astype(BF16)
    wide = top.astype(F32)
    both = jnp.concatenate([wide, value - wide], axis=0).astype(BF16)
    first = jnp.dot(both, high, preferred_element_type=F32)
    return first[:rows] + first[rows:] + jnp.dot(top, low, preferred_element_type=F32)


def kernel(
    wake_hbm, cot_hbm, weight_hbm, small, kz_weight, fwd_hbm, inv_hbm, x_hbm, xt_hbm,
    out_hbm, grad_hbm, spec_hbm, sums_ref,
    wake, cot, weight, fwd, inv, xf, xt,
    values, spectra, slab, grads, lined, pieces, modes, mixed, grad_modes,
    send, recv, all_modes, all_grads, partial, landed, gathered, sums8, sums4,
    out_vmem, grad_vmem,
    load_sem, store_sem, send_sem, recv_sem, dp_send, dp_recv,
):
    dp = lax.axis_index("dp")
    me = lax.axis_index("space")
    z_hi, eight = dp // 8, dp % 8
    x_pos, core = eight // 2, eight % 2
    lane = lax.broadcasted_iota(jnp.int32, (C, 128), 1)
    third = lane // 36
    slot = jnp.where(lane < 108, lane % 36 // 12, 3)

    loads = [
        pltpu.make_async_copy(wake_hbm, wake, load_sem.at[0]),
        pltpu.make_async_copy(fwd_hbm.at[0], fwd.at[0], load_sem.at[1]),
        pltpu.make_async_copy(fwd_hbm.at[1], fwd.at[1], load_sem.at[2]),
        pltpu.make_async_copy(fwd_hbm.at[2], fwd.at[2], load_sem.at[3]),
        pltpu.make_async_copy(x_hbm, xf, load_sem.at[4]),
        pltpu.make_async_copy(weight_hbm, weight, load_sem.at[5]),
        pltpu.make_async_copy(xt_hbm, xt, load_sem.at[6]),
        pltpu.make_async_copy(inv_hbm, inv, load_sem.at[7]),
        pltpu.make_async_copy(cot_hbm, cot, load_sem.at[8]),
    ]
    for load in loads:
        load.start()

    barrier = pltpu.get_barrier_semaphore()
    for r in range(1, 16):
        pl.semaphore_signal(barrier, inc=1, device_id=(dp, (me + r) % 16), device_id_type=MESH)
    for r in range(1, 8):
        peer = z_hi * 8 + (eight + r) % 8
        pl.semaphore_signal(barrier, inc=1, device_id=(peer, me), device_id_type=MESH)
    for r in range(1, 4):
        peer = (z_hi + r) % 4 * 8 + eight
        pl.semaphore_signal(barrier, inc=1, device_id=(peer, me), device_id_type=MESH)

    values[...] = jnp.zeros((TALL, CELLS), F32)
    lined[...] = jnp.zeros((TALL, WIDE), F32)
    pieces[...] = jnp.zeros((TALL, 512), F32)
    mixed[...] = jnp.zeros((2, C, 512), F32)
    loads[0].wait()
    for p in range(PLANES):
        values[ROWS * p : ROWS * p + C, :] = wake[0, 0, p].astype(F32)

    def space_copy(phase, r):
        to = (me + r) % 16
        return pltpu.make_async_remote_copy(
            src_ref=send.at[phase, to], dst_ref=recv.at[phase, me],
            send_sem=send_sem.at[phase, r], recv_sem=recv_sem.at[phase, r],
            device_id=(dp, to), device_id_type=MESH,
        )

    def space_start(phase):
        for r in range(1, 16):
            space_copy(phase, r).start()
        recv[phase, me] = send[phase, me]

    def space_wait(phase):
        for r in range(1, 16):
            space_copy(phase, r).wait()

    def turn(value, shift):
        shift %= 128
        return value if shift == 0 else pltpu.roll(value, shift, 1)

    def choose(where, parts):
        total = jnp.zeros((C, 128), F32)
        for index, part in parts:
            total = jnp.where(where == index, part, total)
        return total

    def slab_to_owners(phase, ride):
        for t in range(TILES):
            held = [spectra[ROWS * p : ROWS * p + C, 128 * t : 128 * t + 128] for p in range(PLANES)]
            for k in range(3):
                if 3 * t + k < SLABS:
                    message = choose(slot, [(p, turn(held[p], 12 * (p - k))) for p in range(PLANES)])
                    send[phase, 3 * t + k] = message if ride is None else message + ride

    def owners_to_slab(phase):
        for t in range(TILES):
            ks = [k for k in range(3) if 3 * t + k < SLABS]
            held = [recv[phase, 3 * t + k] for k in ks]
            for p in range(PLANES):
                lined[ROWS * p : ROWS * p + C, 128 * t : 128 * t + 128] = choose(
                    slot, [(k, turn(held[k], 12 * (k - p))) for k in ks]
                )

    def line_up_planes(phase):
        for u in range(TILES):
            ks = [k for k in range(3) if 3 * u + k < SLABS]
            held = [recv[phase, 3 * u + k] for k in ks]
            for g in range(3):
                lined[ROWS * g : ROWS * g + C, 128 * u : 128 * u + 128] = choose(
                    third, [(k, turn(held[k], 36 * (k - g))) for k in ks]
                )

    def planes_to_slabs(phase, ride):
        for u in range(TILES):
            held = [slab[ROWS * g : ROWS * g + C, 128 * u : 128 * u + 128] for g in range(3)]
            for k in range(3):
                if 3 * u + k < SLABS:
                    message = choose(third, [(g, turn(held[g], 36 * (g - k))) for g in range(3)])
                    send[phase, 3 * u + k] = message if ride is None else message + ride

    def along_x(target, scale):
        result = times(lined[...], xf[0], xf[1])
        for part in range(2):
            block = [result[ROWS * g : ROWS * g + ROWS, 256 * part : 256 * part + 256] for g in range(3)]
            second, last = pltpu.roll(block[1], 16, 1), pltpu.roll(block[2], 32, 1)
            strips = [
                block[0][:, :128],
                block[0][:, 128:] + second[:, :128],
                second[:, 128:] + last[:, :128],
                last[:, 128:],
            ]
            for j in range(4):
                strip = strips[j][:C]
                if scale is not None:
                    strip = strip * scale[:, 128 * j : 128 * j + 128]
                target[part, :, 128 * j : 128 * j + 128] = strip

    def back_along_x():
        for part in range(2):
            full = mixed[part]
            pieces[0:C, 256 * part : 256 * part + 256] = full[:, :256]
            pieces[ROWS : ROWS + C, 256 * part : 256 * part + 256] = pltpu.roll(full, 512 - 144, 1)[:, :256]
            pieces[2 * ROWS : 2 * ROWS + C, 256 * part : 256 * part + 256] = pltpu.roll(full, 512 - 288, 1)[:, :256]
        slab[...] = times(pieces[...], xt[0], xt[1])

    def gather_copy(kind, source, target, r):
        to = (eight + r) % 8
        return pltpu.make_async_remote_copy(
            src_ref=source.at[:, :, pl.ds(pl.multiple_of(to // 2 * 128, 128), 128)],
            dst_ref=target.at[eight],
            send_sem=dp_send.at[kind, r], recv_sem=dp_recv.at[kind, r],
            device_id=(z_hi * 8 + to, me), device_id_type=MESH,
        )

    def gather_start(kind, source, target):
        for r in range(1, 8):
            gather_copy(kind, source, target, r).start()
        target[eight] = source[:, :, pl.ds(pl.multiple_of(x_pos * 128, 128), 128)]

    tall = values[...].astype(BF16)
    for n in range(3):
        loads[1 + n].wait()
        spectra[:, 256 * n : 256 * n + 256] = jnp.dot(
            tall, fwd[n, 0], preferred_element_type=F32
        ) + jnp.dot(tall, fwd[n, 1], preferred_element_type=F32)
    slab_to_owners(0, None)
    pl.semaphore_wait(barrier, 25)
    space_start(0)
    for load in loads[4:]:
        load.wait()
    space_wait(0)
    line_up_planes(0)
    along_x(modes, None)
    gather_start(0, modes, all_modes)

    row = kz_weight[me % 2, 0:1, :]

    def mix_step(c, carry):
        real, imag = carry
        w_real, w_imag = weight[0, c].astype(F32), weight[1, c].astype(F32)
        m_real, m_imag = modes[0, pl.ds(c, 1), :MODES], modes[1, pl.ds(c, 1), :MODES]
        real = real + w_real * m_real - w_imag * m_imag
        imag = imag + w_real * m_imag + w_imag * m_real
        return real, imag

    nothing = jnp.zeros((C, MODES), F32)
    real, imag = lax.fori_loop(0, C, mix_step, (nothing, nothing))
    mixed[0, :, :MODES] = real * row[:, :MODES]
    mixed[1, :, :MODES] = imag * row[:, :MODES]
    back_along_x()
    planes_to_slabs(1, None)
    space_start(1)

    def diagonal(matrix):
        return jnp.concatenate([turn(matrix, ROWS * p) for p in range(PLANES)], axis=0)[:, :TALL].astype(BF16)

    to_out, to_in = diagonal(small[0]), diagonal(small[1])
    bias = jnp.concatenate([small[2]] * PLANES, axis=0)[:, 0:1]
    channel = lax.broadcasted_iota(jnp.int32, (TALL, 256), 0) % ROWS
    space_wait(1)
    owners_to_slab(1)

    full = lined[...]
    rate = math.sqrt(2.0 / math.pi)
    bias_sum = jnp.zeros((TALL, 1), F32)
    for n in range(9):
        columns = slice(256 * n, 256 * n + 256)
        pre = times(full, inv[n, 0], inv[n, 1])
        pre = pre + jnp.dot(to_out, values[:, columns].astype(BF16), preferred_element_type=F32) + bias
        square = pre * pre
        bend = jnp.tanh(rate * (pre + 0.044715 * (square * pre)))
        half = 0.5 * (1.0 + bend)
        slope = half + 0.5 * pre * (1.0 - bend * bend) * (rate * (1.0 + 3 * 0.044715 * square))
        active = half * pre
        for p in range(PLANES):
            out_vmem[0, 0, p, :, columns] = active[ROWS * p : ROWS * p + C].astype(BF16)
            grads[ROWS * p : ROWS * p + C, columns] = slope[ROWS * p : ROWS * p + C] * cot[0, 0, p, :, columns].astype(F32)
            grads[ROWS * p + C : ROWS * p + ROWS, columns] = jnp.zeros((ROWS - C, 256), F32)
        bias_sum = bias_sum + jnp.sum(grads[:, columns], axis=1, keepdims=True)
    store_out = pltpu.make_async_copy(out_vmem, out_hbm, store_sem.at[0])
    store_out.start()

    full = grads[...]
    for n in range(3):
        spectra[:, 256 * n : 256 * n + 256] = times(full, fwd[n, 0], fwd[n, 1])
    bias_own = bias_sum[:C] + bias_sum[ROWS : ROWS + C] + bias_sum[2 * ROWS : 2 * ROWS + C]
    slab_to_owners(2, jnp.where(lane == 108, bias_own, 0.0))
    space_start(2)

    point = jnp.zeros((ROWS, ROWS), F32)
    last = (((1,), (1,)), ((), ()))
    for p in range(PLANES):
        field = values[ROWS * p : ROWS * p + ROWS, :].astype(BF16)
        slope = grads[ROWS * p : ROWS * p + ROWS, :]
        high = slope.astype(BF16)
        low = (slope - high.astype(F32)).astype(BF16)
        point = point + lax.dot_general(field, high, last, preferred_element_type=F32)
        point = point + lax.dot_general(field, low, last, preferred_element_type=F32)
    point = jnp.concatenate([point[:C], jnp.zeros((C, 128 - ROWS), F32)], axis=1)
    point = jnp.where(lane >= 108, turn(point, 108), 0.0)
    for n in range(9):
        columns = slice(256 * n, 256 * n + 256)
        slope = grads[:, columns]
        high = slope.astype(BF16)
        low = (slope - high.astype(F32)).astype(BF16)
        values[:, columns] = jnp.dot(to_in, high, preferred_element_type=F32) + jnp.dot(
            to_in, low, preferred_element_type=F32
        )

    space_wait(2)
    line_up_planes(2)
    along_x(grad_modes, row)
    gather_start(1, grad_modes, all_grads)

    def grad_step(c, carry):
        w_real, w_imag = weight[0, c].astype(F32), weight[1, c].astype(F32)
        g_real, g_imag = grad_modes[0, :, :MODES], grad_modes[1, :, :MODES]
        mixed[0, pl.ds(c, 1), :MODES] = jnp.sum(w_real * g_real + w_imag * g_imag, axis=0, keepdims=True)
        mixed[1, pl.ds(c, 1), :MODES] = jnp.sum(w_real * g_imag - w_imag * g_real, axis=0, keepdims=True)
        return carry

    lax.fori_loop(0, C, grad_step, 0)
    back_along_x()
    planes_to_slabs(3, point)
    space_start(3)

    for r in range(1, 8):
        gather_copy(0, modes, all_modes, r).wait()
        gather_copy(1, grad_modes, all_grads, r).wait()

    def part_step(c, carry):
        total = jnp.zeros((C, 128), F32)
        for b in range(8):
            g_real, g_imag = all_grads[b, 0], all_grads[b, 1]
            first = jnp.where(core == 0, g_real, g_imag)
            second = jnp.where(core == 0, g_imag, -g_real)
            total = total + all_modes[b, 0, pl.ds(c, 1), :] * first + all_modes[b, 1, pl.ds(c, 1), :] * second
        partial[c] = total
        return carry

    lax.fori_loop(0, C, part_step, 0)

    def scatter_copy(r):
        to = (z_hi + r) % 4
        return pltpu.make_async_remote_copy(
            src_ref=partial.at[pl.ds(to * 5, 5)], dst_ref=landed.at[r - 1],
            send_sem=dp_send.at[2, r], recv_sem=dp_recv.at[2, r],
            device_id=(to * 8 + eight, me), device_id_type=MESH,
        )

    for r in range(1, 4):
        scatter_copy(r).start()

    bias_total = jnp.zeros((C, 128), F32)
    for s in range(SLABS):
        bias_total = bias_total + recv[2, s]
    space_wait(3)
    owners_to_slab(3)
    point_total = jnp.zeros((C, 128), F32)
    for s in range(SLABS):
        point_total = point_total + recv[3, s]
    small_sum = jnp.where(lane >= 108, point_total, jnp.where(lane == 0, turn(bias_total, 20), 0.0))
    sums8[eight] = small_sum

    def eight_copy(r):
        to = (eight + r) % 8
        return pltpu.make_async_remote_copy(
            src_ref=sums8.at[eight], dst_ref=sums8.at[eight],
            send_sem=dp_send.at[3, r], recv_sem=dp_recv.at[3, r],
            device_id=(z_hi * 8 + to, me), device_id_type=MESH,
        )

    for r in range(1, 8):
        eight_copy(r).start()

    for r in range(1, 4):
        scatter_copy(r).wait()
    for j in range(5):
        gathered[x_pos, core, z_hi * 5 + j] = (
            partial[z_hi * 5 + j] + landed[0, j] + landed[1, j] + landed[2, j]
        )

    def z_copy(r):
        to = (z_hi + r) % 4
        block = gathered.at[x_pos, core, pl.ds(z_hi * 5, 5)]
        return pltpu.make_async_remote_copy(
            src_ref=block, dst_ref=block,
            send_sem=dp_send.at[4, r], recv_sem=dp_recv.at[4, r],
            device_id=(to * 8 + eight, me), device_id_type=MESH,
        )

    for r in range(1, 4):
        z_copy(r).start()

    full = lined[...]
    for n in range(9):
        columns = slice(256 * n, 256 * n + 256)
        result = times(full, inv[n, 0], inv[n, 1]) + values[:, columns]
        for p in range(PLANES):
            grad_vmem[0, 0, p, :, columns] = result[ROWS * p : ROWS * p + C].astype(BF16)
    store_grad = pltpu.make_async_copy(grad_vmem, grad_hbm, store_sem.at[1])
    store_grad.start()

    for r in range(1, 8):
        eight_copy(r).wait()
    total = sums8[0]
    for b in range(1, 8):
        total = total + sums8[b]
    sums4[z_hi] = total

    def four_copy(r):
        to = (z_hi + r) % 4
        return pltpu.make_async_remote_copy(
            src_ref=sums4.at[z_hi], dst_ref=sums4.at[z_hi],
            send_sem=dp_send.at[5, r], recv_sem=dp_recv.at[5, r],
            device_id=(to * 8 + eight, me), device_id_type=MESH,
        )

    for r in range(1, 4):
        four_copy(r).start()

    for r in range(1, 4):
        z_copy(r).wait()

    def x_copy(r):
        to = (x_pos + r) % 4
        block = gathered.at[x_pos, core]
        return pltpu.make_async_remote_copy(
            src_ref=block, dst_ref=block,
            send_sem=dp_send.at[6, r], recv_sem=dp_recv.at[6, r],
            device_id=(z_hi * 8 + to * 2 + core, me), device_id_type=MESH,
        )

    def core_copy(r):
        block = gathered.at[(x_pos - r) % 4, core]
        return pltpu.make_async_remote_copy(
            src_ref=block, dst_ref=block,
            send_sem=dp_send.at[7, r], recv_sem=dp_recv.at[7, r],
            device_id=(z_hi * 8 + x_pos * 2 + 1 - core, me), device_id_type=MESH,
        )

    def strip_store(r, part):
        strip = (x_pos - r) % 4
        return pltpu.make_async_copy(
            gathered.at[strip, part],
            spec_hbm.at[part, :, :, pl.ds(pl.multiple_of(strip * 128, 128), 128)],
            store_sem.at[2 + 2 * r + (part != core).astype(jnp.int32)],
        )

    for r in range(1, 4):
        x_copy(r).start()
    core_copy(0).start()
    strip_store(0, core).start()
    for r in (1, 3, 2):
        x_copy(r).wait_recv()
        core_copy(r).start()
        strip_store(r, core).start()
    for r in range(1, 4):
        four_copy(r).wait()
    sums_ref[...] = sums4[0] + sums4[1] + sums4[2] + sums4[3]
    for r in (0, 1, 3, 2):
        core_copy(r).wait()
        strip_store(r, 1 - core).start()
    for r in range(1, 4):
        x_copy(r).wait_send()
    for r in range(4):
        strip_store(r, core).wait()
        strip_store(r, 1 - core).wait()
    store_out.wait()
    store_grad.wait()


def on_device(wake_field, spec_weight, point_weight, bias_term, cotangent):
    forward, inverse, x_two, x_inverse, kz_weight = tables()
    matrix = point_weight.astype(F32)
    small = jnp.stack([
        jnp.pad(matrix.T, ((0, ROWS - C), (0, 128 - C))),
        jnp.pad(matrix, ((0, ROWS - C), (0, 128 - C))),
        jnp.pad(jnp.broadcast_to(bias_term[:, None], (C, 128)), ((0, ROWS - C), (0, 0))),
    ])
    anywhere = pl.BlockSpec(memory_space=pl.ANY)
    inside = pl.BlockSpec(memory_space=pltpu.VMEM)
    field = wake_field.shape
    output_field, grad_field, grad_spec, sums = pl.pallas_call(
        kernel,
        out_shape=(
            jax.ShapeDtypeStruct(field, BF16),
            jax.ShapeDtypeStruct(field, BF16),
            jax.ShapeDtypeStruct((2, C, C, 512), F32),
            jax.ShapeDtypeStruct((C, 128), F32),
        ),
        in_specs=[anywhere, anywhere, anywhere, inside, inside, anywhere, anywhere, anywhere, anywhere],
        out_specs=(anywhere, anywhere, anywhere, inside),
        scratch_shapes=[
            pltpu.VMEM(field, BF16),
            pltpu.VMEM(field, BF16),
            pltpu.VMEM(spec_weight.shape, BF16),
            pltpu.VMEM(forward.shape, BF16),
            pltpu.VMEM(inverse.shape, BF16),
            pltpu.VMEM(x_two.shape, BF16),
            pltpu.VMEM(x_inverse.shape, BF16),
            pltpu.VMEM((TALL, CELLS), F32),
            pltpu.VMEM((TALL, WIDE), F32),
            pltpu.VMEM((TALL, WIDE), F32),
            pltpu.VMEM((TALL, CELLS), F32),
            pltpu.VMEM((TALL, WIDE), F32),
            pltpu.VMEM((TALL, 512), F32),
            pltpu.VMEM((2, C, 512), F32),
            pltpu.VMEM((2, C, 512), F32),
            pltpu.VMEM((2, C, 512), F32),
            pltpu.VMEM((4, SLABS, C, 128), F32),
            pltpu.VMEM((4, SLABS, C, 128), F32),
            pltpu.VMEM((8, 2, C, 128), F32),
            pltpu.VMEM((8, 2, C, 128), F32),
            pltpu.VMEM((C, C, 128), F32),
            pltpu.VMEM((3, 5, C, 128), F32),
            pltpu.VMEM((4, 2, C, C, 128), F32),
            pltpu.VMEM((8, C, 128), F32),
            pltpu.VMEM((4, C, 128), F32),
            pltpu.VMEM(field, BF16),
            pltpu.VMEM(field, BF16),
            pltpu.SemaphoreType.DMA((9,)),
            pltpu.SemaphoreType.DMA((10,)),
            pltpu.SemaphoreType.DMA((4, 16)),
            pltpu.SemaphoreType.DMA((4, 16)),
            pltpu.SemaphoreType.DMA((8, 8)),
            pltpu.SemaphoreType.DMA((8, 8)),
        ],
        compiler_params=pltpu.CompilerParams(
            collective_id=0, has_side_effects=True, vmem_limit_bytes=56 * 1024 * 1024
        ),
    )(wake_field, cotangent, spec_weight, small, kz_weight, forward, inverse, x_two, x_inverse)
    return (
        output_field,
        grad_field,
        grad_spec[..., :MODES],
        sums[:, 108:128],
        sums[:, 0],
    )


def solution(mesh):
    placed = (
        P("dp", None, "space", None, None),
        P(None, None, None, "space"),
        P(),
        P(),
        P("dp", None, "space", None, None),
    )
    return jax.shard_map(
        on_device,
        mesh=mesh,
        in_specs=placed,
        out_specs=(
            P("dp", None, "space", None, None),
            P("dp", None, "space", None, None),
            P(None, None, None, "space"),
            P(),
            P(),
        ),
        check_vma=False,
    )
```

```python
import functools
import math

import jax
import jax.numpy as jnp
import numpy as np
from jax import lax
from jax.experimental import pallas as pl
from jax.experimental.pallas import tpu as pltpu
from jax.sharding import PartitionSpec as P

MESH = pl.DeviceIdType.MESH
F32 = jnp.float32
BF16 = jnp.bfloat16

C = 20
N = 48
MZ = 12
CELLS = N * N
KX = 24
SLABS = 16
PLANES = 3
OWN = 18
MODES = OWN * KX
ROWS = 24
TALL = PLANES * ROWS
TILES = 6
WIDE = TILES * 128
PAIRS = 2 * C


def wave(i):
    return np.where(i < 12, i, i - 24)


def halves(table):
    high = table.astype(np.float32).astype(BF16)
    low = (table - high.astype(np.float64)).astype(np.float32).astype(BF16)
    return np.stack([high, low])


def yz_table():
    lane = np.arange(128)
    g, k, part, q6 = lane // 36, lane % 36 // 12, lane % 12 // 6, lane % 6
    owner = 3 * np.arange(TILES)[:, None] + k[None, :]
    used = (lane < 108)[None, :] & (owner < SLABS)
    q = OWN * owner + 6 * g[None, :] + q6[None, :]
    ky, kz = wave(q // MZ), q % MZ
    cell = np.arange(CELLS)
    y, z = cell // N, cell % N
    phase = (y[:, None, None] * ky[None] + z[:, None, None] * kz[None]) % N
    angle = 2.0 * np.pi * phase / N
    table = np.where(part == 0, np.cos(angle), -np.sin(angle)) / N
    return np.where(used[None], table, 0.0).reshape(CELLS, WIDE)


def x_table():
    lane = np.arange(128)
    k, p, part, q6 = lane // 36, lane % 36 // 12, lane % 12 // 6, lane % 6
    slab = 3 * np.arange(TILES)[:, None] + k[None, :]
    used = ((lane < 108)[None, :] & (slab < SLABS)).reshape(-1)
    x = (PLANES * slab + p[None, :]).reshape(-1)
    part, q6 = np.tile(part, TILES), np.tile(q6, TILES)
    column = np.arange(512)
    part_out, rest = column // 256, column % 256
    q6_out, i = rest // KX, rest % KX
    angle = 2.0 * np.pi * (x[:, None] * wave(i)[None, :] % N) / N
    cosine, sine = np.cos(angle), np.sin(angle)
    same = part[:, None] == part_out[None, :]
    table = np.where(same, cosine, np.where(part[:, None] == 1, sine, -sine)) / math.sqrt(N)
    keep = used[:, None] & (rest < 6 * KX)[None, :] & (q6[:, None] == q6_out[None, :])
    return np.where(keep, table, 0.0)


@functools.cache
def tables():
    yz, x = yz_table(), x_table()
    yz_two, x_two = halves(yz), halves(x)
    forward = np.ascontiguousarray(yz_two.reshape(2, CELLS, 3, 256).transpose(2, 0, 1, 3))
    inverse = np.ascontiguousarray(yz_two.transpose(0, 2, 1).reshape(2, WIDE, 9, 256).transpose(2, 0, 1, 3))
    x_inverse = np.ascontiguousarray(x_two.transpose(0, 2, 1))
    own = np.arange(512) // KX
    weight = np.stack([np.where((6 * parity + own) % MZ == 0, 1.0, 2.0) for parity in range(2)])
    weight = np.broadcast_to(weight[:, None, :], (2, 8, 512)).astype(np.float32)
    return forward, inverse, x_two, x_inverse, np.ascontiguousarray(weight)


def times(value, high, low):
    rows = value.shape[0]
    top = value.astype(BF16)
    wide = top.astype(F32)
    both = jnp.concatenate([wide, value - wide], axis=0).astype(BF16)
    first = jnp.dot(both, high, preferred_element_type=F32)
    return first[:rows] + first[rows:] + jnp.dot(top, low, preferred_element_type=F32)


def kernel(
    wake_hbm, cot_hbm, weight_hbm, point_weight, bias_term, kz_weight, fwd_hbm, inv_hbm, x_hbm, xt_hbm,
    out_hbm, grad_hbm, spec_hbm, sums_ref,
    wake, cot, weight, fwd, inv, xf, xt,
    values, slopes, maps, spectra, slab, grads, lined, pieces, modes, mixed, grad_modes, matrix,
    send, recv, all_modes, all_grads, partial, landed, gathered, sums8, sums4,
    out_vmem, grad_vmem,
    load_sem, store_sem, spec_sem, send_sem, recv_sem, dp_send, dp_recv, x_send, x_recv,
):
    dp = lax.axis_index("dp")
    me = lax.axis_index("space")
    z_hi, eight = dp // 8, dp % 8
    x_pos, core = eight // 2, eight % 2
    lane = lax.broadcasted_iota(jnp.int32, (C, 128), 1)
    third = lane // 36
    slot = jnp.where(lane < 108, lane % 36 // 12, 3)
    even = lax.broadcasted_iota(jnp.int32, (PAIRS, 128), 0) % 2 == 0

    loads = [
        pltpu.make_async_copy(wake_hbm, wake, load_sem.at[0]),
        pltpu.make_async_copy(fwd_hbm.at[0], fwd.at[0], load_sem.at[1]),
        pltpu.make_async_copy(fwd_hbm.at[1], fwd.at[1], load_sem.at[2]),
        pltpu.make_async_copy(fwd_hbm.at[2], fwd.at[2], load_sem.at[3]),
        pltpu.make_async_copy(weight_hbm, weight, load_sem.at[4]),
        pltpu.make_async_copy(cot_hbm, cot, load_sem.at[5]),
        pltpu.make_async_copy(x_hbm, xf, load_sem.at[6]),
        pltpu.make_async_copy(xt_hbm, xt, load_sem.at[7]),
        pltpu.make_async_copy(inv_hbm, inv, load_sem.at[8]),
    ]
    for load in loads[:4]:
        load.start()

    barrier = pltpu.get_barrier_semaphore()
    for r in range(1, 16):
        pl.semaphore_signal(barrier, inc=1, device_id=(dp, (me + r) % 16), device_id_type=MESH)
    for r in range(1, 8):
        peer = z_hi * 8 + (eight + r) % 8
        pl.semaphore_signal(barrier, inc=1, device_id=(peer, me), device_id_type=MESH)
    for r in range(1, 4):
        peer = (z_hi + r) % 4 * 8 + eight
        pl.semaphore_signal(barrier, inc=1, device_id=(peer, me), device_id_type=MESH)

    values[...] = jnp.zeros((TALL, CELLS), F32)
    lined[...] = jnp.zeros((TALL, WIDE), F32)
    loads[0].wait()
    for p in range(PLANES):
        values[ROWS * p : ROWS * p + C, :] = wake[0, 0, p].astype(F32)

    def space_copy(phase, r):
        to = (me + r) % 16
        return pltpu.make_async_remote_copy(
            src_ref=send.at[phase, to], dst_ref=recv.at[phase, me],
            send_sem=send_sem.at[phase, r], recv_sem=recv_sem.at[phase, r],
            device_id=(dp, to), device_id_type=MESH,
        )

    def space_start(phase):
        for r in range(1, 16):
            space_copy(phase, r).start()
        recv[phase, me] = send[phase, me]

    def space_wait(phase):
        for r in range(1, 16):
            space_copy(phase, r).wait()

    def turn(value, shift):
        shift %= 128
        return value if shift == 0 else pltpu.roll(value, shift, 1)

    def other(value):
        return jnp.where(even, pltpu.roll(value, PAIRS - 1, 0), -pltpu.roll(value, 1, 0))

    def choose(where, parts):
        total = jnp.zeros((C, 128), F32)
        for index, part in parts:
            total = jnp.where(where == index, part, total)
        return total

    def slab_to_owners(phase, ride):
        for t in range(TILES):
            held = [spectra[ROWS * p : ROWS * p + C, 128 * t : 128 * t + 128] for p in range(PLANES)]
            for k in range(3):
                if 3 * t + k < SLABS:
                    message = choose(slot, [(p, turn(held[p], 12 * (p - k))) for p in range(PLANES)])
                    send[phase, 3 * t + k] = message if ride is None else message + ride

    def owners_to_slab(phase):
        for t in range(TILES):
            ks = [k for k in range(3) if 3 * t + k < SLABS]
            held = [recv[phase, 3 * t + k] for k in ks]
            for p in range(PLANES):
                lined[ROWS * p : ROWS * p + C, 128 * t : 128 * t + 128] = choose(
                    slot, [(k, turn(held[k], 12 * (k - p))) for k in ks]
                )

    def line_up_planes(phase):
        for u in range(TILES):
            ks = [k for k in range(3) if 3 * u + k < SLABS]
            held = [recv[phase, 3 * u + k] for k in ks]
            for g in range(3):
                lined[ROWS * g : ROWS * g + C, 128 * u : 128 * u + 128] = choose(
                    third, [(k, turn(held[k], 36 * (k - g))) for k in ks]
                )

    def planes_to_slabs(phase, ride):
        for u in range(TILES):
            held = [slab[ROWS * g : ROWS * g + C, 128 * u : 128 * u + 128] for g in range(3)]
            for k in range(3):
                if 3 * u + k < SLABS:
                    message = choose(third, [(g, turn(held[g], 36 * (g - k))) for g in range(3)])
                    send[phase, 3 * u + k] = message if ride is None else message + ride

    def along_x(target, scale):
        result = times(lined[...], xf[0], xf[1])
        for part in range(2):
            block = [result[ROWS * g : ROWS * g + ROWS, 256 * part : 256 * part + 256] for g in range(3)]
            second, last = pltpu.roll(block[1], 16, 1), pltpu.roll(block[2], 32, 1)
            strips = [
                block[0][:, :128],
                block[0][:, 128:] + second[:, :128],
                second[:, 128:] + last[:, :128],
                last[:, 128:],
            ]
            for j in range(4):
                strip = strips[j][:C]
                if scale is not None:
                    strip = strip * scale[:, 128 * j : 128 * j + 128]
                target[j, pl.ds(part, C, stride=2), :] = strip

    def back_along_x():
        for part in range(2):
            strips = [mixed[j, pl.ds(part, C, stride=2), :] for j in range(4)]
            full = jnp.concatenate(strips, axis=1)
            pieces[0:C, 256 * part : 256 * part + 256] = full[:, :256]
            pieces[ROWS : ROWS + C, 256 * part : 256 * part + 256] = pltpu.roll(full, 512 - 144, 1)[:, :256]
            pieces[2 * ROWS : 2 * ROWS + C, 256 * part : 256 * part + 256] = pltpu.roll(full, 512 - 288, 1)[:, :256]
        slab[...] = times(pieces[...], xt[0], xt[1])

    def strip_at(index):
        return pl.ds(pl.multiple_of(index * 128, 128), 128)

    def gather_copy(kind, source, target, r):
        to = (eight + r) % 8
        return pltpu.make_async_remote_copy(
            src_ref=source.at[to // 2], dst_ref=target.at[eight],
            send_sem=dp_send.at[kind, r], recv_sem=dp_recv.at[kind, r],
            device_id=(z_hi * 8 + to, me), device_id_type=MESH,
        )

    def gather_start(kind, source, target):
        for r in range(1, 8):
            gather_copy(kind, source, target, r).start()
        target[eight] = source[x_pos]

    tall = values[...].astype(BF16)
    for n in range(3):
        loads[1 + n].wait()
        spectra[:, 256 * n : 256 * n + 256] = jnp.dot(
            tall, fwd[n, 0], preferred_element_type=F32
        ) + jnp.dot(tall, fwd[n, 1], preferred_element_type=F32)
    for load in loads[4:]:
        load.start()
    slab_to_owners(0, None)
    pl.semaphore_wait(barrier, 25)
    space_start(0)

    pieces[...] = jnp.zeros((TALL, 512), F32)
    maps[:, :, 384:] = jnp.zeros((C, PAIRS, 128), F32)
    matrix[...] = jnp.zeros((ROWS, 128), F32)
    slopes[...] = jnp.zeros((TALL, CELLS), F32)
    matrix[0:C, 0:C] = point_weight[...].astype(F32)
    loads[4].wait()

    def cast_step(c, carry):
        maps[c, :, :MODES] = weight[c].astype(F32).reshape(PAIRS, MODES)
        return carry

    lax.fori_loop(0, C, cast_step, 0)
    loads[5].wait()
    for p in range(PLANES):
        slopes[ROWS * p : ROWS * p + C, :] = cot[0, 0, p].astype(F32)
    for load in loads[6:]:
        load.wait()

    space_wait(0)
    line_up_planes(0)
    along_x(modes, None)
    gather_start(0, modes, all_modes)
    row = kz_weight[me % 2, 0:1, :]

    def mix_step(j, carry):
        strip = strip_at(j)
        first, second = jnp.zeros((PAIRS, 128), F32), jnp.zeros((PAIRS, 128), F32)
        for c in range(C):
            weights = maps[c, :, strip]
            first = first + weights * modes[j, 2 * c : 2 * c + 1, :]
            second = second + weights * modes[j, 2 * c + 1 : 2 * c + 2, :]
        mixed[j] = (first - other(second)) * kz_weight[me % 2, 0:1, strip]
        return carry

    lax.fori_loop(0, 4, mix_step, 0)
    back_along_x()
    planes_to_slabs(1, None)
    space_start(1)

    to_in = jnp.concatenate([turn(matrix[...], ROWS * p) for p in range(PLANES)], axis=0)[:, :TALL].astype(BF16)
    here = lax.broadcasted_iota(jnp.int32, (ROWS, C), 0) == lax.broadcasted_iota(jnp.int32, (ROWS, C), 1)
    bias = jnp.sum(jnp.where(here, bias_term[...], 0.0), axis=1, keepdims=True)
    bias = jnp.concatenate([bias] * PLANES, axis=0)
    for n in range(9):
        columns = slice(256 * n, 256 * n + 256)
        grads[:, columns] = bias + lax.dot_general(
            to_in, values[:, columns].astype(BF16), (((0,), (0,)), ((), ())), preferred_element_type=F32
        )
    space_wait(1)
    owners_to_slab(1)

    full = lined[...]
    rate = math.sqrt(2.0 / math.pi)
    bias_sum = jnp.zeros((TALL, 1), F32)
    for n in range(9):
        columns = slice(256 * n, 256 * n + 256)
        pre = times(full, inv[n, 0], inv[n, 1]) + grads[:, columns]
        square = pre * pre
        bend = jnp.tanh(rate * (pre + 0.044715 * (square * pre)))
        half = 0.5 * (1.0 + bend)
        slope = half + 0.5 * pre * (1.0 - bend * bend) * (rate * (1.0 + 3 * 0.044715 * square))
        active = half * pre
        for p in range(PLANES):
            out_vmem[0, 0, p, :, columns] = active[ROWS * p : ROWS * p + C].astype(BF16)
        slope = slope * slopes[:, columns]
        grads[:, columns] = slope
        bias_sum = bias_sum + jnp.sum(slope, axis=1, keepdims=True)
    store_out = pltpu.make_async_copy(out_vmem, out_hbm, store_sem.at[0])
    store_out.start()

    full = grads[...]
    for n in range(3):
        spectra[:, 256 * n : 256 * n + 256] = times(full, fwd[n, 0], fwd[n, 1])
    bias_own = bias_sum[:C] + bias_sum[ROWS : ROWS + C] + bias_sum[2 * ROWS : 2 * ROWS + C]
    slab_to_owners(2, jnp.where(lane == 108, bias_own, 0.0))
    space_start(2)

    point = jnp.zeros((ROWS, ROWS), F32)
    last = (((1,), (1,)), ((), ()))
    for p in range(PLANES):
        field = values[ROWS * p : ROWS * p + ROWS, :].astype(BF16)
        slope = grads[ROWS * p : ROWS * p + ROWS, :]
        high = slope.astype(BF16)
        low = (slope - high.astype(F32)).astype(BF16)
        point = point + lax.dot_general(field, high, last, preferred_element_type=F32)
        point = point + lax.dot_general(field, low, last, preferred_element_type=F32)
    point = jnp.concatenate([point[:C], jnp.zeros((C, 128 - ROWS), F32)], axis=1)
    point = jnp.where(lane >= 108, turn(point, 108), 0.0)
    for n in range(9):
        columns = slice(256 * n, 256 * n + 256)
        slope = grads[:, columns]
        high = slope.astype(BF16)
        low = (slope - high.astype(F32)).astype(BF16)
        values[:, columns] = jnp.dot(to_in, high, preferred_element_type=F32) + jnp.dot(
            to_in, low, preferred_element_type=F32
        )

    space_wait(2)
    line_up_planes(2)
    along_x(grad_modes, row)
    gather_start(1, grad_modes, all_grads)

    def grad_step(j, carry):
        strip = strip_at(j)
        slope = grad_modes[j]
        crossed = other(slope)
        for c in range(C):
            weights = maps[c, :, strip]
            mixed[j, 2 * c : 2 * c + 1, :] = jnp.sum(weights * slope, axis=0, keepdims=True)
            mixed[j, 2 * c + 1 : 2 * c + 2, :] = jnp.sum(weights * crossed, axis=0, keepdims=True)
        return carry

    lax.fori_loop(0, 4, grad_step, 0)
    back_along_x()
    planes_to_slabs(3, point)
    space_start(3)

    partial8 = partial.reshape(8, 25, 4, 128)
    gathered8 = gathered.reshape(4, 8, 25, 4, 128)
    gathered_pairs = gathered.reshape(4, C, C, 2, 128)
    for r in range(1, 8):
        gather_copy(0, modes, all_modes, r).wait()
        gather_copy(1, grad_modes, all_grads, r).wait()

    def scatter_copy(r):
        to = (z_hi + r) % 4
        return pltpu.make_async_remote_copy(
            src_ref=partial8.at[to * 2 + core], dst_ref=landed.at[r - 1],
            send_sem=dp_send.at[2, r], recv_sem=dp_recv.at[2, r],
            device_id=(to * 8 + eight, me), device_id_type=MESH,
        )

    for r in (2, 1, 3, 0):
        start = (z_hi + r) % 4 * 5 + 2 * core

        def part_step(i, carry):
            first, second = jnp.zeros((PAIRS, 128), F32), jnp.zeros((PAIRS, 128), F32)
            for b in range(8):
                slope = all_grads[b]
                first = first + all_modes[b, pl.ds(2 * (start + i), 1), :] * slope
                second = second + all_modes[b, pl.ds(2 * (start + i) + 1, 1), :] * slope
            partial[start + i] = first + other(second)
            return carry

        lax.fori_loop(0, 3, part_step, 0)
        if r != 0:
            scatter_copy(r).start()

    bias_total = jnp.zeros((C, 128), F32)
    for s in range(SLABS):
        bias_total = bias_total + recv[2, s]
    space_wait(3)
    owners_to_slab(3)
    point_total = jnp.zeros((C, 128), F32)
    for s in range(SLABS):
        point_total = point_total + recv[3, s]
    sums8[eight] = jnp.where(lane >= 108, point_total, jnp.where(lane == 0, turn(bias_total, 20), 0.0))

    def eight_copy(r):
        to = (eight + r) % 8
        return pltpu.make_async_remote_copy(
            src_ref=sums8.at[eight], dst_ref=sums8.at[eight],
            send_sem=dp_send.at[3, r], recv_sem=dp_recv.at[3, r],
            device_id=(z_hi * 8 + to, me), device_id_type=MESH,
        )

    for r in range(1, 8):
        eight_copy(r).start()

    full = lined[...]
    for n in range(9):
        columns = slice(256 * n, 256 * n + 256)
        result = times(full, inv[n, 0], inv[n, 1]) + values[:, columns]
        for p in range(PLANES):
            grad_vmem[0, 0, p, :, columns] = result[ROWS * p : ROWS * p + C].astype(BF16)
    store_grad = pltpu.make_async_copy(grad_vmem, grad_hbm, store_sem.at[1])
    store_grad.start()

    for r in range(1, 4):
        scatter_copy(r).wait()
    gathered8[x_pos, z_hi * 2 + core] = partial8[z_hi * 2 + core] + landed[0] + landed[1] + landed[2]

    def z_copy(r):
        block = gathered8.at[x_pos, z_hi * 2 + core]
        return pltpu.make_async_remote_copy(
            src_ref=block, dst_ref=block,
            send_sem=dp_send.at[4, r], recv_sem=dp_recv.at[4, r],
            device_id=((z_hi + r) % 4 * 8 + eight, me), device_id_type=MESH,
        )

    def x_copy(k, r):
        block = gathered8.at[x_pos, (z_hi - k) % 4 * 2 + core]
        return pltpu.make_async_remote_copy(
            src_ref=block, dst_ref=block,
            send_sem=x_send.at[k, r], recv_sem=x_recv.at[k, r],
            device_id=(z_hi * 8 + (x_pos + r) % 4 * 2 + core, me), device_id_type=MESH,
        )

    def core_copy(k):
        block = gathered8.at[:, (z_hi - k) % 4 * 2 + core]
        return pltpu.make_async_remote_copy(
            src_ref=block, dst_ref=block,
            send_sem=dp_send.at[6, k], recv_sem=dp_recv.at[6, k],
            device_id=(z_hi * 8 + x_pos * 2 + 1 - core, me), device_id_type=MESH,
        )

    def spec_store(k, strip):
        rows = pl.ds((z_hi - k) % 4 * 5, 5)
        return pltpu.make_async_copy(
            gathered_pairs.at[strip, rows],
            spec_hbm.at[rows, :, :, 128 * strip : 128 * strip + 128],
            spec_sem.at[k, strip],
        )

    for r in (2, 1, 3):
        z_copy(r).start()
    for r in (2, 1, 3):
        x_copy(0, r).start()

    for r in range(1, 8):
        eight_copy(r).wait()
    total = sums8[0]
    for b in range(1, 8):
        total = total + sums8[b]
    sums4[z_hi] = total

    def four_copy(r):
        to = (z_hi + r) % 4
        return pltpu.make_async_remote_copy(
            src_ref=sums4.at[z_hi], dst_ref=sums4.at[z_hi],
            send_sem=dp_send.at[5, r], recv_sem=dp_recv.at[5, r],
            device_id=(to * 8 + eight, me), device_id_type=MESH,
        )

    for r in range(1, 4):
        four_copy(r).start()
    for k in (1, 3, 2):
        z_copy(k).wait_recv()
        for r in (2, 1, 3):
            x_copy(k, r).start()
    order = (0, 1, 3, 2)
    for index, k in enumerate(order):
        for r in range(1, 4):
            x_copy(k, r).wait_recv()
        core_copy(k).start()
        if index > 0:
            core_copy(order[index - 1]).wait_recv()
            for strip in range(4):
                spec_store(order[index - 1], strip).start()
    for r in range(1, 4):
        four_copy(r).wait()
    sums_ref[...] = sums4[0] + sums4[1] + sums4[2] + sums4[3]
    core_copy(2).wait_recv()
    for strip in range(4):
        spec_store(2, strip).start()
    for r in range(1, 4):
        z_copy(r).wait_send()
        for k in range(4):
            x_copy(k, r).wait_send()
    for k in order:
        core_copy(k).wait_send()
    for k in order:
        for strip in range(4):
            spec_store(k, strip).wait()
    store_out.wait()
    store_grad.wait()


def on_device(wake_field, spec_weight, point_weight, bias_term, cotangent):
    forward, inverse, x_two, x_inverse, kz_weight = tables()
    weight = spec_weight.transpose(1, 2, 0, 3)
    anywhere = pl.BlockSpec(memory_space=pl.ANY)
    inside = pl.BlockSpec(memory_space=pltpu.VMEM)
    field = wake_field.shape
    output_field, grad_field, grad_spec, sums = pl.pallas_call(
        kernel,
        out_shape=(
            jax.ShapeDtypeStruct(field, BF16),
            jax.ShapeDtypeStruct(field, BF16),
            jax.ShapeDtypeStruct((C, C, 2, 512), F32),
            jax.ShapeDtypeStruct((C, 128), F32),
        ),
        in_specs=[anywhere] * 3 + [inside] * 3 + [anywhere] * 4,
        out_specs=(anywhere, anywhere, anywhere, inside),
        scratch_shapes=[
            pltpu.VMEM(field, BF16),
            pltpu.VMEM(field, BF16),
            pltpu.VMEM(weight.shape, BF16),
            pltpu.VMEM(forward.shape, BF16),
            pltpu.VMEM(inverse.shape, BF16),
            pltpu.VMEM(x_two.shape, BF16),
            pltpu.VMEM(x_inverse.shape, BF16),
            pltpu.VMEM((TALL, CELLS), F32),
            pltpu.VMEM((TALL, CELLS), F32),
            pltpu.VMEM((C, PAIRS, 512), F32),
            pltpu.VMEM((TALL, WIDE), F32),
            pltpu.VMEM((TALL, WIDE), F32),
            pltpu.VMEM((TALL, CELLS), F32),
            pltpu.VMEM((TALL, WIDE), F32),
            pltpu.VMEM((TALL, 512), F32),
            pltpu.VMEM((4, PAIRS, 128), F32),
            pltpu.VMEM((4, PAIRS, 128), F32),
            pltpu.VMEM((4, PAIRS, 128), F32),
            pltpu.VMEM((ROWS, 128), F32),
            pltpu.VMEM((4, SLABS, C, 128), F32),
            pltpu.VMEM((4, SLABS, C, 128), F32),
            pltpu.VMEM((8, PAIRS, 128), F32),
            pltpu.VMEM((8, PAIRS, 128), F32),
            pltpu.VMEM((C, PAIRS, 128), F32),
            pltpu.VMEM((3, 25, 4, 128), F32),
            pltpu.VMEM((4, C, PAIRS, 128), F32),
            pltpu.VMEM((8, C, 128), F32),
            pltpu.VMEM((4, C, 128), F32),
            pltpu.VMEM(field, BF16),
            pltpu.VMEM(field, BF16),
            pltpu.SemaphoreType.DMA((9,)),
            pltpu.SemaphoreType.DMA((2,)),
            pltpu.SemaphoreType.DMA((4, 4)),
            pltpu.SemaphoreType.DMA((4, 16)),
            pltpu.SemaphoreType.DMA((4, 16)),
            pltpu.SemaphoreType.DMA((7, 8)),
            pltpu.SemaphoreType.DMA((7, 8)),
            pltpu.SemaphoreType.DMA((4, 4)),
            pltpu.SemaphoreType.DMA((4, 4)),
        ],
        compiler_params=pltpu.CompilerParams(
            collective_id=0, has_side_effects=True, vmem_limit_bytes=56 * 1024 * 1024
        ),
    )(wake_field, cotangent, weight, point_weight, bias_term[None], kz_weight, forward, inverse, x_two, x_inverse)
    return (
        output_field,
        grad_field,
        grad_spec.transpose(2, 0, 1, 3)[..., :MODES],
        sums[:, 108:128],
        sums[:, 0],
    )


def solution(mesh):
    placed = (
        P("dp", None, "space", None, None),
        P(None, None, None, "space"),
        P(),
        P(),
        P("dp", None, "space", None, None),
    )
    return jax.shard_map(
        on_device,
        mesh=mesh,
        in_specs=placed,
        out_specs=(
            P("dp", None, "space", None, None),
            P("dp", None, "space", None, None),
            P(None, None, None, "space"),
            P(),
            P(),
        ),
        check_vma=False,
    )
```

```python
import functools
import math

import jax
import jax.numpy as jnp
import numpy as np
from jax import lax
from jax.experimental import pallas as pl
from jax.experimental.pallas import tpu as pltpu
from jax.sharding import PartitionSpec as P

MESH = pl.DeviceIdType.MESH
F32 = jnp.float32
BF16 = jnp.bfloat16

C = 20
N = 48
MZ = 12
CELLS = N * N
KX = 24
SLABS = 16
PLANES = 3
OWN = 18
MODES = OWN * KX
ROWS = 24
TALL = PLANES * ROWS
TILES = 6
WIDE = TILES * 128
PAIRS = 2 * C
SPLIT = 19


def wave(i):
    return np.where(i < 12, i, i - 24)


def halves(table):
    high = table.astype(np.float32).astype(BF16)
    low = (table - high.astype(np.float64)).astype(np.float32).astype(BF16)
    return np.stack([high, low])


def yz_table():
    lane = np.arange(128)
    g, k, part, q6 = lane // 36, lane % 36 // 12, lane % 12 // 6, lane % 6
    owner = 3 * np.arange(TILES)[:, None] + k[None, :]
    used = (lane < 108)[None, :] & (owner < SLABS)
    q = OWN * owner + 6 * g[None, :] + q6[None, :]
    ky, kz = wave(q // MZ), q % MZ
    cell = np.arange(CELLS)
    y, z = cell // N, cell % N
    phase = (y[:, None, None] * ky[None] + z[:, None, None] * kz[None]) % N
    angle = 2.0 * np.pi * phase / N
    table = np.where(part == 0, np.cos(angle), -np.sin(angle)) / N
    return np.where(used[None], table, 0.0).reshape(CELLS, WIDE)


def x_table():
    lane = np.arange(128)
    k, p, part, q6 = lane // 36, lane % 36 // 12, lane % 12 // 6, lane % 6
    slab = 3 * np.arange(TILES)[:, None] + k[None, :]
    used = ((lane < 108)[None, :] & (slab < SLABS)).reshape(-1)
    x = (PLANES * slab + p[None, :]).reshape(-1)
    part, q6 = np.tile(part, TILES), np.tile(q6, TILES)
    column = np.arange(512)
    part_out, rest = column // 256, column % 256
    q6_out, i = rest // KX, rest % KX
    angle = 2.0 * np.pi * (x[:, None] * wave(i)[None, :] % N) / N
    cosine, sine = np.cos(angle), np.sin(angle)
    same = part[:, None] == part_out[None, :]
    table = np.where(same, cosine, np.where(part[:, None] == 1, sine, -sine)) / math.sqrt(N)
    keep = used[:, None] & (rest < 6 * KX)[None, :] & (q6[:, None] == q6_out[None, :])
    return np.where(keep, table, 0.0)


@functools.cache
def tables():
    yz, x = yz_table(), x_table()
    yz_two, x_two = halves(yz), halves(x)
    forward = np.ascontiguousarray(yz_two.reshape(2, CELLS, 3, 256).transpose(2, 0, 1, 3))
    inverse = np.ascontiguousarray(yz_two.transpose(0, 2, 1).reshape(2, WIDE, 9, 256).transpose(2, 0, 1, 3))
    x_inverse = np.ascontiguousarray(x_two.transpose(0, 2, 1))
    own = np.arange(512) // KX
    weight = np.stack([np.where((6 * parity + own) % MZ == 0, 1.0, 2.0) for parity in range(2)])
    weight = np.broadcast_to(weight[:, None, :], (2, 8, 512)).astype(np.float32)
    return forward, inverse, x_two, x_inverse, np.ascontiguousarray(weight)


def times(value, high, low):
    rows = value.shape[0]
    top = value.astype(BF16)
    wide = top.astype(F32)
    both = jnp.concatenate([wide, value - wide], axis=0).astype(BF16)
    first = jnp.dot(both, high, preferred_element_type=F32)
    return first[:rows] + first[rows:] + jnp.dot(top, low, preferred_element_type=F32)


def kernel(
    wake_hbm, cot_hbm, weight_hbm, point_weight, bias_term, kz_weight, fwd_hbm, inv_hbm, x_hbm, xt_hbm,
    out_hbm, grad_hbm, spec_hbm, sums_ref,
    wake, cot, weight, fwd, inv, xf, xt,
    values, slopes, maps, spectra, slab, grads, lined, pieces, modes, mixed, grad_modes, matrix,
    send, recv, all_modes, all_grads, partial, landed, gathered, sums8, sums4,
    out_vmem, grad_vmem,
    load_sem, store_sem, spec_sem, send_sem, recv_sem, dp_send, dp_recv, x_send, x_recv, z_send, z_recv,
):
    dp = lax.axis_index("dp")
    me = lax.axis_index("space")
    z_hi, eight = dp // 8, dp % 8
    x_pos, core = eight // 2, eight % 2
    lane = lax.broadcasted_iota(jnp.int32, (C, 128), 1)
    third = lane // 36
    slot = jnp.where(lane < 108, lane % 36 // 12, 3)
    even = lax.broadcasted_iota(jnp.int32, (PAIRS, 128), 0) % 2 == 0

    loads = [
        pltpu.make_async_copy(wake_hbm, wake, load_sem.at[0]),
        pltpu.make_async_copy(fwd_hbm.at[0], fwd.at[0], load_sem.at[1]),
        pltpu.make_async_copy(fwd_hbm.at[1], fwd.at[1], load_sem.at[2]),
        pltpu.make_async_copy(fwd_hbm.at[2], fwd.at[2], load_sem.at[3]),
        pltpu.make_async_copy(weight_hbm, weight, load_sem.at[4]),
        pltpu.make_async_copy(cot_hbm, cot, load_sem.at[5]),
        pltpu.make_async_copy(x_hbm, xf, load_sem.at[6]),
        pltpu.make_async_copy(xt_hbm, xt, load_sem.at[7]),
        pltpu.make_async_copy(inv_hbm, inv, load_sem.at[8]),
    ]
    for load in loads[:4]:
        load.start()

    barrier = pltpu.get_barrier_semaphore()
    for r in range(1, 16):
        pl.semaphore_signal(barrier, inc=1, device_id=(dp, (me + r) % 16), device_id_type=MESH)
    for r in range(1, 8):
        peer = z_hi * 8 + (eight + r) % 8
        pl.semaphore_signal(barrier, inc=1, device_id=(peer, me), device_id_type=MESH)
    for r in range(1, 4):
        peer = (z_hi + r) % 4 * 8 + eight
        pl.semaphore_signal(barrier, inc=1, device_id=(peer, me), device_id_type=MESH)

    values[...] = jnp.zeros((TALL, CELLS), F32)
    lined[...] = jnp.zeros((TALL, WIDE), F32)
    loads[0].wait()
    for p in range(PLANES):
        values[ROWS * p : ROWS * p + C, :] = wake[0, 0, p].astype(F32)

    def space_copy(phase, r):
        to = (me + r) % 16
        return pltpu.make_async_remote_copy(
            src_ref=send.at[phase, to], dst_ref=recv.at[phase, me],
            send_sem=send_sem.at[phase, r], recv_sem=recv_sem.at[phase, r],
            device_id=(dp, to), device_id_type=MESH,
        )

    def space_start(phase):
        for r in range(1, 16):
            space_copy(phase, r).start()
        recv[phase, me] = send[phase, me]

    def space_wait(phase):
        for r in range(1, 16):
            space_copy(phase, r).wait()

    def turn(value, shift):
        shift %= 128
        return value if shift == 0 else pltpu.roll(value, shift, 1)

    def other(value):
        return jnp.where(even, pltpu.roll(value, PAIRS - 1, 0), -pltpu.roll(value, 1, 0))

    def choose(where, parts):
        total = jnp.zeros((C, 128), F32)
        for index, part in parts:
            total = jnp.where(where == index, part, total)
        return total

    def slab_to_owners(phase, ride):
        for t in range(TILES):
            held = [spectra[ROWS * p : ROWS * p + C, 128 * t : 128 * t + 128] for p in range(PLANES)]
            for k in range(3):
                if 3 * t + k < SLABS:
                    message = choose(slot, [(p, turn(held[p], 12 * (p - k))) for p in range(PLANES)])
                    send[phase, 3 * t + k] = message if ride is None else message + ride

    def owners_to_slab(phase):
        for t in range(TILES):
            ks = [k for k in range(3) if 3 * t + k < SLABS]
            held = [recv[phase, 3 * t + k] for k in ks]
            for p in range(PLANES):
                lined[ROWS * p : ROWS * p + C, 128 * t : 128 * t + 128] = choose(
                    slot, [(k, turn(held[k], 12 * (k - p))) for k in ks]
                )

    def line_up_planes(phase):
        for u in range(TILES):
            ks = [k for k in range(3) if 3 * u + k < SLABS]
            held = [recv[phase, 3 * u + k] for k in ks]
            for g in range(3):
                lined[ROWS * g : ROWS * g + C, 128 * u : 128 * u + 128] = choose(
                    third, [(k, turn(held[k], 36 * (k - g))) for k in ks]
                )

    def planes_to_slabs(phase, ride):
        for u in range(TILES):
            held = [slab[ROWS * g : ROWS * g + C, 128 * u : 128 * u + 128] for g in range(3)]
            for k in range(3):
                if 3 * u + k < SLABS:
                    message = choose(third, [(g, turn(held[g], 36 * (g - k))) for g in range(3)])
                    send[phase, 3 * u + k] = message if ride is None else message + ride

    def along_x(target, scale):
        result = times(lined[...], xf[0], xf[1])
        for part in range(2):
            block = [result[ROWS * g : ROWS * g + ROWS, 256 * part : 256 * part + 256] for g in range(3)]
            second, last = pltpu.roll(block[1], 16, 1), pltpu.roll(block[2], 32, 1)
            strips = [
                block[0][:, :128],
                block[0][:, 128:] + second[:, :128],
                second[:, 128:] + last[:, :128],
                last[:, 128:],
            ]
            for j in range(4):
                strip = strips[j][:C]
                if scale is not None:
                    strip = strip * scale[:, 128 * j : 128 * j + 128]
                target[j, pl.ds(part, C, stride=2), :] = strip

    def back_along_x():
        for part in range(2):
            strips = [mixed[j, pl.ds(part, C, stride=2), :] for j in range(4)]
            full = jnp.concatenate(strips, axis=1)
            pieces[0:C, 256 * part : 256 * part + 256] = full[:, :256]
            pieces[ROWS : ROWS + C, 256 * part : 256 * part + 256] = pltpu.roll(full, 512 - 144, 1)[:, :256]
            pieces[2 * ROWS : 2 * ROWS + C, 256 * part : 256 * part + 256] = pltpu.roll(full, 512 - 288, 1)[:, :256]
        slab[...] = times(pieces[...], xt[0], xt[1])

    def strip_at(index):
        return pl.ds(pl.multiple_of(index * 128, 128), 128)

    def gather_copy(kind, source, target, r):
        to = (eight + r) % 8
        return pltpu.make_async_remote_copy(
            src_ref=source.at[to // 2], dst_ref=target.at[eight],
            send_sem=dp_send.at[kind, r], recv_sem=dp_recv.at[kind, r],
            device_id=(z_hi * 8 + to, me), device_id_type=MESH,
        )

    def gather_start(kind, source, target):
        for r in range(1, 8):
            gather_copy(kind, source, target, r).start()
        target[eight] = source[x_pos]

    tall = values[...].astype(BF16)
    for n in range(3):
        loads[1 + n].wait()
        spectra[:, 256 * n : 256 * n + 256] = jnp.dot(
            tall, fwd[n, 0], preferred_element_type=F32
        ) + jnp.dot(tall, fwd[n, 1], preferred_element_type=F32)
    for load in loads[4:]:
        load.start()
    slab_to_owners(0, None)
    pl.semaphore_wait(barrier, 25)
    space_start(0)

    pieces[...] = jnp.zeros((TALL, 512), F32)
    maps[:, :, 384:] = jnp.zeros((C, PAIRS, 128), F32)
    matrix[...] = jnp.zeros((ROWS, 128), F32)
    slopes[...] = jnp.zeros((TALL, CELLS), F32)
    matrix[0:C, 0:C] = point_weight[...].astype(F32)
    loads[4].wait()

    def cast_step(c, carry):
        maps[c, :, :MODES] = weight[c].astype(F32).reshape(PAIRS, MODES)
        return carry

    lax.fori_loop(0, C, cast_step, 0)
    loads[5].wait()
    for p in range(PLANES):
        slopes[ROWS * p : ROWS * p + C, :] = cot[0, 0, p].astype(F32)
    for load in loads[6:]:
        load.wait()

    space_wait(0)
    line_up_planes(0)
    along_x(modes, None)
    gather_start(0, modes, all_modes)
    row = kz_weight[me % 2, 0:1, :]

    def mix_step(j, carry):
        strip = strip_at(j)
        first, second = jnp.zeros((PAIRS, 128), F32), jnp.zeros((PAIRS, 128), F32)
        for c in range(C):
            weights = maps[c, :, strip]
            first = first + weights * modes[j, 2 * c : 2 * c + 1, :]
            second = second + weights * modes[j, 2 * c + 1 : 2 * c + 2, :]
        mixed[j] = (first - other(second)) * kz_weight[me % 2, 0:1, strip]
        return carry

    lax.fori_loop(0, 4, mix_step, 0)
    back_along_x()
    planes_to_slabs(1, None)
    space_start(1)

    to_in = jnp.concatenate([turn(matrix[...], ROWS * p) for p in range(PLANES)], axis=0)[:, :TALL].astype(BF16)
    here = lax.broadcasted_iota(jnp.int32, (ROWS, C), 0) == lax.broadcasted_iota(jnp.int32, (ROWS, C), 1)
    bias = jnp.sum(jnp.where(here, bias_term[...], 0.0), axis=1, keepdims=True)
    bias = jnp.concatenate([bias] * PLANES, axis=0)
    for n in range(9):
        columns = slice(256 * n, 256 * n + 256)
        grads[:, columns] = bias + lax.dot_general(
            to_in, values[:, columns].astype(BF16), (((0,), (0,)), ((), ())), preferred_element_type=F32
        )
    space_wait(1)
    owners_to_slab(1)

    full = lined[...]
    rate = math.sqrt(2.0 / math.pi)
    bias_sum = jnp.zeros((TALL, 1), F32)
    for n in range(9):
        columns = slice(256 * n, 256 * n + 256)
        pre = times(full, inv[n, 0], inv[n, 1]) + grads[:, columns]
        square = pre * pre
        bend = jnp.tanh(rate * (pre + 0.044715 * (square * pre)))
        half = 0.5 * (1.0 + bend)
        slope = half + 0.5 * pre * (1.0 - bend * bend) * (rate * (1.0 + 3 * 0.044715 * square))
        active = half * pre
        for p in range(PLANES):
            out_vmem[0, 0, p, :, columns] = active[ROWS * p : ROWS * p + C].astype(BF16)
        slope = slope * slopes[:, columns]
        grads[:, columns] = slope
        bias_sum = bias_sum + jnp.sum(slope, axis=1, keepdims=True)
    store_out = pltpu.make_async_copy(out_vmem, out_hbm, store_sem.at[0])
    store_out.start()

    full = grads[...]
    for n in range(3):
        spectra[:, 256 * n : 256 * n + 256] = times(full, fwd[n, 0], fwd[n, 1])
    bias_own = bias_sum[:C] + bias_sum[ROWS : ROWS + C] + bias_sum[2 * ROWS : 2 * ROWS + C]
    slab_to_owners(2, jnp.where(lane == 108, bias_own, 0.0))
    space_start(2)

    point = jnp.zeros((ROWS, ROWS), F32)
    last = (((1,), (1,)), ((), ()))
    for p in range(PLANES):
        field = values[ROWS * p : ROWS * p + ROWS, :].astype(BF16)
        slope = grads[ROWS * p : ROWS * p + ROWS, :]
        high = slope.astype(BF16)
        low = (slope - high.astype(F32)).astype(BF16)
        point = point + lax.dot_general(field, high, last, preferred_element_type=F32)
        point = point + lax.dot_general(field, low, last, preferred_element_type=F32)
    point = jnp.concatenate([point[:C], jnp.zeros((C, 128 - ROWS), F32)], axis=1)
    point = jnp.where(lane >= 108, turn(point, 108), 0.0)
    for n in range(9):
        columns = slice(256 * n, 256 * n + 256)
        slope = grads[:, columns]
        high = slope.astype(BF16)
        low = (slope - high.astype(F32)).astype(BF16)
        values[:, columns] = jnp.dot(to_in, high, preferred_element_type=F32) + jnp.dot(
            to_in, low, preferred_element_type=F32
        )

    space_wait(2)
    line_up_planes(2)
    along_x(grad_modes, row)
    gather_start(1, grad_modes, all_grads)

    def grad_step(j, carry):
        strip = strip_at(j)
        slope = grad_modes[j]
        crossed = other(slope)
        for c in range(C):
            weights = maps[c, :, strip]
            mixed[j, 2 * c : 2 * c + 1, :] = jnp.sum(weights * slope, axis=0, keepdims=True)
            mixed[j, 2 * c + 1 : 2 * c + 2, :] = jnp.sum(weights * crossed, axis=0, keepdims=True)
        return carry

    lax.fori_loop(0, 4, grad_step, 0)
    back_along_x()
    planes_to_slabs(3, point)
    space_start(3)

    partial8 = partial.reshape(8, 25, 4, 128)
    gathered8 = gathered.reshape(4, 8, 25, 4, 128)
    gathered_pairs = gathered.reshape(4, C, C, 2, 128)
    for r in range(1, 8):
        gather_copy(0, modes, all_modes, r).wait()
        gather_copy(1, grad_modes, all_grads, r).wait()

    def scatter_copy(r):
        to = (z_hi + r) % 4
        return pltpu.make_async_remote_copy(
            src_ref=partial8.at[to * 2 + core], dst_ref=landed.at[r - 1],
            send_sem=dp_send.at[2, r], recv_sem=dp_recv.at[2, r],
            device_id=(to * 8 + eight, me), device_id_type=MESH,
        )

    for r in (2, 1, 3, 0):
        start = (z_hi + r) % 4 * 5 + 2 * core

        def part_step(i, carry):
            first, second = jnp.zeros((PAIRS, 128), F32), jnp.zeros((PAIRS, 128), F32)
            for b in range(8):
                slope = all_grads[b]
                first = first + all_modes[b, pl.ds(2 * (start + i), 1), :] * slope
                second = second + all_modes[b, pl.ds(2 * (start + i) + 1, 1), :] * slope
            partial[start + i] = first + other(second)
            return carry

        lax.fori_loop(0, 3, part_step, 0)
        if r != 0:
            scatter_copy(r).start()

    bias_total = jnp.zeros((C, 128), F32)
    for s in range(SLABS):
        bias_total = bias_total + recv[2, s]
    space_wait(3)
    owners_to_slab(3)
    point_total = jnp.zeros((C, 128), F32)
    for s in range(SLABS):
        point_total = point_total + recv[3, s]
    sums8[eight] = jnp.where(lane >= 108, point_total, jnp.where(lane == 0, turn(bias_total, 20), 0.0))

    def eight_copy(r):
        to = (eight + r) % 8
        return pltpu.make_async_remote_copy(
            src_ref=sums8.at[eight], dst_ref=sums8.at[eight],
            send_sem=dp_send.at[3, r], recv_sem=dp_recv.at[3, r],
            device_id=(z_hi * 8 + to, me), device_id_type=MESH,
        )

    for r in range(1, 8):
        eight_copy(r).start()

    full = lined[...]
    for n in range(9):
        columns = slice(256 * n, 256 * n + 256)
        result = times(full, inv[n, 0], inv[n, 1]) + values[:, columns]
        for p in range(PLANES):
            grad_vmem[0, 0, p, :, columns] = result[ROWS * p : ROWS * p + C].astype(BF16)
    store_grad = pltpu.make_async_copy(grad_vmem, grad_hbm, store_sem.at[1])
    store_grad.start()

    for r in range(1, 4):
        scatter_copy(r).wait()
    gathered8[x_pos, z_hi * 2 + core] = partial8[z_hi * 2 + core] + landed[0] + landed[1] + landed[2]

    def own(k):
        return (z_hi - k) % 4 * 2 + core

    def to_z(block, send_at, recv_at, r):
        return pltpu.make_async_remote_copy(
            src_ref=block, dst_ref=block, send_sem=send_at, recv_sem=recv_at,
            device_id=((z_hi + r) % 4 * 8 + eight, me), device_id_type=MESH,
        )

    def to_x(block, send_at, recv_at, r):
        return pltpu.make_async_remote_copy(
            src_ref=block, dst_ref=block, send_sem=send_at, recv_sem=recv_at,
            device_id=(z_hi * 8 + (x_pos + r) % 4 * 2 + core, me), device_id_type=MESH,
        )

    def z_copy(r):
        return to_z(gathered8.at[x_pos, own(0), 0:SPLIT], dp_send.at[4, r], dp_recv.at[4, r], r)

    def x_copy(k, r):
        return to_x(gathered8.at[x_pos, own(k), 0:SPLIT], x_send.at[k, r], x_recv.at[k, r], r)

    def x_first(r):
        return to_x(gathered8.at[x_pos, own(0), SPLIT:25], dp_send.at[7, r], dp_recv.at[7, r], r)

    def z_second(j, r):
        return to_z(gathered8.at[(x_pos - j) % 4, own(0), SPLIT:25], z_send.at[j, r], z_recv.at[j, r], r)

    def core_copy(k):
        block = gathered8.at[:, (z_hi - k) % 4 * 2 + core]
        return pltpu.make_async_remote_copy(
            src_ref=block, dst_ref=block,
            send_sem=dp_send.at[6, k], recv_sem=dp_recv.at[6, k],
            device_id=(z_hi * 8 + x_pos * 2 + 1 - core, me), device_id_type=MESH,
        )

    def spec_store(k, strip):
        rows = pl.ds((z_hi - k) % 4 * 5, 5)
        return pltpu.make_async_copy(
            gathered_pairs.at[strip, rows],
            spec_hbm.at[rows, :, :, 128 * strip : 128 * strip + 128],
            spec_sem.at[k, strip],
        )

    for r in (2, 1, 3):
        x_first(r).start()
    for r in (2, 1, 3):
        z_copy(r).start()
    for r in (2, 1, 3):
        z_second(0, r).start()
        x_copy(0, r).start()

    for r in range(1, 8):
        eight_copy(r).wait()
    total = sums8[0]
    for b in range(1, 8):
        total = total + sums8[b]
    sums4[z_hi] = total

    def four_copy(r):
        to = (z_hi + r) % 4
        return pltpu.make_async_remote_copy(
            src_ref=sums4.at[z_hi], dst_ref=sums4.at[z_hi],
            send_sem=dp_send.at[5, r], recv_sem=dp_recv.at[5, r],
            device_id=(to * 8 + eight, me), device_id_type=MESH,
        )

    for r in range(1, 4):
        four_copy(r).start()
    for j in (1, 3, 2):
        x_first(j).wait_recv()
        for r in (2, 1, 3):
            z_second(j, r).start()
    for k in (1, 3, 2):
        z_copy(k).wait_recv()
        for r in (2, 1, 3):
            x_copy(k, r).start()
    order = (0, 1, 3, 2)
    for index, k in enumerate(order):
        for r in range(1, 4):
            x_copy(k, r).wait_recv()
        if k != 0:
            for j in range(4):
                z_second(j, k).wait_recv()
        core_copy(k).start()
        if index > 0:
            core_copy(order[index - 1]).wait_recv()
            for strip in range(4):
                spec_store(order[index - 1], strip).start()
    for r in range(1, 4):
        four_copy(r).wait()
    total = turn(sums4[0] + sums4[1] + sums4[2] + sums4[3], 20)
    sums_ref[0:C, :] = total
    square = lax.broadcasted_iota(jnp.int32, (C, 128), 0) == lane
    sums_ref[C : C + 1, :] = jnp.sum(jnp.where(square, total[:, C : C + 1], 0.0), axis=0, keepdims=True)
    core_copy(2).wait_recv()
    for strip in range(4):
        spec_store(2, strip).start()
    for r in range(1, 4):
        z_copy(r).wait_send()
        x_first(r).wait_send()
        for j in range(4):
            z_second(j, r).wait_send()
        for k in range(4):
            x_copy(k, r).wait_send()
    for k in order:
        core_copy(k).wait_send()
    for k in order:
        for strip in range(4):
            spec_store(k, strip).wait()
    store_out.wait()
    store_grad.wait()


def results(out_from, grad_from, spec_from, sums, out_to, grad_to, spec_to, point_to, bias_to, sem):
    copies = []
    for j in range(10):
        rows = pl.ds(2 * j, 2)
        copies.append(pltpu.make_async_copy(spec_from.at[rows], spec_to.at[rows], sem.at[j]))
    for p in range(PLANES):
        copies.append(pltpu.make_async_copy(out_from.at[0, 0, p], out_to.at[0, 0, p], sem.at[10 + p]))
        copies.append(pltpu.make_async_copy(grad_from.at[0, 0, p], grad_to.at[0, 0, p], sem.at[13 + p]))
    for copy in copies:
        copy.start()
    point_to[...] = sums[0:C, 0:C]
    bias_to[...] = sums[C : C + 1, 0:C]
    for copy in copies:
        copy.wait()


def on_device(wake_field, spec_weight, point_weight, bias_term, cotangent):
    forward, inverse, x_two, x_inverse, kz_weight = tables()
    weight = spec_weight.transpose(1, 2, 0, 3)
    anywhere = pl.BlockSpec(memory_space=pl.ANY)
    inside = pl.BlockSpec(memory_space=pltpu.VMEM)
    field = wake_field.shape
    output_field, grad_field, grad_spec, sums = pl.pallas_call(
        kernel,
        out_shape=(
            jax.ShapeDtypeStruct(field, BF16),
            jax.ShapeDtypeStruct(field, BF16),
            jax.ShapeDtypeStruct((C, C, 2, 512), F32),
            jax.ShapeDtypeStruct((ROWS, 128), F32),
        ),
        in_specs=[anywhere] * 3 + [inside] * 3 + [anywhere] * 4,
        out_specs=(anywhere, anywhere, anywhere, inside),
        scratch_shapes=[
            pltpu.VMEM(field, BF16),
            pltpu.VMEM(field, BF16),
            pltpu.VMEM(weight.shape, BF16),
            pltpu.VMEM(forward.shape, BF16),
            pltpu.VMEM(inverse.shape, BF16),
            pltpu.VMEM(x_two.shape, BF16),
            pltpu.VMEM(x_inverse.shape, BF16),
            pltpu.VMEM((TALL, CELLS), F32),
            pltpu.VMEM((TALL, CELLS), F32),
            pltpu.VMEM((C, PAIRS, 512), F32),
            pltpu.VMEM((TALL, WIDE), F32),
            pltpu.VMEM((TALL, WIDE), F32),
            pltpu.VMEM((TALL, CELLS), F32),
            pltpu.VMEM((TALL, WIDE), F32),
            pltpu.VMEM((TALL, 512), F32),
            pltpu.VMEM((4, PAIRS, 128), F32),
            pltpu.VMEM((4, PAIRS, 128), F32),
            pltpu.VMEM((4, PAIRS, 128), F32),
            pltpu.VMEM((ROWS, 128), F32),
            pltpu.VMEM((4, SLABS, C, 128), F32),
            pltpu.VMEM((4, SLABS, C, 128), F32),
            pltpu.VMEM((8, PAIRS, 128), F32),
            pltpu.VMEM((8, PAIRS, 128), F32),
            pltpu.VMEM((C, PAIRS, 128), F32),
            pltpu.VMEM((3, 25, 4, 128), F32),
            pltpu.VMEM((4, C, PAIRS, 128), F32),
            pltpu.VMEM((8, C, 128), F32),
            pltpu.VMEM((4, C, 128), F32),
            pltpu.VMEM(field, BF16),
            pltpu.VMEM(field, BF16),
            pltpu.SemaphoreType.DMA((9,)),
            pltpu.SemaphoreType.DMA((2,)),
            pltpu.SemaphoreType.DMA((4, 4)),
            pltpu.SemaphoreType.DMA((4, 16)),
            pltpu.SemaphoreType.DMA((4, 16)),
            pltpu.SemaphoreType.DMA((8, 8)),
            pltpu.SemaphoreType.DMA((8, 8)),
            pltpu.SemaphoreType.DMA((4, 4)),
            pltpu.SemaphoreType.DMA((4, 4)),
            pltpu.SemaphoreType.DMA((4, 4)),
            pltpu.SemaphoreType.DMA((4, 4)),
        ],
        compiler_params=pltpu.CompilerParams(
            collective_id=0, has_side_effects=True, vmem_limit_bytes=56 * 1024 * 1024
        ),
    )(wake_field, cotangent, weight, point_weight, bias_term[None], kz_weight, forward, inverse, x_two, x_inverse)
    output_field, grad_field, grad_spec, grad_point, grad_bias = pl.pallas_call(
        results,
        out_shape=(
            jax.ShapeDtypeStruct(field, BF16),
            jax.ShapeDtypeStruct(field, BF16),
            jax.ShapeDtypeStruct((C, C, 2, 512), F32),
            jax.ShapeDtypeStruct((C, C), F32),
            jax.ShapeDtypeStruct((1, C), F32),
        ),
        in_specs=[anywhere] * 3 + [inside],
        out_specs=(anywhere, anywhere, anywhere, inside, inside),
        scratch_shapes=[pltpu.SemaphoreType.DMA((16,))],
    )(output_field, grad_field, grad_spec, sums)
    return (
        output_field,
        grad_field,
        grad_spec.transpose(2, 0, 1, 3)[..., :MODES],
        grad_point,
        grad_bias.reshape(C),
    )


def solution(mesh):
    placed = (
        P("dp", None, "space", None, None),
        P(None, None, None, "space"),
        P(),
        P(),
        P("dp", None, "space", None, None),
    )
    return jax.shard_map(
        on_device,
        mesh=mesh,
        in_specs=placed,
        out_specs=(
            P("dp", None, "space", None, None),
            P("dp", None, "space", None, None),
            P(None, None, None, "space"),
            P(),
            P(),
        ),
        check_vma=False,
    )
```

```python
import functools
import math

import jax
import jax.numpy as jnp
import numpy as np
from jax import lax
from jax.experimental import pallas as pl
from jax.experimental.pallas import tpu as pltpu
from jax.sharding import PartitionSpec as P

MESH = pl.DeviceIdType.MESH
F32 = jnp.float32
BF16 = jnp.bfloat16

C = 20
N = 48
MZ = 12
CELLS = N * N
KX = 24
SLABS = 16
PLANES = 3
OWN = 18
MODES = OWN * KX
ROWS = 24
TALL = PLANES * ROWS
TILES = 6
WIDE = TILES * 128
PAIRS = 2 * C
SPLIT = 19


def wave(i):
    return np.where(i < 12, i, i - 24)


def halves(table):
    high = table.astype(np.float32).astype(BF16)
    low = (table - high.astype(np.float64)).astype(np.float32).astype(BF16)
    return np.stack([high, low])


def yz_table():
    lane = np.arange(128)
    g, k, part, q6 = lane // 36, lane % 36 // 12, lane % 12 // 6, lane % 6
    owner = 3 * np.arange(TILES)[:, None] + k[None, :]
    used = (lane < 108)[None, :] & (owner < SLABS)
    q = OWN * owner + 6 * g[None, :] + q6[None, :]
    ky, kz = wave(q // MZ), q % MZ
    cell = np.arange(CELLS)
    y, z = cell // N, cell % N
    phase = (y[:, None, None] * ky[None] + z[:, None, None] * kz[None]) % N
    angle = 2.0 * np.pi * phase / N
    table = np.where(part == 0, np.cos(angle), -np.sin(angle)) / N
    return np.where(used[None], table, 0.0).reshape(CELLS, WIDE)


def x_table():
    lane = np.arange(128)
    k, p, part, q6 = lane // 36, lane % 36 // 12, lane % 12 // 6, lane % 6
    slab = 3 * np.arange(TILES)[:, None] + k[None, :]
    used = ((lane < 108)[None, :] & (slab < SLABS)).reshape(-1)
    x = (PLANES * slab + p[None, :]).reshape(-1)
    part, q6 = np.tile(part, TILES), np.tile(q6, TILES)
    column = np.arange(512)
    part_out, rest = column // 256, column % 256
    q6_out, i = rest // KX, rest % KX
    angle = 2.0 * np.pi * (x[:, None] * wave(i)[None, :] % N) / N
    cosine, sine = np.cos(angle), np.sin(angle)
    same = part[:, None] == part_out[None, :]
    table = np.where(same, cosine, np.where(part[:, None] == 1, sine, -sine)) / math.sqrt(N)
    keep = used[:, None] & (rest < 6 * KX)[None, :] & (q6[:, None] == q6_out[None, :])
    return np.where(keep, table, 0.0)


@functools.cache
def tables():
    yz, x = yz_table(), x_table()
    yz_two, x_two = halves(yz), halves(x)
    forward = np.ascontiguousarray(yz_two.reshape(2, CELLS, 3, 256).transpose(2, 0, 1, 3))
    inverse = np.ascontiguousarray(yz_two.transpose(0, 2, 1).reshape(2, WIDE, 9, 256).transpose(2, 0, 1, 3))
    x_inverse = np.ascontiguousarray(x_two.transpose(0, 2, 1))
    own = np.arange(512) // KX
    weight = np.stack([np.where((6 * parity + own) % MZ == 0, 1.0, 2.0) for parity in range(2)])
    weight = np.broadcast_to(weight[:, None, :], (2, 8, 512)).astype(np.float32)
    return forward, inverse, x_two, x_inverse, np.ascontiguousarray(weight)


def times(value, high, low):
    rows = value.shape[0]
    top = value.astype(BF16)
    wide = top.astype(F32)
    both = jnp.concatenate([wide, value - wide], axis=0).astype(BF16)
    first = jnp.dot(both, high, preferred_element_type=F32)
    return first[:rows] + first[rows:] + jnp.dot(top, low, preferred_element_type=F32)


def kernel(
    wake_hbm, cot_hbm, weight_hbm, point_weight, bias_term, kz_weight, fwd_hbm, inv_hbm, x_hbm, xt_hbm,
    out_vmem, grad_vmem, gathered, sums_ref,
    wake, cot, weight, fwd, inv, xf, xt,
    values, slopes, maps, spectra, slab, grads, lined, pieces, modes, mixed, grad_modes, matrix,
    send, recv, all_modes, all_grads, partial, landed, sums8, sums4,
    load_sem, send_sem, recv_sem, dp_send, dp_recv, x_send, x_recv, z_send, z_recv,
):
    dp = lax.axis_index("dp")
    me = lax.axis_index("space")
    z_hi, eight = dp // 8, dp % 8
    x_pos, core = eight // 2, eight % 2
    lane = lax.broadcasted_iota(jnp.int32, (C, 128), 1)
    third = lane // 36
    slot = jnp.where(lane < 108, lane % 36 // 12, 3)
    even = lax.broadcasted_iota(jnp.int32, (PAIRS, 128), 0) % 2 == 0

    loads = [
        pltpu.make_async_copy(wake_hbm, wake, load_sem.at[0]),
        pltpu.make_async_copy(fwd_hbm.at[0], fwd.at[0], load_sem.at[1]),
        pltpu.make_async_copy(fwd_hbm.at[1], fwd.at[1], load_sem.at[2]),
        pltpu.make_async_copy(fwd_hbm.at[2], fwd.at[2], load_sem.at[3]),
        pltpu.make_async_copy(weight_hbm, weight, load_sem.at[4]),
        pltpu.make_async_copy(cot_hbm, cot, load_sem.at[5]),
        pltpu.make_async_copy(x_hbm, xf, load_sem.at[6]),
        pltpu.make_async_copy(xt_hbm, xt, load_sem.at[7]),
        pltpu.make_async_copy(inv_hbm, inv, load_sem.at[8]),
    ]
    for load in loads[:4]:
        load.start()

    barrier = pltpu.get_barrier_semaphore()
    for r in range(1, 16):
        pl.semaphore_signal(barrier, inc=1, device_id=(dp, (me + r) % 16), device_id_type=MESH)
    for r in range(1, 8):
        peer = z_hi * 8 + (eight + r) % 8
        pl.semaphore_signal(barrier, inc=1, device_id=(peer, me), device_id_type=MESH)
    for r in range(1, 4):
        peer = (z_hi + r) % 4 * 8 + eight
        pl.semaphore_signal(barrier, inc=1, device_id=(peer, me), device_id_type=MESH)

    values[...] = jnp.zeros((TALL, CELLS), F32)
    lined[...] = jnp.zeros((TALL, WIDE), F32)
    loads[0].wait()
    for p in range(PLANES):
        values[ROWS * p : ROWS * p + C, :] = wake[0, 0, p].astype(F32)

    def space_copy(phase, r):
        to = (me + r) % 16
        return pltpu.make_async_remote_copy(
            src_ref=send.at[phase, to], dst_ref=recv.at[phase, me],
            send_sem=send_sem.at[phase, r], recv_sem=recv_sem.at[phase, r],
            device_id=(dp, to), device_id_type=MESH,
        )

    def space_start(phase):
        for r in range(1, 16):
            space_copy(phase, r).start()
        recv[phase, me] = send[phase, me]

    def space_wait(phase):
        for r in range(1, 16):
            space_copy(phase, r).wait()

    def turn(value, shift):
        shift %= 128
        return value if shift == 0 else pltpu.roll(value, shift, 1)

    def other(value):
        return jnp.where(even, pltpu.roll(value, PAIRS - 1, 0), -pltpu.roll(value, 1, 0))

    def choose(where, parts):
        total = jnp.zeros((C, 128), F32)
        for index, part in parts:
            total = jnp.where(where == index, part, total)
        return total

    def slab_to_owners(phase, ride):
        for t in range(TILES):
            held = [spectra[ROWS * p : ROWS * p + C, 128 * t : 128 * t + 128] for p in range(PLANES)]
            for k in range(3):
                if 3 * t + k < SLABS:
                    message = choose(slot, [(p, turn(held[p], 12 * (p - k))) for p in range(PLANES)])
                    send[phase, 3 * t + k] = message if ride is None else message + ride

    def owners_to_slab(phase):
        for t in range(TILES):
            ks = [k for k in range(3) if 3 * t + k < SLABS]
            held = [recv[phase, 3 * t + k] for k in ks]
            for p in range(PLANES):
                lined[ROWS * p : ROWS * p + C, 128 * t : 128 * t + 128] = choose(
                    slot, [(k, turn(held[k], 12 * (k - p))) for k in ks]
                )

    def line_up_planes(phase):
        for u in range(TILES):
            ks = [k for k in range(3) if 3 * u + k < SLABS]
            held = [recv[phase, 3 * u + k] for k in ks]
            for g in range(3):
                lined[ROWS * g : ROWS * g + C, 128 * u : 128 * u + 128] = choose(
                    third, [(k, turn(held[k], 36 * (k - g))) for k in ks]
                )

    def planes_to_slabs(phase, ride):
        for u in range(TILES):
            held = [slab[ROWS * g : ROWS * g + C, 128 * u : 128 * u + 128] for g in range(3)]
            for k in range(3):
                if 3 * u + k < SLABS:
                    message = choose(third, [(g, turn(held[g], 36 * (g - k))) for g in range(3)])
                    send[phase, 3 * u + k] = message if ride is None else message + ride

    def along_x(target, scale):
        result = times(lined[...], xf[0], xf[1])
        for part in range(2):
            block = [result[ROWS * g : ROWS * g + ROWS, 256 * part : 256 * part + 256] for g in range(3)]
            second, last = pltpu.roll(block[1], 16, 1), pltpu.roll(block[2], 32, 1)
            strips = [
                block[0][:, :128],
                block[0][:, 128:] + second[:, :128],
                second[:, 128:] + last[:, :128],
                last[:, 128:],
            ]
            for j in range(4):
                strip = strips[j][:C]
                if scale is not None:
                    strip = strip * scale[:, 128 * j : 128 * j + 128]
                target[j, pl.ds(part, C, stride=2), :] = strip

    def back_along_x():
        for part in range(2):
            strips = [mixed[j, pl.ds(part, C, stride=2), :] for j in range(4)]
            full = jnp.concatenate(strips, axis=1)
            pieces[0:C, 256 * part : 256 * part + 256] = full[:, :256]
            pieces[ROWS : ROWS + C, 256 * part : 256 * part + 256] = pltpu.roll(full, 512 - 144, 1)[:, :256]
            pieces[2 * ROWS : 2 * ROWS + C, 256 * part : 256 * part + 256] = pltpu.roll(full, 512 - 288, 1)[:, :256]
        slab[...] = times(pieces[...], xt[0], xt[1])

    def strip_at(index):
        return pl.ds(pl.multiple_of(index * 128, 128), 128)

    def gather_copy(kind, source, target, r):
        to = (eight + r) % 8
        return pltpu.make_async_remote_copy(
            src_ref=source.at[to // 2], dst_ref=target.at[eight],
            send_sem=dp_send.at[kind, r], recv_sem=dp_recv.at[kind, r],
            device_id=(z_hi * 8 + to, me), device_id_type=MESH,
        )

    def gather_start(kind, source, target):
        for r in range(1, 8):
            gather_copy(kind, source, target, r).start()
        target[eight] = source[x_pos]

    tall = values[...].astype(BF16)
    for n in range(3):
        loads[1 + n].wait()
        spectra[:, 256 * n : 256 * n + 256] = jnp.dot(
            tall, fwd[n, 0], preferred_element_type=F32
        ) + jnp.dot(tall, fwd[n, 1], preferred_element_type=F32)
    for load in loads[4:]:
        load.start()
    slab_to_owners(0, None)
    pl.semaphore_wait(barrier, 25)
    space_start(0)

    pieces[...] = jnp.zeros((TALL, 512), F32)
    maps[:, :, 384:] = jnp.zeros((C, PAIRS, 128), F32)
    matrix[...] = jnp.zeros((ROWS, 128), F32)
    slopes[...] = jnp.zeros((TALL, CELLS), F32)
    matrix[0:C, 0:C] = point_weight[...].astype(F32)
    loads[4].wait()

    def cast_step(c, carry):
        maps[c, :, :MODES] = weight[c].astype(F32).reshape(PAIRS, MODES)
        return carry

    lax.fori_loop(0, C, cast_step, 0)
    loads[5].wait()
    for p in range(PLANES):
        slopes[ROWS * p : ROWS * p + C, :] = cot[0, 0, p].astype(F32)
    for load in loads[6:]:
        load.wait()

    space_wait(0)
    line_up_planes(0)
    along_x(modes, None)
    gather_start(0, modes, all_modes)
    row = kz_weight[me % 2, 0:1, :]

    def mix_step(j, carry):
        strip = strip_at(j)
        first, second = jnp.zeros((PAIRS, 128), F32), jnp.zeros((PAIRS, 128), F32)
        for c in range(C):
            weights = maps[c, :, strip]
            first = first + weights * modes[j, 2 * c : 2 * c + 1, :]
            second = second + weights * modes[j, 2 * c + 1 : 2 * c + 2, :]
        mixed[j] = (first - other(second)) * kz_weight[me % 2, 0:1, strip]
        return carry

    lax.fori_loop(0, 4, mix_step, 0)
    back_along_x()
    planes_to_slabs(1, None)
    space_start(1)

    to_in = jnp.concatenate([turn(matrix[...], ROWS * p) for p in range(PLANES)], axis=0)[:, :TALL].astype(BF16)
    here = lax.broadcasted_iota(jnp.int32, (ROWS, C), 0) == lax.broadcasted_iota(jnp.int32, (ROWS, C), 1)
    bias = jnp.sum(jnp.where(here, bias_term[...], 0.0), axis=1, keepdims=True)
    bias = jnp.concatenate([bias] * PLANES, axis=0)
    for n in range(9):
        columns = slice(256 * n, 256 * n + 256)
        grads[:, columns] = bias + lax.dot_general(
            to_in, values[:, columns].astype(BF16), (((0,), (0,)), ((), ())), preferred_element_type=F32
        )
    space_wait(1)
    owners_to_slab(1)

    full = lined[...]
    rate = math.sqrt(2.0 / math.pi)
    bias_sum = jnp.zeros((TALL, 1), F32)
    for n in range(9):
        columns = slice(256 * n, 256 * n + 256)
        pre = times(full, inv[n, 0], inv[n, 1]) + grads[:, columns]
        square = pre * pre
        bend = jnp.tanh(rate * (pre + 0.044715 * (square * pre)))
        half = 0.5 * (1.0 + bend)
        slope = half + 0.5 * pre * (1.0 - bend * bend) * (rate * (1.0 + 3 * 0.044715 * square))
        active = half * pre
        for p in range(PLANES):
            out_vmem[0, 0, p, :, columns] = active[ROWS * p : ROWS * p + C].astype(BF16)
        slope = slope * slopes[:, columns]
        grads[:, columns] = slope
        bias_sum = bias_sum + jnp.sum(slope, axis=1, keepdims=True)

    full = grads[...]
    for n in range(3):
        spectra[:, 256 * n : 256 * n + 256] = times(full, fwd[n, 0], fwd[n, 1])
    bias_own = bias_sum[:C] + bias_sum[ROWS : ROWS + C] + bias_sum[2 * ROWS : 2 * ROWS + C]
    slab_to_owners(2, jnp.where(lane == 108, bias_own, 0.0))
    space_start(2)

    point = jnp.zeros((ROWS, ROWS), F32)
    last = (((1,), (1,)), ((), ()))
    for p in range(PLANES):
        field = values[ROWS * p : ROWS * p + ROWS, :].astype(BF16)
        slope = grads[ROWS * p : ROWS * p + ROWS, :]
        high = slope.astype(BF16)
        low = (slope - high.astype(F32)).astype(BF16)
        point = point + lax.dot_general(field, high, last, preferred_element_type=F32)
        point = point + lax.dot_general(field, low, last, preferred_element_type=F32)
    point = jnp.concatenate([point[:C], jnp.zeros((C, 128 - ROWS), F32)], axis=1)
    point = jnp.where(lane >= 108, turn(point, 108), 0.0)
    for n in range(9):
        columns = slice(256 * n, 256 * n + 256)
        slope = grads[:, columns]
        high = slope.astype(BF16)
        low = (slope - high.astype(F32)).astype(BF16)
        values[:, columns] = jnp.dot(to_in, high, preferred_element_type=F32) + jnp.dot(
            to_in, low, preferred_element_type=F32
        )

    space_wait(2)
    line_up_planes(2)
    along_x(grad_modes, row)
    gather_start(1, grad_modes, all_grads)

    def grad_step(j, carry):
        strip = strip_at(j)
        slope = grad_modes[j]
        crossed = other(slope)
        for c in range(C):
            weights = maps[c, :, strip]
            mixed[j, 2 * c : 2 * c + 1, :] = jnp.sum(weights * slope, axis=0, keepdims=True)
            mixed[j, 2 * c + 1 : 2 * c + 2, :] = jnp.sum(weights * crossed, axis=0, keepdims=True)
        return carry

    lax.fori_loop(0, 4, grad_step, 0)
    back_along_x()
    planes_to_slabs(3, point)
    space_start(3)

    partial8 = partial.reshape(8, 25, 4, 128)
    gathered8 = gathered.reshape(4, 8, 25, 4, 128)
    for r in range(1, 8):
        gather_copy(0, modes, all_modes, r).wait()
        gather_copy(1, grad_modes, all_grads, r).wait()

    def scatter_copy(r):
        to = (z_hi + r) % 4
        return pltpu.make_async_remote_copy(
            src_ref=partial8.at[to * 2 + core], dst_ref=landed.at[r - 1],
            send_sem=dp_send.at[2, r], recv_sem=dp_recv.at[2, r],
            device_id=(to * 8 + eight, me), device_id_type=MESH,
        )

    for r in (2, 1, 3, 0):
        start = (z_hi + r) % 4 * 5 + 2 * core

        def part_step(i, carry):
            first, second = jnp.zeros((PAIRS, 128), F32), jnp.zeros((PAIRS, 128), F32)
            for b in range(8):
                slope = all_grads[b]
                first = first + all_modes[b, pl.ds(2 * (start + i), 1), :] * slope
                second = second + all_modes[b, pl.ds(2 * (start + i) + 1, 1), :] * slope
            partial[start + i] = first + other(second)
            return carry

        lax.fori_loop(0, 3, part_step, 0)
        if r != 0:
            scatter_copy(r).start()

    bias_total = jnp.zeros((C, 128), F32)
    for s in range(SLABS):
        bias_total = bias_total + recv[2, s]
    space_wait(3)
    owners_to_slab(3)
    point_total = jnp.zeros((C, 128), F32)
    for s in range(SLABS):
        point_total = point_total + recv[3, s]
    sums8[eight] = jnp.where(lane >= 108, point_total, jnp.where(lane == 0, turn(bias_total, 20), 0.0))

    def eight_copy(r):
        to = (eight + r) % 8
        return pltpu.make_async_remote_copy(
            src_ref=sums8.at[eight], dst_ref=sums8.at[eight],
            send_sem=dp_send.at[3, r], recv_sem=dp_recv.at[3, r],
            device_id=(z_hi * 8 + to, me), device_id_type=MESH,
        )

    for r in range(1, 8):
        eight_copy(r).start()

    full = lined[...]
    for n in range(9):
        columns = slice(256 * n, 256 * n + 256)
        result = times(full, inv[n, 0], inv[n, 1]) + values[:, columns]
        for p in range(PLANES):
            grad_vmem[0, 0, p, :, columns] = result[ROWS * p : ROWS * p + C].astype(BF16)

    for r in range(1, 4):
        scatter_copy(r).wait()
    gathered8[x_pos, z_hi * 2 + core] = partial8[z_hi * 2 + core] + landed[0] + landed[1] + landed[2]

    def own(k):
        return (z_hi - k) % 4 * 2 + core

    def to_z(block, send_at, recv_at, r):
        return pltpu.make_async_remote_copy(
            src_ref=block, dst_ref=block, send_sem=send_at, recv_sem=recv_at,
            device_id=((z_hi + r) % 4 * 8 + eight, me), device_id_type=MESH,
        )

    def to_x(block, send_at, recv_at, r):
        return pltpu.make_async_remote_copy(
            src_ref=block, dst_ref=block, send_sem=send_at, recv_sem=recv_at,
            device_id=(z_hi * 8 + (x_pos + r) % 4 * 2 + core, me), device_id_type=MESH,
        )

    def z_copy(r):
        return to_z(gathered8.at[x_pos, own(0), 0:SPLIT], dp_send.at[4, r], dp_recv.at[4, r], r)

    def x_copy(k, r):
        return to_x(gathered8.at[x_pos, own(k), 0:SPLIT], x_send.at[k, r], x_recv.at[k, r], r)

    def x_first(r):
        return to_x(gathered8.at[x_pos, own(0), SPLIT:25], dp_send.at[7, r], dp_recv.at[7, r], r)

    def z_second(j, r):
        return to_z(gathered8.at[(x_pos - j) % 4, own(0), SPLIT:25], z_send.at[j, r], z_recv.at[j, r], r)

    def core_copy(k):
        block = gathered8.at[:, (z_hi - k) % 4 * 2 + core]
        return pltpu.make_async_remote_copy(
            src_ref=block, dst_ref=block,
            send_sem=dp_send.at[6, k], recv_sem=dp_recv.at[6, k],
            device_id=(z_hi * 8 + x_pos * 2 + 1 - core, me), device_id_type=MESH,
        )

    for r in (2, 1, 3):
        x_first(r).start()
    for r in (2, 1, 3):
        z_copy(r).start()
    for r in (2, 1, 3):
        z_second(0, r).start()
        x_copy(0, r).start()

    for r in range(1, 8):
        eight_copy(r).wait()
    total = sums8[0]
    for b in range(1, 8):
        total = total + sums8[b]
    sums4[z_hi] = total

    def four_copy(r):
        to = (z_hi + r) % 4
        return pltpu.make_async_remote_copy(
            src_ref=sums4.at[z_hi], dst_ref=sums4.at[z_hi],
            send_sem=dp_send.at[5, r], recv_sem=dp_recv.at[5, r],
            device_id=(to * 8 + eight, me), device_id_type=MESH,
        )

    for r in range(1, 4):
        four_copy(r).start()
    for j in (1, 3, 2):
        x_first(j).wait_recv()
        for r in (2, 1, 3):
            z_second(j, r).start()
    for k in (1, 3, 2):
        z_copy(k).wait_recv()
        for r in (2, 1, 3):
            x_copy(k, r).start()
    order = (0, 1, 3, 2)
    for k in order:
        for r in range(1, 4):
            x_copy(k, r).wait_recv()
        if k != 0:
            for j in range(4):
                z_second(j, k).wait_recv()
        core_copy(k).start()
    for r in range(1, 4):
        four_copy(r).wait()
    total = turn(sums4[0] + sums4[1] + sums4[2] + sums4[3], 20)
    sums_ref[0:C, :] = total
    square = lax.broadcasted_iota(jnp.int32, (C, 128), 0) == lane
    sums_ref[C : C + 1, :] = jnp.sum(jnp.where(square, total[:, C : C + 1], 0.0), axis=0, keepdims=True)
    for r in range(1, 4):
        z_copy(r).wait_send()
        x_first(r).wait_send()
        for j in range(4):
            z_second(j, r).wait_send()
        for k in range(4):
            x_copy(k, r).wait_send()
    for k in order:
        core_copy(k).wait()


def results(out_from, grad_from, spec_from, sums, out_to, grad_to, spec_to, point_to, bias_to, sem):
    copies = []
    strips = spec_from.reshape(4, C, C, 2, 128)
    for j in range(4):
        for k in range(4):
            rows = pl.ds(5 * k, 5)
            copies.append(
                pltpu.make_async_copy(
                    strips.at[j, rows], spec_to.at[rows, :, :, 128 * j : 128 * j + 128], sem.at[4 * j + k]
                )
            )
    for p in range(PLANES):
        copies.append(pltpu.make_async_copy(out_from.at[0, 0, p], out_to.at[0, 0, p], sem.at[16 + p]))
        copies.append(pltpu.make_async_copy(grad_from.at[0, 0, p], grad_to.at[0, 0, p], sem.at[19 + p]))
    for copy in copies:
        copy.start()
    point_to[...] = sums[0:C, 0:C]
    bias_to[...] = sums[C : C + 1, 0:C]
    for copy in copies:
        copy.wait()


def on_device(wake_field, spec_weight, point_weight, bias_term, cotangent):
    forward, inverse, x_two, x_inverse, kz_weight = tables()
    weight = spec_weight.transpose(1, 2, 0, 3)
    anywhere = pl.BlockSpec(memory_space=pl.ANY)
    inside = pl.BlockSpec(memory_space=pltpu.VMEM)
    field = wake_field.shape
    output_field, grad_field, grad_spec, sums = pl.pallas_call(
        kernel,
        out_shape=(
            pltpu.VMEM(field, BF16),
            pltpu.VMEM(field, BF16),
            pltpu.VMEM((4, C, PAIRS, 128), F32),
            pltpu.VMEM((ROWS, 128), F32),
        ),
        in_specs=[anywhere] * 3 + [inside] * 3 + [anywhere] * 4,
        out_specs=(inside, inside, inside, inside),
        scratch_shapes=[
            pltpu.VMEM(field, BF16),
            pltpu.VMEM(field, BF16),
            pltpu.VMEM(weight.shape, BF16),
            pltpu.VMEM(forward.shape, BF16),
            pltpu.VMEM(inverse.shape, BF16),
            pltpu.VMEM(x_two.shape, BF16),
            pltpu.VMEM(x_inverse.shape, BF16),
            pltpu.VMEM((TALL, CELLS), F32),
            pltpu.VMEM((TALL, CELLS), F32),
            pltpu.VMEM((C, PAIRS, 512), F32),
            pltpu.VMEM((TALL, WIDE), F32),
            pltpu.VMEM((TALL, WIDE), F32),
            pltpu.VMEM((TALL, CELLS), F32),
            pltpu.VMEM((TALL, WIDE), F32),
            pltpu.VMEM((TALL, 512), F32),
            pltpu.VMEM((4, PAIRS, 128), F32),
            pltpu.VMEM((4, PAIRS, 128), F32),
            pltpu.VMEM((4, PAIRS, 128), F32),
            pltpu.VMEM((ROWS, 128), F32),
            pltpu.VMEM((4, SLABS, C, 128), F32),
            pltpu.VMEM((4, SLABS, C, 128), F32),
            pltpu.VMEM((8, PAIRS, 128), F32),
            pltpu.VMEM((8, PAIRS, 128), F32),
            pltpu.VMEM((C, PAIRS, 128), F32),
            pltpu.VMEM((3, 25, 4, 128), F32),
            pltpu.VMEM((8, C, 128), F32),
            pltpu.VMEM((4, C, 128), F32),
            pltpu.SemaphoreType.DMA((9,)),
            pltpu.SemaphoreType.DMA((4, 16)),
            pltpu.SemaphoreType.DMA((4, 16)),
            pltpu.SemaphoreType.DMA((8, 8)),
            pltpu.SemaphoreType.DMA((8, 8)),
            pltpu.SemaphoreType.DMA((4, 4)),
            pltpu.SemaphoreType.DMA((4, 4)),
            pltpu.SemaphoreType.DMA((4, 4)),
            pltpu.SemaphoreType.DMA((4, 4)),
        ],
        compiler_params=pltpu.CompilerParams(
            collective_id=0, has_side_effects=True, vmem_limit_bytes=52 * 1024 * 1024
        ),
    )(wake_field, cotangent, weight, point_weight, bias_term[None], kz_weight, forward, inverse, x_two, x_inverse)
    output_field, grad_field, grad_spec, grad_point, grad_bias = pl.pallas_call(
        results,
        out_shape=(
            jax.ShapeDtypeStruct(field, BF16),
            jax.ShapeDtypeStruct(field, BF16),
            jax.ShapeDtypeStruct((C, C, 2, 512), F32),
            jax.ShapeDtypeStruct((C, C), F32),
            jax.ShapeDtypeStruct((1, C), F32),
        ),
        in_specs=[inside] * 4,
        out_specs=(anywhere, anywhere, anywhere, inside, inside),
        scratch_shapes=[pltpu.SemaphoreType.DMA((22,))],
    )(*[pltpu.with_memory_space_constraint(array, pltpu.VMEM) for array in (output_field, grad_field, grad_spec, sums)])
    return (
        output_field,
        grad_field,
        grad_spec.transpose(2, 0, 1, 3)[..., :MODES],
        grad_point,
        grad_bias.reshape(C),
    )


def solution(mesh):
    placed = (
        P("dp", None, "space", None, None),
        P(None, None, None, "space"),
        P(),
        P(),
        P("dp", None, "space", None, None),
    )
    return jax.shard_map(
        on_device,
        mesh=mesh,
        in_specs=placed,
        out_specs=(
            P("dp", None, "space", None, None),
            P("dp", None, "space", None, None),
            P(None, None, None, "space"),
            P(),
            P(),
        ),
        check_vma=False,
    )
```

```python
import functools
import math

import jax
import jax.numpy as jnp
import numpy as np
from jax import lax
from jax.experimental import pallas as pl
from jax.experimental.pallas import tpu as pltpu
from jax.sharding import PartitionSpec as P

MESH = pl.DeviceIdType.MESH
F32 = jnp.float32
BF16 = jnp.bfloat16

C = 20
N = 48
MZ = 12
CELLS = N * N
KX = 24
SLABS = 16
PLANES = 3
OWN = 18
MODES = OWN * KX
ROWS = 24
TALL = PLANES * ROWS
TILES = 6
WIDE = TILES * 128
PAIRS = 2 * C
SPLIT = 8


def wave(i):
    return np.where(i < 12, i, i - 24)


def halves(table):
    high = table.astype(np.float32).astype(BF16)
    low = (table - high.astype(np.float64)).astype(np.float32).astype(BF16)
    return np.stack([high, low])


def yz_table():
    lane = np.arange(128)
    g, k, part, q6 = lane // 36, lane % 36 // 12, lane % 12 // 6, lane % 6
    owner = 3 * np.arange(TILES)[:, None] + k[None, :]
    used = (lane < 108)[None, :] & (owner < SLABS)
    q = OWN * owner + 6 * g[None, :] + q6[None, :]
    ky, kz = wave(q // MZ), q % MZ
    cell = np.arange(CELLS)
    y, z = cell // N, cell % N
    phase = (y[:, None, None] * ky[None] + z[:, None, None] * kz[None]) % N
    angle = 2.0 * np.pi * phase / N
    table = np.where(part == 0, np.cos(angle), -np.sin(angle)) / N
    return np.where(used[None], table, 0.0).reshape(CELLS, WIDE)


def x_table():
    lane = np.arange(128)
    k, p, part, q6 = lane // 36, lane % 36 // 12, lane % 12 // 6, lane % 6
    slab = 3 * np.arange(TILES)[:, None] + k[None, :]
    used = ((lane < 108)[None, :] & (slab < SLABS)).reshape(-1)
    x = (PLANES * slab + p[None, :]).reshape(-1)
    part, q6 = np.tile(part, TILES), np.tile(q6, TILES)
    column = np.arange(512)
    part_out, rest = column // 256, column % 256
    q6_out, i = rest // KX, rest % KX
    angle = 2.0 * np.pi * (x[:, None] * wave(i)[None, :] % N) / N
    cosine, sine = np.cos(angle), np.sin(angle)
    same = part[:, None] == part_out[None, :]
    table = np.where(same, cosine, np.where(part[:, None] == 1, sine, -sine)) / math.sqrt(N)
    keep = used[:, None] & (rest < 6 * KX)[None, :] & (q6[:, None] == q6_out[None, :])
    return np.where(keep, table, 0.0)


@functools.cache
def tables():
    yz, x = yz_table(), x_table()
    yz_two, x_two = halves(yz), halves(x)
    forward = np.ascontiguousarray(yz_two.reshape(2, CELLS, 3, 256).transpose(2, 0, 1, 3))
    inverse = np.ascontiguousarray(yz_two.transpose(0, 2, 1).reshape(2, WIDE, 9, 256).transpose(2, 0, 1, 3))
    x_inverse = np.ascontiguousarray(x_two.transpose(0, 2, 1))
    own = np.arange(512) // KX
    weight = np.stack([np.where((6 * parity + own) % MZ == 0, 1.0, 2.0) for parity in range(2)])
    weight = np.broadcast_to(weight[:, None, :], (2, 8, 512)).astype(np.float32)
    return forward, inverse, x_two, x_inverse, np.ascontiguousarray(weight)


def times(value, high, low):
    rows = value.shape[0]
    top = value.astype(BF16)
    wide = top.astype(F32)
    both = jnp.concatenate([wide, value - wide], axis=0).astype(BF16)
    first = jnp.dot(both, high, preferred_element_type=F32)
    return first[:rows] + first[rows:] + jnp.dot(top, low, preferred_element_type=F32)


def kernel(
    wake_hbm, cot_hbm, weight_hbm, point_weight, bias_term, kz_weight, fwd_hbm, inv_hbm, x_hbm, xt_hbm,
    out_vmem, grad_vmem, gathered, sums_ref,
    wake, cot, weight, fwd, inv, xf, xt,
    values, slopes, maps, spectra, slab, grads, lined, pieces, modes, mixed, grad_modes, matrix,
    send, recv, all_modes, all_grads, partial, landed, own_sum, sums8, sums4,
    load_sem, local_sem, send_sem, recv_sem, dp_send, dp_recv, x_send, x_recv, z_send, z_recv,
):
    dp = lax.axis_index("dp")
    me = lax.axis_index("space")
    z_hi, eight = dp // 8, dp % 8
    x_pos, core = eight // 2, eight % 2
    lane = lax.broadcasted_iota(jnp.int32, (C, 128), 1)
    third = lane // 36
    slot = jnp.where(lane < 108, lane % 36 // 12, 3)
    home = z_hi * 4 + x_pos
    far_first = (8, 7, 9, 6, 10, 5, 11, 4, 12, 3, 13, 2, 14, 1, 15)

    loads = [
        pltpu.make_async_copy(wake_hbm, wake, load_sem.at[0]),
        pltpu.make_async_copy(fwd_hbm.at[0], fwd.at[0], load_sem.at[1]),
        pltpu.make_async_copy(fwd_hbm.at[1], fwd.at[1], load_sem.at[2]),
        pltpu.make_async_copy(fwd_hbm.at[2], fwd.at[2], load_sem.at[3]),
        pltpu.make_async_copy(weight_hbm, weight, load_sem.at[4]),
        pltpu.make_async_copy(cot_hbm, cot, load_sem.at[5]),
        pltpu.make_async_copy(x_hbm, xf, load_sem.at[6]),
        pltpu.make_async_copy(xt_hbm, xt, load_sem.at[7]),
        pltpu.make_async_copy(inv_hbm, inv, load_sem.at[8]),
    ]
    for load in loads[:4]:
        load.start()

    barrier = pltpu.get_barrier_semaphore()
    for r in range(1, 16):
        pl.semaphore_signal(barrier, inc=1, device_id=(dp, (me + r) % 16), device_id_type=MESH)
    for r in range(1, 8):
        peer = z_hi * 8 + (eight + r) % 8
        pl.semaphore_signal(barrier, inc=1, device_id=(peer, me), device_id_type=MESH)
    for i in range(1, 4):
        for j in range(4):
            peer = (z_hi + i) % 4 * 8 + (x_pos + j) % 4 * 2 + core
            pl.semaphore_signal(barrier, inc=1, device_id=(peer, me), device_id_type=MESH)

    values[...] = jnp.zeros((TALL, CELLS), F32)
    lined[...] = jnp.zeros((TALL, WIDE), F32)
    loads[0].wait()
    for p in range(PLANES):
        values[ROWS * p : ROWS * p + C, :] = wake[0, 0, p].astype(F32)

    def space_copy(phase, r):
        to = (me + r) % 16
        return pltpu.make_async_remote_copy(
            src_ref=send.at[phase, to], dst_ref=recv.at[phase, me],
            send_sem=send_sem.at[phase, r], recv_sem=recv_sem.at[phase, r],
            device_id=(dp, to), device_id_type=MESH,
        )

    def space_start(phase):
        for r in range(1, 16):
            space_copy(phase, r).start()
        recv[phase, me] = send[phase, me]

    def space_wait(phase):
        for r in range(1, 16):
            space_copy(phase, r).wait()

    def turn(value, shift):
        shift %= 128
        return value if shift == 0 else pltpu.roll(value, shift, 1)

    def other(value):
        rows = value.shape[0]
        even = lax.broadcasted_iota(jnp.int32, (rows, 128), 0) % 2 == 0
        return jnp.where(even, pltpu.roll(value, rows - 1, 0), -pltpu.roll(value, 1, 0))

    def choose(where, parts):
        total = jnp.zeros((C, 128), F32)
        for index, part in parts:
            total = jnp.where(where == index, part, total)
        return total

    def slab_to_owners(phase, ride):
        for t in range(TILES):
            held = [spectra[ROWS * p : ROWS * p + C, 128 * t : 128 * t + 128] for p in range(PLANES)]
            for k in range(3):
                if 3 * t + k < SLABS:
                    message = choose(slot, [(p, turn(held[p], 12 * (p - k))) for p in range(PLANES)])
                    send[phase, 3 * t + k] = message if ride is None else message + ride

    def owners_to_slab(phase):
        for t in range(TILES):
            ks = [k for k in range(3) if 3 * t + k < SLABS]
            held = [recv[phase, 3 * t + k] for k in ks]
            for p in range(PLANES):
                lined[ROWS * p : ROWS * p + C, 128 * t : 128 * t + 128] = choose(
                    slot, [(k, turn(held[k], 12 * (k - p))) for k in ks]
                )

    def line_up_planes(phase):
        for u in range(TILES):
            ks = [k for k in range(3) if 3 * u + k < SLABS]
            held = [recv[phase, 3 * u + k] for k in ks]
            for g in range(3):
                lined[ROWS * g : ROWS * g + C, 128 * u : 128 * u + 128] = choose(
                    third, [(k, turn(held[k], 36 * (k - g))) for k in ks]
                )

    def planes_to_slabs(phase, ride):
        for u in range(TILES):
            held = [slab[ROWS * g : ROWS * g + C, 128 * u : 128 * u + 128] for g in range(3)]
            for k in range(3):
                if 3 * u + k < SLABS:
                    message = choose(third, [(g, turn(held[g], 36 * (g - k))) for g in range(3)])
                    send[phase, 3 * u + k] = message if ride is None else message + ride

    def along_x(target, scale):
        result = times(lined[...], xf[0], xf[1])
        for part in range(2):
            block = [result[ROWS * g : ROWS * g + ROWS, 256 * part : 256 * part + 256] for g in range(3)]
            second, last = pltpu.roll(block[1], 16, 1), pltpu.roll(block[2], 32, 1)
            strips = [
                block[0][:, :128],
                block[0][:, 128:] + second[:, :128],
                second[:, 128:] + last[:, :128],
                last[:, 128:],
            ]
            for j in range(4):
                strip = strips[j][:C]
                if scale is not None:
                    strip = strip * scale[:, 128 * j : 128 * j + 128]
                target[j, pl.ds(part, C, stride=2), :] = strip

    def back_along_x():
        for part in range(2):
            strips = [mixed[j, pl.ds(part, C, stride=2), :] for j in range(4)]
            full = jnp.concatenate(strips, axis=1)
            pieces[0:C, 256 * part : 256 * part + 256] = full[:, :256]
            pieces[ROWS : ROWS + C, 256 * part : 256 * part + 256] = pltpu.roll(full, 512 - 144, 1)[:, :256]
            pieces[2 * ROWS : 2 * ROWS + C, 256 * part : 256 * part + 256] = pltpu.roll(full, 512 - 288, 1)[:, :256]
        slab[...] = times(pieces[...], xt[0], xt[1])

    def strip_at(index):
        return pl.ds(pl.multiple_of(index * 128, 128), 128)

    grad_pairs = grad_modes.reshape(4, C, 2, 128)
    landing = all_grads.reshape(16, 8, 2, 128)

    def gather_to(r):
        to = (home + r) % 16
        return to // 4, to % 4, (to * 2 + core, me)

    def modes_copy(r):
        _, x_to, device = gather_to(r)
        return pltpu.make_async_remote_copy(
            src_ref=modes.at[x_to], dst_ref=all_modes.at[home],
            send_sem=dp_send.at[0, r], recv_sem=dp_recv.at[0, r],
            device_id=device, device_id_type=MESH,
        )

    def grads_copy(r):
        z_to, x_to, device = gather_to(r)
        return pltpu.make_async_remote_copy(
            src_ref=grad_pairs.at[x_to, pl.ds(5 * z_to, 5)], dst_ref=landing.at[home, 0:5],
            send_sem=dp_send.at[1, r], recv_sem=dp_recv.at[1, r],
            device_id=device, device_id_type=MESH,
        )

    grads_own = pltpu.make_async_copy(
        grad_pairs.at[x_pos, pl.ds(5 * z_hi, 5)], landing.at[home, 0:5], local_sem.at[0]
    )

    tall = values[...].astype(BF16)
    for n in range(3):
        loads[1 + n].wait()
        spectra[:, 256 * n : 256 * n + 256] = jnp.dot(
            tall, fwd[n, 0], preferred_element_type=F32
        ) + jnp.dot(tall, fwd[n, 1], preferred_element_type=F32)
    for load in loads[4:]:
        load.start()
    slab_to_owners(0, None)
    pl.semaphore_wait(barrier, 34)
    space_start(0)

    pieces[...] = jnp.zeros((TALL, 512), F32)
    maps[:, :, 384:] = jnp.zeros((C, PAIRS, 128), F32)
    matrix[...] = jnp.zeros((ROWS, 128), F32)
    slopes[...] = jnp.zeros((TALL, CELLS), F32)
    matrix[0:C, 0:C] = point_weight[...].astype(F32)
    loads[4].wait()

    def cast_step(c, carry):
        maps[c, :, :MODES] = weight[c].astype(F32).reshape(PAIRS, MODES)
        return carry

    lax.fori_loop(0, C, cast_step, 0)
    loads[5].wait()
    for p in range(PLANES):
        slopes[ROWS * p : ROWS * p + C, :] = cot[0, 0, p].astype(F32)
    for load in loads[6:]:
        load.wait()

    space_wait(0)
    line_up_planes(0)
    along_x(modes, None)
    row = kz_weight[me % 2, 0:1, :]

    def mix_step(j, carry):
        strip = strip_at(j)
        first, second = jnp.zeros((PAIRS, 128), F32), jnp.zeros((PAIRS, 128), F32)
        for c in range(C):
            weights = maps[c, :, strip]
            first = first + weights * modes[j, 2 * c : 2 * c + 1, :]
            second = second + weights * modes[j, 2 * c + 1 : 2 * c + 2, :]
        mixed[j] = (first - other(second)) * kz_weight[me % 2, 0:1, strip]
        return carry

    lax.fori_loop(0, 4, mix_step, 0)
    back_along_x()
    planes_to_slabs(1, None)
    space_start(1)

    to_in = jnp.concatenate([turn(matrix[...], ROWS * p) for p in range(PLANES)], axis=0)[:, :TALL].astype(BF16)
    here = lax.broadcasted_iota(jnp.int32, (ROWS, C), 0) == lax.broadcasted_iota(jnp.int32, (ROWS, C), 1)
    bias = jnp.sum(jnp.where(here, bias_term[...], 0.0), axis=1, keepdims=True)
    bias = jnp.concatenate([bias] * PLANES, axis=0)
    for n in range(9):
        columns = slice(256 * n, 256 * n + 256)
        grads[:, columns] = bias + lax.dot_general(
            to_in, values[:, columns].astype(BF16), (((0,), (0,)), ((), ())), preferred_element_type=F32
        )
    space_wait(1)
    for r in far_first:
        modes_copy(r).start()
    all_modes[home] = modes[x_pos]
    owners_to_slab(1)

    full = lined[...]
    rate = math.sqrt(2.0 / math.pi)
    bias_sum = jnp.zeros((TALL, 1), F32)
    for n in range(9):
        columns = slice(256 * n, 256 * n + 256)
        pre = times(full, inv[n, 0], inv[n, 1]) + grads[:, columns]
        square = pre * pre
        bend = jnp.tanh(rate * (pre + 0.044715 * (square * pre)))
        half = 0.5 * (1.0 + bend)
        slope = half + 0.5 * pre * (1.0 - bend * bend) * (rate * (1.0 + 3 * 0.044715 * square))
        active = half * pre
        for p in range(PLANES):
            out_vmem[0, 0, p, :, columns] = active[ROWS * p : ROWS * p + C].astype(BF16)
        slope = slope * slopes[:, columns]
        grads[:, columns] = slope
        bias_sum = bias_sum + jnp.sum(slope, axis=1, keepdims=True)

    full = grads[...]
    for n in range(3):
        spectra[:, 256 * n : 256 * n + 256] = times(full, fwd[n, 0], fwd[n, 1])
    bias_own = bias_sum[:C] + bias_sum[ROWS : ROWS + C] + bias_sum[2 * ROWS : 2 * ROWS + C]
    slab_to_owners(2, jnp.where(lane == 108, bias_own, 0.0))
    space_start(2)

    point = jnp.zeros((ROWS, ROWS), F32)
    last = (((1,), (1,)), ((), ()))
    for p in range(PLANES):
        field = values[ROWS * p : ROWS * p + ROWS, :].astype(BF16)
        slope = grads[ROWS * p : ROWS * p + ROWS, :]
        high = slope.astype(BF16)
        low = (slope - high.astype(F32)).astype(BF16)
        point = point + lax.dot_general(field, high, last, preferred_element_type=F32)
        point = point + lax.dot_general(field, low, last, preferred_element_type=F32)
    point = jnp.concatenate([point[:C], jnp.zeros((C, 128 - ROWS), F32)], axis=1)
    point = jnp.where(lane >= 108, turn(point, 108), 0.0)
    for n in range(9):
        columns = slice(256 * n, 256 * n + 256)
        slope = grads[:, columns]
        high = slope.astype(BF16)
        low = (slope - high.astype(F32)).astype(BF16)
        values[:, columns] = jnp.dot(to_in, high, preferred_element_type=F32) + jnp.dot(
            to_in, low, preferred_element_type=F32
        )

    space_wait(2)
    line_up_planes(2)
    along_x(grad_modes, row)
    for r in far_first:
        grads_copy(r).start()
    grads_own.start()

    def grad_step(j, carry):
        strip = strip_at(j)
        slope = grad_modes[j]
        crossed = other(slope)
        for c in range(C):
            weights = maps[c, :, strip]
            mixed[j, 2 * c : 2 * c + 1, :] = jnp.sum(weights * slope, axis=0, keepdims=True)
            mixed[j, 2 * c + 1 : 2 * c + 2, :] = jnp.sum(weights * crossed, axis=0, keepdims=True)
        return carry

    lax.fori_loop(0, 4, grad_step, 0)
    back_along_x()
    planes_to_slabs(3, point)
    space_start(3)

    partial_pairs = partial.reshape(C, 8, 2, 128)
    own_pairs = own_sum.reshape(10, 8, 2, 128)
    blocks = gathered.reshape(4, C, C, 2, 128)
    for r in far_first:
        modes_copy(r).wait()
        grads_copy(r).wait()
    grads_own.wait()

    def part_step(i, carry):
        c = (i + 10 * (1 - core)) % C
        first, second = jnp.zeros((16, 128), F32), jnp.zeros((16, 128), F32)
        for b in range(16):
            slope = all_grads[b]
            first = first + all_modes[b, pl.ds(2 * c, 1), :] * slope
            second = second + all_modes[b, pl.ds(2 * c + 1, 1), :] * slope
        partial[c] = first + other(second)
        return carry

    core_sum = pltpu.make_async_remote_copy(
        src_ref=partial_pairs.at[pl.ds(10 * (1 - core), 10), 0:5],
        dst_ref=landed.reshape(10, 8, 2, 128).at[:, 0:5],
        send_sem=dp_send.at[2, 0], recv_sem=dp_recv.at[2, 0],
        device_id=(z_hi * 8 + x_pos * 2 + 1 - core, me), device_id_type=MESH,
    )
    lax.fori_loop(0, 10, part_step, 0)
    core_sum.start()
    lax.fori_loop(10, 20, part_step, 0)
    core_sum.wait()
    for j in range(10):
        own_sum[j] = partial[10 * core + j] + landed[j]

    def first_part(strip, k):
        return blocks.at[strip, pl.ds(10 * core, SPLIT), pl.ds((z_hi - k) % 4 * 5, 5)]

    def second_part(strip, k):
        return blocks.at[strip, pl.ds(10 * core + SPLIT, 10 - SPLIT), pl.ds((z_hi - k) % 4 * 5, 5)]

    own_first = own_pairs.at[0:SPLIT, 0:5]
    own_second = own_pairs.at[SPLIT:10, 0:5]
    keep = pltpu.make_async_copy(
        own_pairs.at[:, 0:5], blocks.at[x_pos, pl.ds(10 * core, 10), pl.ds(5 * z_hi, 5)], local_sem.at[1]
    )

    def to_z(source, block, send_at, recv_at, r):
        return pltpu.make_async_remote_copy(
            src_ref=source, dst_ref=block, send_sem=send_at, recv_sem=recv_at,
            device_id=((z_hi + r) % 4 * 8 + eight, me), device_id_type=MESH,
        )

    def to_x(source, block, send_at, recv_at, r):
        return pltpu.make_async_remote_copy(
            src_ref=source, dst_ref=block, send_sem=send_at, recv_sem=recv_at,
            device_id=(z_hi * 8 + (x_pos + r) % 4 * 2 + core, me), device_id_type=MESH,
        )

    def z_copy(r):
        return to_z(own_first, first_part(x_pos, 0), dp_send.at[4, r], dp_recv.at[4, r], r)

    def x_copy(k, r):
        block = first_part(x_pos, k)
        return to_x(own_first if k == 0 else block, block, x_send.at[k, r], x_recv.at[k, r], r)

    def x_first(r):
        return to_x(own_second, second_part(x_pos, 0), dp_send.at[6, r], dp_recv.at[6, r], r)

    def z_second(j, r):
        block = second_part((x_pos - j) % 4, 0)
        return to_z(own_second if j == 0 else block, block, z_send.at[j, r], z_recv.at[j, r], r)

    def core_copy(k):
        block = blocks.at[:, pl.ds(10 * core, 10), pl.ds((z_hi - k) % 4 * 5, 5)]
        return pltpu.make_async_remote_copy(
            src_ref=block, dst_ref=block,
            send_sem=dp_send.at[7, k], recv_sem=dp_recv.at[7, k],
            device_id=(z_hi * 8 + x_pos * 2 + 1 - core, me), device_id_type=MESH,
        )

    keep.start()
    for r in (2, 1, 3):
        x_first(r).start()
    for r in (2, 1, 3):
        z_copy(r).start()
    for r in (2, 1, 3):
        z_second(0, r).start()
        x_copy(0, r).start()

    bias_total = jnp.zeros((C, 128), F32)
    for s in range(SLABS):
        bias_total = bias_total + recv[2, s]
    space_wait(3)
    owners_to_slab(3)
    point_total = jnp.zeros((C, 128), F32)
    for s in range(SLABS):
        point_total = point_total + recv[3, s]
    sums8[eight] = jnp.where(lane >= 108, point_total, jnp.where(lane == 0, turn(bias_total, 20), 0.0))

    def eight_copy(r):
        to = (eight + r) % 8
        return pltpu.make_async_remote_copy(
            src_ref=sums8.at[eight], dst_ref=sums8.at[eight],
            send_sem=dp_send.at[3, r], recv_sem=dp_recv.at[3, r],
            device_id=(z_hi * 8 + to, me), device_id_type=MESH,
        )

    for r in range(1, 8):
        eight_copy(r).start()

    for j in (1, 3, 2):
        x_first(j).wait_recv()
        for r in (2, 1, 3):
            z_second(j, r).start()
    full = lined[...]
    for n in range(9):
        columns = slice(256 * n, 256 * n + 256)
        result = times(full, inv[n, 0], inv[n, 1]) + values[:, columns]
        for p in range(PLANES):
            grad_vmem[0, 0, p, :, columns] = result[ROWS * p : ROWS * p + C].astype(BF16)

    for r in range(1, 8):
        eight_copy(r).wait()
    total = sums8[0]
    for b in range(1, 8):
        total = total + sums8[b]
    sums4[z_hi] = total

    def four_copy(r):
        to = (z_hi + r) % 4
        return pltpu.make_async_remote_copy(
            src_ref=sums4.at[z_hi], dst_ref=sums4.at[z_hi],
            send_sem=dp_send.at[5, r], recv_sem=dp_recv.at[5, r],
            device_id=(to * 8 + eight, me), device_id_type=MESH,
        )

    for r in range(1, 4):
        four_copy(r).start()
    keep.wait()
    for k in (1, 3, 2):
        z_copy(k).wait_recv()
        for r in (2, 1, 3):
            x_copy(k, r).start()
    order = (0, 1, 3, 2)
    for k in order:
        for r in range(1, 4):
            x_copy(k, r).wait_recv()
        if k != 0:
            for j in range(4):
                z_second(j, k).wait_recv()
        core_copy(k).start()
    for r in range(1, 4):
        four_copy(r).wait()
    total = turn(sums4[0] + sums4[1] + sums4[2] + sums4[3], 20)
    sums_ref[0:C, :] = total
    square = lax.broadcasted_iota(jnp.int32, (C, 128), 0) == lane
    sums_ref[C : C + 1, :] = jnp.sum(jnp.where(square, total[:, C : C + 1], 0.0), axis=0, keepdims=True)
    for r in range(1, 4):
        z_copy(r).wait_send()
        x_first(r).wait_send()
        for j in range(4):
            z_second(j, r).wait_send()
        for k in range(4):
            x_copy(k, r).wait_send()
    for k in order:
        core_copy(k).wait()


def results(out_from, grad_from, spec_from, sums, out_to, grad_to, spec_to, point_to, bias_to, sem):
    copies = []
    strips = spec_from.reshape(4, C, C, 2, 128)
    for j in range(4):
        for k in range(4):
            rows = pl.ds(5 * k, 5)
            copies.append(
                pltpu.make_async_copy(
                    strips.at[j, rows], spec_to.at[rows, :, :, 128 * j : 128 * j + 128], sem.at[4 * j + k]
                )
            )
    for p in range(PLANES):
        copies.append(pltpu.make_async_copy(out_from.at[0, 0, p], out_to.at[0, 0, p], sem.at[16 + p]))
        copies.append(pltpu.make_async_copy(grad_from.at[0, 0, p], grad_to.at[0, 0, p], sem.at[19 + p]))
    for copy in copies:
        copy.start()
    point_to[...] = sums[0:C, 0:C]
    bias_to[...] = sums[C : C + 1, 0:C]
    for copy in copies:
        copy.wait()


def on_device(wake_field, spec_weight, point_weight, bias_term, cotangent):
    forward, inverse, x_two, x_inverse, kz_weight = tables()
    weight = spec_weight.transpose(1, 2, 0, 3)
    anywhere = pl.BlockSpec(memory_space=pl.ANY)
    inside = pl.BlockSpec(memory_space=pltpu.VMEM)
    field = wake_field.shape
    output_field, grad_field, grad_spec, sums = pl.pallas_call(
        kernel,
        out_shape=(
            pltpu.VMEM(field, BF16),
            pltpu.VMEM(field, BF16),
            pltpu.VMEM((4, C, PAIRS, 128), F32),
            pltpu.VMEM((ROWS, 128), F32),
        ),
        in_specs=[anywhere] * 3 + [inside] * 3 + [anywhere] * 4,
        out_specs=(inside, inside, inside, inside),
        scratch_shapes=[
            pltpu.VMEM(field, BF16),
            pltpu.VMEM(field, BF16),
            pltpu.VMEM(weight.shape, BF16),
            pltpu.VMEM(forward.shape, BF16),
            pltpu.VMEM(inverse.shape, BF16),
            pltpu.VMEM(x_two.shape, BF16),
            pltpu.VMEM(x_inverse.shape, BF16),
            pltpu.VMEM((TALL, CELLS), F32),
            pltpu.VMEM((TALL, CELLS), F32),
            pltpu.VMEM((C, PAIRS, 512), F32),
            pltpu.VMEM((TALL, WIDE), F32),
            pltpu.VMEM((TALL, WIDE), F32),
            pltpu.VMEM((TALL, CELLS), F32),
            pltpu.VMEM((TALL, WIDE), F32),
            pltpu.VMEM((TALL, 512), F32),
            pltpu.VMEM((4, PAIRS, 128), F32),
            pltpu.VMEM((4, PAIRS, 128), F32),
            pltpu.VMEM((4, PAIRS, 128), F32),
            pltpu.VMEM((ROWS, 128), F32),
            pltpu.VMEM((4, SLABS, C, 128), F32),
            pltpu.VMEM((4, SLABS, C, 128), F32),
            pltpu.VMEM((16, PAIRS, 128), F32),
            pltpu.VMEM((16, 16, 128), F32),
            pltpu.VMEM((C, 16, 128), F32),
            pltpu.VMEM((10, 16, 128), F32),
            pltpu.VMEM((10, 16, 128), F32),
            pltpu.VMEM((8, C, 128), F32),
            pltpu.VMEM((4, C, 128), F32),
            pltpu.SemaphoreType.DMA((9,)),
            pltpu.SemaphoreType.DMA((2,)),
            pltpu.SemaphoreType.DMA((4, 16)),
            pltpu.SemaphoreType.DMA((4, 16)),
            pltpu.SemaphoreType.DMA((8, 16)),
            pltpu.SemaphoreType.DMA((8, 16)),
            pltpu.SemaphoreType.DMA((4, 4)),
            pltpu.SemaphoreType.DMA((4, 4)),
            pltpu.SemaphoreType.DMA((4, 4)),
            pltpu.SemaphoreType.DMA((4, 4)),
        ],
        compiler_params=pltpu.CompilerParams(
            collective_id=0, has_side_effects=True, vmem_limit_bytes=52 * 1024 * 1024
        ),
    )(wake_field, cotangent, weight, point_weight, bias_term[None], kz_weight, forward, inverse, x_two, x_inverse)
    output_field, grad_field, grad_spec, grad_point, grad_bias = pl.pallas_call(
        results,
        out_shape=(
            jax.ShapeDtypeStruct(field, BF16),
            jax.ShapeDtypeStruct(field, BF16),
            jax.ShapeDtypeStruct((C, C, 2, 512), F32),
            jax.ShapeDtypeStruct((C, C), F32),
            jax.ShapeDtypeStruct((1, C), F32),
        ),
        in_specs=[inside] * 4,
        out_specs=(anywhere, anywhere, anywhere, inside, inside),
        scratch_shapes=[pltpu.SemaphoreType.DMA((22,))],
    )(*[pltpu.with_memory_space_constraint(array, pltpu.VMEM) for array in (output_field, grad_field, grad_spec, sums)])
    return (
        output_field,
        grad_field,
        grad_spec.transpose(2, 0, 1, 3)[..., :MODES],
        grad_point,
        grad_bias.reshape(C),
    )


def solution(mesh):
    placed = (
        P("dp", None, "space", None, None),
        P(None, None, None, "space"),
        P(),
        P(),
        P("dp", None, "space", None, None),
    )
    return jax.shard_map(
        on_device,
        mesh=mesh,
        in_specs=placed,
        out_specs=(
            P("dp", None, "space", None, None),
            P("dp", None, "space", None, None),
            P(None, None, None, "space"),
            P(),
            P(),
        ),
        check_vma=False,
    )
```

```python
import functools
import math

import jax
import jax.numpy as jnp
import numpy as np
from jax import lax
from jax.experimental import pallas as pl
from jax.experimental.pallas import tpu as pltpu
from jax.sharding import PartitionSpec as P

MESH = pl.DeviceIdType.MESH
F32 = jnp.float32
BF16 = jnp.bfloat16

C = 20
N = 48
MZ = 12
CELLS = N * N
KX = 24
SLABS = 16
PLANES = 3
OWN = 18
MODES = OWN * KX
ROWS = 24
TALL = PLANES * ROWS
TILES = 6
WIDE = TILES * 128
PAIRS = 2 * C
SPLIT = 8


def wave(i):
    return np.where(i < 12, i, i - 24)


def halves(table):
    high = table.astype(np.float32).astype(BF16)
    low = (table - high.astype(np.float64)).astype(np.float32).astype(BF16)
    return np.stack([high, low])


def yz_table():
    lane = np.arange(128)
    g, k, part, q6 = lane // 36, lane % 36 // 12, lane % 12 // 6, lane % 6
    owner = 3 * np.arange(TILES)[:, None] + k[None, :]
    used = (lane < 108)[None, :] & (owner < SLABS)
    q = OWN * owner + 6 * g[None, :] + q6[None, :]
    ky, kz = wave(q // MZ), q % MZ
    cell = np.arange(CELLS)
    y, z = cell // N, cell % N
    phase = (y[:, None, None] * ky[None] + z[:, None, None] * kz[None]) % N
    angle = 2.0 * np.pi * phase / N
    table = np.where(part == 0, np.cos(angle), -np.sin(angle)) / N
    return np.where(used[None], table, 0.0).reshape(CELLS, WIDE)


def x_table():
    lane = np.arange(128)
    k, p, part, q6 = lane // 36, lane % 36 // 12, lane % 12 // 6, lane % 6
    slab = 3 * np.arange(TILES)[:, None] + k[None, :]
    used = ((lane < 108)[None, :] & (slab < SLABS)).reshape(-1)
    x = (PLANES * slab + p[None, :]).reshape(-1)
    part, q6 = np.tile(part, TILES), np.tile(q6, TILES)
    column = np.arange(512)
    part_out, rest = column // 256, column % 256
    q6_out, i = rest // KX, rest % KX
    angle = 2.0 * np.pi * (x[:, None] * wave(i)[None, :] % N) / N
    cosine, sine = np.cos(angle), np.sin(angle)
    same = part[:, None] == part_out[None, :]
    table = np.where(same, cosine, np.where(part[:, None] == 1, sine, -sine)) / math.sqrt(N)
    keep = used[:, None] & (rest < 6 * KX)[None, :] & (q6[:, None] == q6_out[None, :])
    return np.where(keep, table, 0.0)


@functools.cache
def tables():
    yz, x = yz_table(), x_table()
    yz_two, x_two = halves(yz), halves(x)
    forward = np.ascontiguousarray(yz_two.reshape(2, CELLS, 3, 256).transpose(2, 0, 1, 3))
    inverse = np.ascontiguousarray(yz_two.transpose(0, 2, 1).reshape(2, WIDE, 9, 256).transpose(2, 0, 1, 3))
    x_inverse = np.ascontiguousarray(x_two.transpose(0, 2, 1))
    own = np.arange(512) // KX
    weight = np.stack([np.where((6 * parity + own) % MZ == 0, 1.0, 2.0) for parity in range(2)])
    weight = np.broadcast_to(weight[:, None, :], (2, 8, 512)).astype(np.float32)
    return forward, inverse, x_two, x_inverse, np.ascontiguousarray(weight)


def times(value, high, low):
    rows = value.shape[0]
    top = value.astype(BF16)
    wide = top.astype(F32)
    both = jnp.concatenate([wide, value - wide], axis=0).astype(BF16)
    first = jnp.dot(both, high, preferred_element_type=F32)
    return first[:rows] + first[rows:] + jnp.dot(top, low, preferred_element_type=F32)


def kernel(
    wake_hbm, cot_hbm, weight_hbm, point_weight, bias_term, kz_weight, fwd_hbm, inv_hbm, x_hbm, xt_hbm,
    out_vmem, grad_vmem, gathered, sums_ref,
    wake, cot, weight, fwd, inv, xf, xt,
    values, slopes, maps, slab, grads, lined, pieces, modes, mixed, grad_modes, matrix,
    send, recv, all_modes, all_grads, partial, landed, own_sum, sums8, sums4,
    load_sem, local_sem, send_sem, recv_sem, dp_send, dp_recv, x_send, x_recv, z_send, z_recv,
):
    dp = lax.axis_index("dp")
    me = lax.axis_index("space")
    z_hi, eight = dp // 8, dp % 8
    x_pos, core = eight // 2, eight % 2
    lane = lax.broadcasted_iota(jnp.int32, (C, 128), 1)
    third = lane // 36
    slot = jnp.where(lane < 108, lane % 36 // 12, 3)
    home = z_hi * 4 + x_pos
    far_first = (8, 7, 9, 6, 10, 5, 11, 4, 12, 3, 13, 2, 14, 1, 15)

    third_at = [(me + i) % 3 for i in range(3)]

    loads = [
        pltpu.make_async_copy(wake_hbm, wake, load_sem.at[0]),
        pltpu.make_async_copy(fwd_hbm.at[third_at[0]], fwd.at[third_at[0]], load_sem.at[1]),
        pltpu.make_async_copy(fwd_hbm.at[third_at[1]], fwd.at[third_at[1]], load_sem.at[2]),
        pltpu.make_async_copy(fwd_hbm.at[third_at[2]], fwd.at[third_at[2]], load_sem.at[3]),
        pltpu.make_async_copy(weight_hbm, weight, load_sem.at[4]),
        pltpu.make_async_copy(cot_hbm, cot, load_sem.at[5]),
        pltpu.make_async_copy(x_hbm, xf, load_sem.at[6]),
        pltpu.make_async_copy(xt_hbm, xt, load_sem.at[7]),
        pltpu.make_async_copy(inv_hbm, inv, load_sem.at[8]),
    ]
    for load in loads[:4]:
        load.start()

    barrier = pltpu.get_barrier_semaphore()
    for r in range(1, 16):
        pl.semaphore_signal(barrier, inc=1, device_id=(dp, (me + r) % 16), device_id_type=MESH)
    for r in range(1, 8):
        peer = z_hi * 8 + (eight + r) % 8
        pl.semaphore_signal(barrier, inc=1, device_id=(peer, me), device_id_type=MESH)
    for i in range(1, 4):
        for j in range(4):
            peer = (z_hi + i) % 4 * 8 + (x_pos + j) % 4 * 2 + core
            pl.semaphore_signal(barrier, inc=1, device_id=(peer, me), device_id_type=MESH)

    values[...] = jnp.zeros((TALL, CELLS), F32)
    lined[...] = jnp.zeros((TALL, WIDE), F32)
    loads[0].wait()
    for p in range(PLANES):
        values[ROWS * p : ROWS * p + C, :] = wake[0, 0, p].astype(F32)

    def space_copy(phase, r):
        to = (me + r) % 16
        return pltpu.make_async_remote_copy(
            src_ref=send.at[phase, to], dst_ref=recv.at[phase, me],
            send_sem=send_sem.at[phase, r], recv_sem=recv_sem.at[phase, r],
            device_id=(dp, to), device_id_type=MESH,
        )

    def space_start(phase):
        for r in range(1, 16):
            space_copy(phase, r).start()
        recv[phase, me] = send[phase, me]

    def space_wait(phase):
        for r in range(1, 16):
            space_copy(phase, r).wait()

    def turn(value, shift):
        shift %= 128
        return value if shift == 0 else pltpu.roll(value, shift, 1)

    def other(value):
        rows = value.shape[0]
        even = lax.broadcasted_iota(jnp.int32, (rows, 128), 0) % 2 == 0
        return jnp.where(even, pltpu.roll(value, rows - 1, 0), -pltpu.roll(value, 1, 0))

    def choose(where, parts):
        total = jnp.zeros((C, 128), F32)
        for index, part in parts:
            total = jnp.where(where == index, part, total)
        return total

    def slab_to_owners(phase, n, spectra, ride):
        for t in range(2):
            held = [spectra[ROWS * p : ROWS * p + C, 128 * t : 128 * t + 128] for p in range(PLANES)]
            for k in range(3):
                message = choose(slot, [(p, turn(held[p], 12 * (p - k))) for p in range(PLANES)])
                send[phase, 6 * n + 3 * t + k] = message if ride is None else message + ride
        for j in range(6):
            to = 6 * n + j

            @pl.when((to < SLABS) & (to != me))
            def _():
                space_copy(phase, (to + SLABS - me) % SLABS).start()

    def owners_to_slab(phase):
        for t in range(TILES):
            ks = [k for k in range(3) if 3 * t + k < SLABS]
            held = [recv[phase, 3 * t + k] for k in ks]
            for p in range(PLANES):
                lined[ROWS * p : ROWS * p + C, 128 * t : 128 * t + 128] = choose(
                    slot, [(k, turn(held[k], 12 * (k - p))) for k in ks]
                )

    def line_up_planes(phase):
        for u in range(TILES):
            ks = [k for k in range(3) if 3 * u + k < SLABS]
            held = [recv[phase, 3 * u + k] for k in ks]
            for g in range(3):
                lined[ROWS * g : ROWS * g + C, 128 * u : 128 * u + 128] = choose(
                    third, [(k, turn(held[k], 36 * (k - g))) for k in ks]
                )

    def planes_to_slabs(phase, ride):
        for u in range(TILES):
            held = [slab[ROWS * g : ROWS * g + C, 128 * u : 128 * u + 128] for g in range(3)]
            for k in range(3):
                if 3 * u + k < SLABS:
                    message = choose(third, [(g, turn(held[g], 36 * (g - k))) for g in range(3)])
                    send[phase, 3 * u + k] = message if ride is None else message + ride

    def along_x(target, scale):
        result = times(lined[...], xf[0], xf[1])
        for part in range(2):
            block = [result[ROWS * g : ROWS * g + ROWS, 256 * part : 256 * part + 256] for g in range(3)]
            second, last = pltpu.roll(block[1], 16, 1), pltpu.roll(block[2], 32, 1)
            strips = [
                block[0][:, :128],
                block[0][:, 128:] + second[:, :128],
                second[:, 128:] + last[:, :128],
                last[:, 128:],
            ]
            for j in range(4):
                strip = strips[j][:C]
                if scale is not None:
                    strip = strip * scale[:, 128 * j : 128 * j + 128]
                target[j, pl.ds(part, C, stride=2), :] = strip

    def back_along_x():
        for part in range(2):
            strips = [mixed[j, pl.ds(part, C, stride=2), :] for j in range(4)]
            full = jnp.concatenate(strips, axis=1)
            pieces[0:C, 256 * part : 256 * part + 256] = full[:, :256]
            pieces[ROWS : ROWS + C, 256 * part : 256 * part + 256] = pltpu.roll(full, 512 - 144, 1)[:, :256]
            pieces[2 * ROWS : 2 * ROWS + C, 256 * part : 256 * part + 256] = pltpu.roll(full, 512 - 288, 1)[:, :256]
        slab[...] = times(pieces[...], xt[0], xt[1])

    def strip_at(index):
        return pl.ds(pl.multiple_of(index * 128, 128), 128)

    grad_pairs = grad_modes.reshape(4, C, 2, 128)
    landing = all_grads.reshape(16, 8, 2, 128)

    def gather_to(r):
        to = (home + r) % 16
        return to // 4, to % 4, (to * 2 + core, me)

    def modes_copy(r):
        _, x_to, device = gather_to(r)
        return pltpu.make_async_remote_copy(
            src_ref=modes.at[x_to], dst_ref=all_modes.at[home],
            send_sem=dp_send.at[0, r], recv_sem=dp_recv.at[0, r],
            device_id=device, device_id_type=MESH,
        )

    def grads_copy(r):
        z_to, x_to, device = gather_to(r)
        return pltpu.make_async_remote_copy(
            src_ref=grad_pairs.at[x_to, pl.ds(5 * z_to, 5)], dst_ref=landing.at[home, 0:5],
            send_sem=dp_send.at[1, r], recv_sem=dp_recv.at[1, r],
            device_id=device, device_id_type=MESH,
        )

    grads_own = pltpu.make_async_copy(
        grad_pairs.at[x_pos, pl.ds(5 * z_hi, 5)], landing.at[home, 0:5], local_sem.at[0]
    )

    tall = values[...].astype(BF16)
    for i, n in enumerate(third_at):
        loads[1 + i].wait()
        spectra = jnp.dot(tall, fwd[n, 0], preferred_element_type=F32) + jnp.dot(
            tall, fwd[n, 1], preferred_element_type=F32
        )
        if i == 0:
            pl.semaphore_wait(barrier, 34)
        slab_to_owners(0, n, spectra, None)
    for load in loads[4:]:
        load.start()
    recv[0, me] = send[0, me]

    pieces[...] = jnp.zeros((TALL, 512), F32)
    maps[:, :, 384:] = jnp.zeros((C, PAIRS, 128), F32)
    matrix[...] = jnp.zeros((ROWS, 128), F32)
    slopes[...] = jnp.zeros((TALL, CELLS), F32)
    matrix[0:C, 0:C] = point_weight[...].astype(F32)
    loads[4].wait()

    def cast_step(c, carry):
        maps[c, :, :MODES] = weight[c].astype(F32).reshape(PAIRS, MODES)
        return carry

    lax.fori_loop(0, C, cast_step, 0)
    loads[5].wait()
    for p in range(PLANES):
        slopes[ROWS * p : ROWS * p + C, :] = cot[0, 0, p].astype(F32)
    for load in loads[6:]:
        load.wait()

    space_wait(0)
    line_up_planes(0)
    along_x(modes, None)
    row = kz_weight[me % 2, 0:1, :]

    def mix_step(j, carry):
        strip = strip_at(j)
        first, second = jnp.zeros((PAIRS, 128), F32), jnp.zeros((PAIRS, 128), F32)
        for c in range(C):
            weights = maps[c, :, strip]
            first = first + weights * modes[j, 2 * c : 2 * c + 1, :]
            second = second + weights * modes[j, 2 * c + 1 : 2 * c + 2, :]
        mixed[j] = (first - other(second)) * kz_weight[me % 2, 0:1, strip]
        return carry

    lax.fori_loop(0, 4, mix_step, 0)
    back_along_x()
    planes_to_slabs(1, None)
    space_start(1)

    to_in = jnp.concatenate([turn(matrix[...], ROWS * p) for p in range(PLANES)], axis=0)[:, :TALL].astype(BF16)
    here = lax.broadcasted_iota(jnp.int32, (ROWS, C), 0) == lax.broadcasted_iota(jnp.int32, (ROWS, C), 1)
    bias = jnp.sum(jnp.where(here, bias_term[...], 0.0), axis=1, keepdims=True)
    bias = jnp.concatenate([bias] * PLANES, axis=0)
    for n in range(9):
        columns = slice(256 * n, 256 * n + 256)
        grads[:, columns] = bias + lax.dot_general(
            to_in, values[:, columns].astype(BF16), (((0,), (0,)), ((), ())), preferred_element_type=F32
        )
    space_wait(1)
    for r in far_first:
        modes_copy(r).start()
    all_modes[home] = modes[x_pos]
    owners_to_slab(1)

    full = lined[...]
    rate = math.sqrt(2.0 / math.pi)
    bias_sum = jnp.zeros((TALL, 1), F32)
    for n in range(9):
        columns = slice(256 * n, 256 * n + 256)
        pre = times(full, inv[n, 0], inv[n, 1]) + grads[:, columns]
        square = pre * pre
        bend = jnp.tanh(rate * (pre + 0.044715 * (square * pre)))
        half = 0.5 * (1.0 + bend)
        slope = half + 0.5 * pre * (1.0 - bend * bend) * (rate * (1.0 + 3 * 0.044715 * square))
        active = half * pre
        for p in range(PLANES):
            out_vmem[0, 0, p, :, columns] = active[ROWS * p : ROWS * p + C].astype(BF16)
        slope = slope * slopes[:, columns]
        grads[:, columns] = slope
        bias_sum = bias_sum + jnp.sum(slope, axis=1, keepdims=True)

    full = grads[...]
    bias_own = bias_sum[:C] + bias_sum[ROWS : ROWS + C] + bias_sum[2 * ROWS : 2 * ROWS + C]
    ride = jnp.where(lane == 108, bias_own, 0.0)
    for n in third_at:
        slab_to_owners(2, n, times(full, fwd[n, 0], fwd[n, 1]), ride)
    recv[2, me] = send[2, me]

    point = jnp.zeros((ROWS, ROWS), F32)
    last = (((1,), (1,)), ((), ()))
    for p in range(PLANES):
        field = values[ROWS * p : ROWS * p + ROWS, :].astype(BF16)
        slope = grads[ROWS * p : ROWS * p + ROWS, :]
        high = slope.astype(BF16)
        low = (slope - high.astype(F32)).astype(BF16)
        point = point + lax.dot_general(field, high, last, preferred_element_type=F32)
        point = point + lax.dot_general(field, low, last, preferred_element_type=F32)
    point = jnp.concatenate([point[:C], jnp.zeros((C, 128 - ROWS), F32)], axis=1)
    point = jnp.where(lane >= 108, turn(point, 108), 0.0)
    for n in range(9):
        columns = slice(256 * n, 256 * n + 256)
        slope = grads[:, columns]
        high = slope.astype(BF16)
        low = (slope - high.astype(F32)).astype(BF16)
        values[:, columns] = jnp.dot(to_in, high, preferred_element_type=F32) + jnp.dot(
            to_in, low, preferred_element_type=F32
        )

    space_wait(2)
    line_up_planes(2)
    along_x(grad_modes, row)
    for r in far_first:
        grads_copy(r).start()
    grads_own.start()

    def grad_step(j, carry):
        strip = strip_at(j)
        slope = grad_modes[j]
        crossed = other(slope)
        for c in range(C):
            weights = maps[c, :, strip]
            mixed[j, 2 * c : 2 * c + 1, :] = jnp.sum(weights * slope, axis=0, keepdims=True)
            mixed[j, 2 * c + 1 : 2 * c + 2, :] = jnp.sum(weights * crossed, axis=0, keepdims=True)
        return carry

    lax.fori_loop(0, 4, grad_step, 0)
    back_along_x()
    planes_to_slabs(3, point)
    space_start(3)

    partial_pairs = partial.reshape(C, 8, 2, 128)
    own_pairs = own_sum.reshape(10, 8, 2, 128)
    blocks = gathered.reshape(4, C, C, 2, 128)
    for r in far_first:
        modes_copy(r).wait()
        grads_copy(r).wait()
    grads_own.wait()

    def part_step(i, carry):
        c = (i + 10 * (1 - core)) % C
        first, second = jnp.zeros((16, 128), F32), jnp.zeros((16, 128), F32)
        for b in range(16):
            slope = all_grads[b]
            first = first + all_modes[b, pl.ds(2 * c, 1), :] * slope
            second = second + all_modes[b, pl.ds(2 * c + 1, 1), :] * slope
        partial[c] = first + other(second)
        return carry

    core_sum = pltpu.make_async_remote_copy(
        src_ref=partial_pairs.at[pl.ds(10 * (1 - core), 10), 0:5],
        dst_ref=landed.reshape(10, 8, 2, 128).at[:, 0:5],
        send_sem=dp_send.at[2, 0], recv_sem=dp_recv.at[2, 0],
        device_id=(z_hi * 8 + x_pos * 2 + 1 - core, me), device_id_type=MESH,
    )
    lax.fori_loop(0, 10, part_step, 0)
    core_sum.start()
    lax.fori_loop(10, 20, part_step, 0)
    core_sum.wait()
    for j in range(10):
        own_sum[j] = partial[10 * core + j] + landed[j]

    def first_part(strip, k):
        return blocks.at[strip, pl.ds(10 * core, SPLIT), pl.ds((z_hi - k) % 4 * 5, 5)]

    def second_part(strip, k):
        return blocks.at[strip, pl.ds(10 * core + SPLIT, 10 - SPLIT), pl.ds((z_hi - k) % 4 * 5, 5)]

    own_first = own_pairs.at[0:SPLIT, 0:5]
    own_second = own_pairs.at[SPLIT:10, 0:5]
    keep = pltpu.make_async_copy(
        own_pairs.at[:, 0:5], blocks.at[x_pos, pl.ds(10 * core, 10), pl.ds(5 * z_hi, 5)], local_sem.at[1]
    )

    def to_z(source, block, send_at, recv_at, r):
        return pltpu.make_async_remote_copy(
            src_ref=source, dst_ref=block, send_sem=send_at, recv_sem=recv_at,
            device_id=((z_hi + r) % 4 * 8 + eight, me), device_id_type=MESH,
        )

    def to_x(source, block, send_at, recv_at, r):
        return pltpu.make_async_remote_copy(
            src_ref=source, dst_ref=block, send_sem=send_at, recv_sem=recv_at,
            device_id=(z_hi * 8 + (x_pos + r) % 4 * 2 + core, me), device_id_type=MESH,
        )

    def z_copy(r):
        return to_z(own_first, first_part(x_pos, 0), dp_send.at[4, r], dp_recv.at[4, r], r)

    def x_copy(k, r):
        block = first_part(x_pos, k)
        return to_x(own_first if k == 0 else block, block, x_send.at[k, r], x_recv.at[k, r], r)

    def x_first(r):
        return to_x(own_second, second_part(x_pos, 0), dp_send.at[6, r], dp_recv.at[6, r], r)

    def z_second(j, r):
        block = second_part((x_pos - j) % 4, 0)
        return to_z(own_second if j == 0 else block, block, z_send.at[j, r], z_recv.at[j, r], r)

    def core_copy(k):
        block = blocks.at[:, pl.ds(10 * core, 10), pl.ds((z_hi - k) % 4 * 5, 5)]
        return pltpu.make_async_remote_copy(
            src_ref=block, dst_ref=block,
            send_sem=dp_send.at[7, k], recv_sem=dp_recv.at[7, k],
            device_id=(z_hi * 8 + x_pos * 2 + 1 - core, me), device_id_type=MESH,
        )

    keep.start()
    for r in (2, 1, 3):
        x_first(r).start()
    for r in (2, 1, 3):
        z_copy(r).start()
    for r in (2, 1, 3):
        z_second(0, r).start()
        x_copy(0, r).start()

    bias_total = jnp.zeros((C, 128), F32)
    for s in range(SLABS):
        bias_total = bias_total + recv[2, s]
    space_wait(3)
    owners_to_slab(3)
    point_total = jnp.zeros((C, 128), F32)
    for s in range(SLABS):
        point_total = point_total + recv[3, s]
    sums8[eight] = jnp.where(lane >= 108, point_total, jnp.where(lane == 0, turn(bias_total, 20), 0.0))

    def eight_copy(r):
        to = (eight + r) % 8
        return pltpu.make_async_remote_copy(
            src_ref=sums8.at[eight], dst_ref=sums8.at[eight],
            send_sem=dp_send.at[3, r], recv_sem=dp_recv.at[3, r],
            device_id=(z_hi * 8 + to, me), device_id_type=MESH,
        )

    for r in range(1, 8):
        eight_copy(r).start()

    for j in (1, 3, 2):
        x_first(j).wait_recv()
        for r in (2, 1, 3):
            z_second(j, r).start()
    full = lined[...]
    for n in range(9):
        columns = slice(256 * n, 256 * n + 256)
        result = times(full, inv[n, 0], inv[n, 1]) + values[:, columns]
        for p in range(PLANES):
            grad_vmem[0, 0, p, :, columns] = result[ROWS * p : ROWS * p + C].astype(BF16)

    for r in range(1, 8):
        eight_copy(r).wait()
    total = sums8[0]
    for b in range(1, 8):
        total = total + sums8[b]
    sums4[z_hi] = total

    def four_copy(r):
        to = (z_hi + r) % 4
        return pltpu.make_async_remote_copy(
            src_ref=sums4.at[z_hi], dst_ref=sums4.at[z_hi],
            send_sem=dp_send.at[5, r], recv_sem=dp_recv.at[5, r],
            device_id=(to * 8 + eight, me), device_id_type=MESH,
        )

    for r in range(1, 4):
        four_copy(r).start()
    keep.wait()
    for k in (1, 3, 2):
        z_copy(k).wait_recv()
        for r in (2, 1, 3):
            x_copy(k, r).start()
    order = (0, 1, 3, 2)
    for k in order:
        for r in range(1, 4):
            x_copy(k, r).wait_recv()
        if k != 0:
            for j in range(4):
                z_second(j, k).wait_recv()
        core_copy(k).start()
    for r in range(1, 4):
        four_copy(r).wait()
    total = turn(sums4[0] + sums4[1] + sums4[2] + sums4[3], 20)
    sums_ref[0:C, :] = total
    square = lax.broadcasted_iota(jnp.int32, (C, 128), 0) == lane
    sums_ref[C : C + 1, :] = jnp.sum(jnp.where(square, total[:, C : C + 1], 0.0), axis=0, keepdims=True)
    for r in range(1, 4):
        z_copy(r).wait_send()
        x_first(r).wait_send()
        for j in range(4):
            z_second(j, r).wait_send()
        for k in range(4):
            x_copy(k, r).wait_send()
    for k in order:
        core_copy(k).wait()


def results(out_from, grad_from, spec_from, sums, out_to, grad_to, spec_to, point_to, bias_to, sem):
    copies = []
    strips = spec_from.reshape(4, C, C, 2, 128)
    for j in range(4):
        for k in range(4):
            rows = pl.ds(5 * k, 5)
            copies.append(
                pltpu.make_async_copy(
                    strips.at[j, rows], spec_to.at[rows, :, :, 128 * j : 128 * j + 128], sem.at[4 * j + k]
                )
            )
    for p in range(PLANES):
        copies.append(pltpu.make_async_copy(out_from.at[0, 0, p], out_to.at[0, 0, p], sem.at[16 + p]))
        copies.append(pltpu.make_async_copy(grad_from.at[0, 0, p], grad_to.at[0, 0, p], sem.at[19 + p]))
    for copy in copies:
        copy.start()
    point_to[...] = sums[0:C, 0:C]
    bias_to[...] = sums[C : C + 1, 0:C]
    for copy in copies:
        copy.wait()


def on_device(wake_field, spec_weight, point_weight, bias_term, cotangent):
    forward, inverse, x_two, x_inverse, kz_weight = tables()
    weight = spec_weight.transpose(1, 2, 0, 3)
    anywhere = pl.BlockSpec(memory_space=pl.ANY)
    inside = pl.BlockSpec(memory_space=pltpu.VMEM)
    field = wake_field.shape
    output_field, grad_field, grad_spec, sums = pl.pallas_call(
        kernel,
        out_shape=(
            pltpu.VMEM(field, BF16),
            pltpu.VMEM(field, BF16),
            pltpu.VMEM((4, C, PAIRS, 128), F32),
            pltpu.VMEM((ROWS, 128), F32),
        ),
        in_specs=[anywhere] * 3 + [inside] * 3 + [anywhere] * 4,
        out_specs=(inside, inside, inside, inside),
        scratch_shapes=[
            pltpu.VMEM(field, BF16),
            pltpu.VMEM(field, BF16),
            pltpu.VMEM(weight.shape, BF16),
            pltpu.VMEM(forward.shape, BF16),
            pltpu.VMEM(inverse.shape, BF16),
            pltpu.VMEM(x_two.shape, BF16),
            pltpu.VMEM(x_inverse.shape, BF16),
            pltpu.VMEM((TALL, CELLS), F32),
            pltpu.VMEM((TALL, CELLS), F32),
            pltpu.VMEM((C, PAIRS, 512), F32),
            pltpu.VMEM((TALL, WIDE), F32),
            pltpu.VMEM((TALL, CELLS), F32),
            pltpu.VMEM((TALL, WIDE), F32),
            pltpu.VMEM((TALL, 512), F32),
            pltpu.VMEM((4, PAIRS, 128), F32),
            pltpu.VMEM((4, PAIRS, 128), F32),
            pltpu.VMEM((4, PAIRS, 128), F32),
            pltpu.VMEM((ROWS, 128), F32),
            pltpu.VMEM((4, 3 * TILES, C, 128), F32),
            pltpu.VMEM((4, SLABS, C, 128), F32),
            pltpu.VMEM((16, PAIRS, 128), F32),
            pltpu.VMEM((16, 16, 128), F32),
            pltpu.VMEM((C, 16, 128), F32),
            pltpu.VMEM((10, 16, 128), F32),
            pltpu.VMEM((10, 16, 128), F32),
            pltpu.VMEM((8, C, 128), F32),
            pltpu.VMEM((4, C, 128), F32),
            pltpu.SemaphoreType.DMA((9,)),
            pltpu.SemaphoreType.DMA((2,)),
            pltpu.SemaphoreType.DMA((4, 16)),
            pltpu.SemaphoreType.DMA((4, 16)),
            pltpu.SemaphoreType.DMA((8, 16)),
            pltpu.SemaphoreType.DMA((8, 16)),
            pltpu.SemaphoreType.DMA((4, 4)),
            pltpu.SemaphoreType.DMA((4, 4)),
            pltpu.SemaphoreType.DMA((4, 4)),
            pltpu.SemaphoreType.DMA((4, 4)),
        ],
        compiler_params=pltpu.CompilerParams(
            collective_id=0, has_side_effects=True, vmem_limit_bytes=52 * 1024 * 1024
        ),
    )(wake_field, cotangent, weight, point_weight, bias_term[None], kz_weight, forward, inverse, x_two, x_inverse)
    output_field, grad_field, grad_spec, grad_point, grad_bias = pl.pallas_call(
        results,
        out_shape=(
            jax.ShapeDtypeStruct(field, BF16),
            jax.ShapeDtypeStruct(field, BF16),
            jax.ShapeDtypeStruct((C, C, 2, 512), F32),
            jax.ShapeDtypeStruct((C, C), F32),
            jax.ShapeDtypeStruct((1, C), F32),
        ),
        in_specs=[inside] * 4,
        out_specs=(anywhere, anywhere, anywhere, inside, inside),
        scratch_shapes=[pltpu.SemaphoreType.DMA((22,))],
    )(*[pltpu.with_memory_space_constraint(array, pltpu.VMEM) for array in (output_field, grad_field, grad_spec, sums)])
    return (
        output_field,
        grad_field,
        grad_spec.transpose(2, 0, 1, 3)[..., :MODES],
        grad_point,
        grad_bias.reshape(C),
    )


def solution(mesh):
    placed = (
        P("dp", None, "space", None, None),
        P(None, None, None, "space"),
        P(),
        P(),
        P("dp", None, "space", None, None),
    )
    return jax.shard_map(
        on_device,
        mesh=mesh,
        in_specs=placed,
        out_specs=(
            P("dp", None, "space", None, None),
            P("dp", None, "space", None, None),
            P(None, None, None, "space"),
            P(),
            P(),
        ),
        check_vma=False,
    )
```

```python
import functools
import math

import jax
import jax.numpy as jnp
import numpy as np
from jax import lax
from jax.experimental import pallas as pl
from jax.experimental.pallas import tpu as pltpu
from jax.sharding import PartitionSpec as P

MESH = pl.DeviceIdType.MESH
F32 = jnp.float32
BF16 = jnp.bfloat16

C = 20
N = 48
MZ = 12
CELLS = N * N
KX = 24
SLABS = 16
PLANES = 3
OWN = 18
MODES = OWN * KX
ROWS = 24
TALL = PLANES * ROWS
TILES = 6
WIDE = TILES * 128
PAIRS = 2 * C
SPLIT = 8


def wave(i):
    return np.where(i < 12, i, i - 24)


def halves(table):
    high = table.astype(np.float32).astype(BF16)
    low = (table - high.astype(np.float64)).astype(np.float32).astype(BF16)
    return np.stack([high, low])


def yz_table():
    lane = np.arange(128)
    g, k, part, q6 = lane // 36, lane % 36 // 12, lane % 12 // 6, lane % 6
    owner = 3 * np.arange(TILES)[:, None] + k[None, :]
    used = (lane < 108)[None, :] & (owner < SLABS)
    q = OWN * owner + 6 * g[None, :] + q6[None, :]
    ky, kz = wave(q // MZ), q % MZ
    cell = np.arange(CELLS)
    y, z = cell // N, cell % N
    phase = (y[:, None, None] * ky[None] + z[:, None, None] * kz[None]) % N
    angle = 2.0 * np.pi * phase / N
    table = np.where(part == 0, np.cos(angle), -np.sin(angle)) / N
    return np.where(used[None], table, 0.0).reshape(CELLS, WIDE)


def x_table():
    lane = np.arange(128)
    k, p, part, q6 = lane // 36, lane % 36 // 12, lane % 12 // 6, lane % 6
    slab = 3 * np.arange(TILES)[:, None] + k[None, :]
    used = ((lane < 108)[None, :] & (slab < SLABS)).reshape(-1)
    x = (PLANES * slab + p[None, :]).reshape(-1)
    part, q6 = np.tile(part, TILES), np.tile(q6, TILES)
    column = np.arange(512)
    part_out, rest = column // 256, column % 256
    q6_out, i = rest // KX, rest % KX
    angle = 2.0 * np.pi * (x[:, None] * wave(i)[None, :] % N) / N
    cosine, sine = np.cos(angle), np.sin(angle)
    same = part[:, None] == part_out[None, :]
    table = np.where(same, cosine, np.where(part[:, None] == 1, sine, -sine)) / math.sqrt(N)
    keep = used[:, None] & (rest < 6 * KX)[None, :] & (q6[:, None] == q6_out[None, :])
    return np.where(keep, table, 0.0)


@functools.cache
def tables():
    yz, x = yz_table(), x_table()
    yz_two, x_two = halves(yz), halves(x)
    forward = np.ascontiguousarray(yz_two.reshape(2, CELLS, 3, 256).transpose(2, 0, 1, 3))
    inverse = np.ascontiguousarray(yz_two.transpose(0, 2, 1).reshape(2, WIDE, 9, 256).transpose(2, 0, 1, 3))
    x_inverse = np.ascontiguousarray(x_two.transpose(0, 2, 1))
    own = np.arange(512) // KX
    weight = np.stack([np.where((6 * parity + own) % MZ == 0, 1.0, 2.0) for parity in range(2)])
    weight = np.broadcast_to(weight[:, None, :], (2, 8, 512)).astype(np.float32)
    return forward, inverse, x_two, x_inverse, np.ascontiguousarray(weight)


def times(value, high, low):
    rows = value.shape[0]
    top = value.astype(BF16)
    wide = top.astype(F32)
    both = jnp.concatenate([wide, value - wide], axis=0).astype(BF16)
    first = jnp.dot(both, high, preferred_element_type=F32)
    return first[:rows] + first[rows:] + jnp.dot(top, low, preferred_element_type=F32)


def kernel(
    wake_hbm, cot_hbm, weight_hbm, point_weight, bias_term, kz_weight, fwd_hbm, inv_hbm, x_hbm, xt_hbm,
    out_vmem, grad_vmem, gathered, sums_ref,
    wake, cot, weight, fwd, inv, xf, xt,
    values, slopes, maps, spectra, slab, grads, lined, pieces, modes, mixed, grad_modes, matrix,
    send, recv, all_modes, all_grads, partial, landed, own_sum, sums8, sums4,
    load_sem, local_sem, send_sem, recv_sem, dp_send, dp_recv, x_send, x_recv, z_send, z_recv,
):
    dp = lax.axis_index("dp")
    me = lax.axis_index("space")
    z_hi, eight = dp // 8, dp % 8
    x_pos, core = eight // 2, eight % 2
    lane = lax.broadcasted_iota(jnp.int32, (C, 128), 1)
    third = lane // 36
    slot = jnp.where(lane < 108, lane % 36 // 12, 3)
    home = z_hi * 4 + x_pos
    far_first = (8, 7, 9, 6, 10, 5, 11, 4, 12, 3, 13, 2, 14, 1, 15)

    loads = [
        pltpu.make_async_copy(wake_hbm, wake, load_sem.at[0]),
        pltpu.make_async_copy(fwd_hbm.at[0], fwd.at[0], load_sem.at[1]),
        pltpu.make_async_copy(fwd_hbm.at[1], fwd.at[1], load_sem.at[2]),
        pltpu.make_async_copy(fwd_hbm.at[2], fwd.at[2], load_sem.at[3]),
        pltpu.make_async_copy(weight_hbm, weight, load_sem.at[4]),
        pltpu.make_async_copy(cot_hbm, cot, load_sem.at[5]),
        pltpu.make_async_copy(x_hbm, xf, load_sem.at[6]),
        pltpu.make_async_copy(xt_hbm, xt, load_sem.at[7]),
        pltpu.make_async_copy(inv_hbm, inv, load_sem.at[8]),
    ]
    for load in loads[:4]:
        load.start()

    barrier = pltpu.get_barrier_semaphore()
    for r in range(1, 16):
        pl.semaphore_signal(barrier, inc=1, device_id=(dp, (me + r) % 16), device_id_type=MESH)
    for r in range(1, 8):
        peer = z_hi * 8 + (eight + r) % 8
        pl.semaphore_signal(barrier, inc=1, device_id=(peer, me), device_id_type=MESH)
    for i in range(1, 4):
        for j in range(4):
            peer = (z_hi + i) % 4 * 8 + (x_pos + j) % 4 * 2 + core
            pl.semaphore_signal(barrier, inc=1, device_id=(peer, me), device_id_type=MESH)

    values[...] = jnp.zeros((TALL, CELLS), F32)
    lined[...] = jnp.zeros((TALL, WIDE), F32)
    loads[0].wait()
    for p in range(PLANES):
        values[ROWS * p : ROWS * p + C, :] = wake[0, 0, p].astype(F32)

    def space_copy(phase, r):
        to = (me + r) % 16
        return pltpu.make_async_remote_copy(
            src_ref=send.at[phase, to], dst_ref=recv.at[phase, me],
            send_sem=send_sem.at[phase, r], recv_sem=recv_sem.at[phase, r],
            device_id=(dp, to), device_id_type=MESH,
        )

    def space_start(phase):
        for r in range(1, 16):
            space_copy(phase, r).start()
        recv[phase, me] = send[phase, me]

    def space_wait(phase):
        for r in range(1, 16):
            space_copy(phase, r).wait()

    def turn(value, shift):
        shift %= 128
        return value if shift == 0 else pltpu.roll(value, shift, 1)

    def other(value):
        rows = value.shape[0]
        even = lax.broadcasted_iota(jnp.int32, (rows, 128), 0) % 2 == 0
        return jnp.where(even, pltpu.roll(value, rows - 1, 0), -pltpu.roll(value, 1, 0))

    def choose(where, parts):
        total = jnp.zeros((C, 128), F32)
        for index, part in parts:
            total = jnp.where(where == index, part, total)
        return total

    def slab_to_owners(phase, ride):
        for t in range(TILES):
            held = [spectra[ROWS * p : ROWS * p + C, 128 * t : 128 * t + 128] for p in range(PLANES)]
            for k in range(3):
                if 3 * t + k < SLABS:
                    message = choose(slot, [(p, turn(held[p], 12 * (p - k))) for p in range(PLANES)])
                    send[phase, 3 * t + k] = message if ride is None else message + ride

    def owners_to_slab(phase):
        for t in range(TILES):
            ks = [k for k in range(3) if 3 * t + k < SLABS]
            held = [recv[phase, 3 * t + k] for k in ks]
            for p in range(PLANES):
                lined[ROWS * p : ROWS * p + C, 128 * t : 128 * t + 128] = choose(
                    slot, [(k, turn(held[k], 12 * (k - p))) for k in ks]
                )

    def line_up_planes(phase):
        for u in range(TILES):
            ks = [k for k in range(3) if 3 * u + k < SLABS]
            held = [recv[phase, 3 * u + k] for k in ks]
            for g in range(3):
                lined[ROWS * g : ROWS * g + C, 128 * u : 128 * u + 128] = choose(
                    third, [(k, turn(held[k], 36 * (k - g))) for k in ks]
                )

    def planes_to_slabs(phase, ride):
        for u in range(TILES):
            held = [slab[ROWS * g : ROWS * g + C, 128 * u : 128 * u + 128] for g in range(3)]
            for k in range(3):
                if 3 * u + k < SLABS:
                    message = choose(third, [(g, turn(held[g], 36 * (g - k))) for g in range(3)])
                    send[phase, 3 * u + k] = message if ride is None else message + ride

    def along_x(target, scale):
        result = times(lined[...], xf[0], xf[1])
        for part in range(2):
            block = [result[ROWS * g : ROWS * g + ROWS, 256 * part : 256 * part + 256] for g in range(3)]
            second, last = pltpu.roll(block[1], 16, 1), pltpu.roll(block[2], 32, 1)
            strips = [
                block[0][:, :128],
                block[0][:, 128:] + second[:, :128],
                second[:, 128:] + last[:, :128],
                last[:, 128:],
            ]
            for j in range(4):
                strip = strips[j][:C]
                if scale is not None:
                    strip = strip * scale[:, 128 * j : 128 * j + 128]
                target[j, pl.ds(part, C, stride=2), :] = strip

    def back_along_x():
        for part in range(2):
            strips = [mixed[j, pl.ds(part, C, stride=2), :] for j in range(4)]
            full = jnp.concatenate(strips, axis=1)
            pieces[0:C, 256 * part : 256 * part + 256] = full[:, :256]
            pieces[ROWS : ROWS + C, 256 * part : 256 * part + 256] = pltpu.roll(full, 512 - 144, 1)[:, :256]
            pieces[2 * ROWS : 2 * ROWS + C, 256 * part : 256 * part + 256] = pltpu.roll(full, 512 - 288, 1)[:, :256]
        slab[...] = times(pieces[...], xt[0], xt[1])

    def strip_at(index):
        return pl.ds(pl.multiple_of(index * 128, 128), 128)

    grad_pairs = grad_modes.reshape(4, C, 2, 128)
    landing = all_grads.reshape(16, 8, 2, 128)

    def gather_to(r):
        to = (home + r) % 16
        return to // 4, to % 4, (to * 2 + core, me)

    def modes_copy(r):
        _, x_to, device = gather_to(r)
        return pltpu.make_async_remote_copy(
            src_ref=modes.at[x_to], dst_ref=all_modes.at[home],
            send_sem=dp_send.at[0, r], recv_sem=dp_recv.at[0, r],
            device_id=device, device_id_type=MESH,
        )

    def grads_copy(r):
        z_to, x_to, device = gather_to(r)
        return pltpu.make_async_remote_copy(
            src_ref=grad_pairs.at[x_to, pl.ds(5 * z_to, 5)], dst_ref=landing.at[home, 0:5],
            send_sem=dp_send.at[1, r], recv_sem=dp_recv.at[1, r],
            device_id=device, device_id_type=MESH,
        )

    grads_own = pltpu.make_async_copy(
        grad_pairs.at[x_pos, pl.ds(5 * z_hi, 5)], landing.at[home, 0:5], local_sem.at[0]
    )

    tall = values[...].astype(BF16)
    for n in range(3):
        loads[1 + n].wait()
        spectra[:, 256 * n : 256 * n + 256] = jnp.dot(
            tall, fwd[n, 0], preferred_element_type=F32
        ) + jnp.dot(tall, fwd[n, 1], preferred_element_type=F32)
    for load in loads[4:]:
        load.start()
    slab_to_owners(0, None)
    pl.semaphore_wait(barrier, 34)
    space_start(0)

    pieces[...] = jnp.zeros((TALL, 512), F32)
    maps[:, :, 384:] = jnp.zeros((C, PAIRS, 128), F32)
    matrix[...] = jnp.zeros((ROWS, 128), F32)
    slopes[...] = jnp.zeros((TALL, CELLS), F32)
    matrix[0:C, 0:C] = point_weight[...].astype(F32)
    loads[4].wait()

    def cast_step(c, carry):
        maps[c, :, :MODES] = weight[c].astype(F32).reshape(PAIRS, MODES)
        return carry

    lax.fori_loop(0, C, cast_step, 0)
    loads[5].wait()
    for p in range(PLANES):
        slopes[ROWS * p : ROWS * p + C, :] = cot[0, 0, p].astype(F32)
    for load in loads[6:]:
        load.wait()

    space_wait(0)
    line_up_planes(0)
    along_x(modes, None)
    row = kz_weight[me % 2, 0:1, :]

    def mix_step(j, carry):
        strip = strip_at(j)
        first, second = jnp.zeros((PAIRS, 128), F32), jnp.zeros((PAIRS, 128), F32)
        for c in range(C):
            weights = maps[c, :, strip]
            first = first + weights * modes[j, 2 * c : 2 * c + 1, :]
            second = second + weights * modes[j, 2 * c + 1 : 2 * c + 2, :]
        mixed[j] = (first - other(second)) * kz_weight[me % 2, 0:1, strip]
        return carry

    lax.fori_loop(0, 4, mix_step, 0)
    back_along_x()
    planes_to_slabs(1, None)
    space_start(1)

    to_in = jnp.concatenate([turn(matrix[...], ROWS * p) for p in range(PLANES)], axis=0)[:, :TALL].astype(BF16)
    here = lax.broadcasted_iota(jnp.int32, (ROWS, C), 0) == lax.broadcasted_iota(jnp.int32, (ROWS, C), 1)
    bias = jnp.sum(jnp.where(here, bias_term[...], 0.0), axis=1, keepdims=True)
    bias = jnp.concatenate([bias] * PLANES, axis=0)
    for n in range(9):
        columns = slice(256 * n, 256 * n + 256)
        grads[:, columns] = bias + lax.dot_general(
            to_in, values[:, columns].astype(BF16), (((0,), (0,)), ((), ())), preferred_element_type=F32
        )
    space_wait(1)
    for r in far_first:
        modes_copy(r).start()
    all_modes[home] = modes[x_pos]
    owners_to_slab(1)

    full = lined[...]
    rate = math.sqrt(2.0 / math.pi)
    bias_sum = jnp.zeros((TALL, 1), F32)
    for n in range(9):
        columns = slice(256 * n, 256 * n + 256)
        pre = times(full, inv[n, 0], inv[n, 1]) + grads[:, columns]
        square = pre * pre
        bend = jnp.tanh(rate * (pre + 0.044715 * (square * pre)))
        half = 0.5 * (1.0 + bend)
        slope = half + 0.5 * pre * (1.0 - bend * bend) * (rate * (1.0 + 3 * 0.044715 * square))
        active = half * pre
        for p in range(PLANES):
            out_vmem[0, 0, p, :, columns] = active[ROWS * p : ROWS * p + C].astype(BF16)
        slope = slope * slopes[:, columns]
        grads[:, columns] = slope
        bias_sum = bias_sum + jnp.sum(slope, axis=1, keepdims=True)

    full = grads[...]
    for n in range(3):
        spectra[:, 256 * n : 256 * n + 256] = times(full, fwd[n, 0], fwd[n, 1])
    bias_own = bias_sum[:C] + bias_sum[ROWS : ROWS + C] + bias_sum[2 * ROWS : 2 * ROWS + C]
    slab_to_owners(2, jnp.where(lane == 108, bias_own, 0.0))
    space_start(2)

    point = jnp.zeros((ROWS, ROWS), F32)
    last = (((1,), (1,)), ((), ()))
    for p in range(PLANES):
        field = values[ROWS * p : ROWS * p + ROWS, :].astype(BF16)
        slope = grads[ROWS * p : ROWS * p + ROWS, :]
        high = slope.astype(BF16)
        low = (slope - high.astype(F32)).astype(BF16)
        point = point + lax.dot_general(field, high, last, preferred_element_type=F32)
        point = point + lax.dot_general(field, low, last, preferred_element_type=F32)
    point = jnp.concatenate([point[:C], jnp.zeros((C, 128 - ROWS), F32)], axis=1)
    point = jnp.where(lane >= 108, turn(point, 108), 0.0)
    for n in range(9):
        columns = slice(256 * n, 256 * n + 256)
        slope = grads[:, columns]
        high = slope.astype(BF16)
        low = (slope - high.astype(F32)).astype(BF16)
        values[:, columns] = jnp.dot(to_in, high, preferred_element_type=F32) + jnp.dot(
            to_in, low, preferred_element_type=F32
        )

    space_wait(2)
    line_up_planes(2)
    along_x(grad_modes, row)
    for r in far_first:
        grads_copy(r).start()
    grads_own.start()

    def grad_step(j, carry):
        strip = strip_at(j)
        slope = grad_modes[j]
        crossed = other(slope)
        for c in range(C):
            weights = maps[c, :, strip]
            mixed[j, 2 * c : 2 * c + 1, :] = jnp.sum(weights * slope, axis=0, keepdims=True)
            mixed[j, 2 * c + 1 : 2 * c + 2, :] = jnp.sum(weights * crossed, axis=0, keepdims=True)
        return carry

    lax.fori_loop(0, 4, grad_step, 0)
    back_along_x()
    planes_to_slabs(3, point)
    space_start(3)

    partial_pairs = partial.reshape(C, 8, 2, 128)
    own_pairs = own_sum.reshape(10, 8, 2, 128)
    blocks = gathered.reshape(4, C, C, 2, 128)
    for r in far_first:
        modes_copy(r).wait()
        grads_copy(r).wait()
    grads_own.wait()

    def part_step(i, carry):
        c = (i + 10 * (1 - core)) % C
        first, second = jnp.zeros((16, 128), F32), jnp.zeros((16, 128), F32)
        for b in range(16):
            slope = all_grads[b]
            first = first + all_modes[b, pl.ds(2 * c, 1), :] * slope
            second = second + all_modes[b, pl.ds(2 * c + 1, 1), :] * slope
        partial[c] = first + other(second)
        return carry

    core_sum = pltpu.make_async_remote_copy(
        src_ref=partial_pairs.at[pl.ds(10 * (1 - core), 10), 0:5],
        dst_ref=landed.reshape(10, 8, 2, 128).at[:, 0:5],
        send_sem=dp_send.at[2, 0], recv_sem=dp_recv.at[2, 0],
        device_id=(z_hi * 8 + x_pos * 2 + 1 - core, me), device_id_type=MESH,
    )
    lax.fori_loop(0, 10, part_step, 0)
    core_sum.start()
    lax.fori_loop(10, 20, part_step, 0)
    core_sum.wait()
    for j in range(10):
        own_sum[j] = partial[10 * core + j] + landed[j]

    def first_part(strip, k):
        return blocks.at[strip, pl.ds(10 * core, SPLIT), pl.ds((z_hi - k) % 4 * 5, 5)]

    def second_part(strip, k):
        return blocks.at[strip, pl.ds(10 * core + SPLIT, 10 - SPLIT), pl.ds((z_hi - k) % 4 * 5, 5)]

    own_first = own_pairs.at[0:SPLIT, 0:5]
    own_second = own_pairs.at[SPLIT:10, 0:5]
    keep = pltpu.make_async_copy(
        own_pairs.at[:, 0:5], blocks.at[x_pos, pl.ds(10 * core, 10), pl.ds(5 * z_hi, 5)], local_sem.at[1]
    )

    def to_z(source, block, send_at, recv_at, r):
        return pltpu.make_async_remote_copy(
            src_ref=source, dst_ref=block, send_sem=send_at, recv_sem=recv_at,
            device_id=((z_hi + r) % 4 * 8 + eight, me), device_id_type=MESH,
        )

    def to_x(source, block, send_at, recv_at, r):
        return pltpu.make_async_remote_copy(
            src_ref=source, dst_ref=block, send_sem=send_at, recv_sem=recv_at,
            device_id=(z_hi * 8 + (x_pos + r) % 4 * 2 + core, me), device_id_type=MESH,
        )

    def z_copy(r):
        return to_z(own_first, first_part(x_pos, 0), dp_send.at[4, r], dp_recv.at[4, r], r)

    def x_copy(k, r):
        block = first_part(x_pos, k)
        return to_x(own_first if k == 0 else block, block, x_send.at[k, r], x_recv.at[k, r], r)

    def x_first(r):
        return to_x(own_second, second_part(x_pos, 0), dp_send.at[6, r], dp_recv.at[6, r], r)

    def z_second(r):
        block = blocks.at[:, pl.ds(10 * core + SPLIT, 10 - SPLIT), pl.ds(5 * z_hi, 5)]
        return to_z(block, block, z_send.at[r], z_recv.at[r], r)

    def core_copy(k):
        block = blocks.at[:, pl.ds(10 * core, 10), pl.ds((z_hi - k) % 4 * 5, 5)]
        return pltpu.make_async_remote_copy(
            src_ref=block, dst_ref=block,
            send_sem=dp_send.at[7, k], recv_sem=dp_recv.at[7, k],
            device_id=(z_hi * 8 + x_pos * 2 + 1 - core, me), device_id_type=MESH,
        )

    keep.start()
    for r in (2, 1, 3):
        x_first(r).start()
    for r in (2, 1, 3):
        z_copy(r).start()
    for r in (2, 1, 3):
        x_copy(0, r).start()

    bias_total = jnp.zeros((C, 128), F32)
    for s in range(SLABS):
        bias_total = bias_total + recv[2, s]
    space_wait(3)
    owners_to_slab(3)
    point_total = jnp.zeros((C, 128), F32)
    for s in range(SLABS):
        point_total = point_total + recv[3, s]
    sums8[eight] = jnp.where(lane >= 108, point_total, jnp.where(lane == 0, turn(bias_total, 20), 0.0))

    def eight_copy(r):
        to = (eight + r) % 8
        return pltpu.make_async_remote_copy(
            src_ref=sums8.at[eight], dst_ref=sums8.at[eight],
            send_sem=dp_send.at[3, r], recv_sem=dp_recv.at[3, r],
            device_id=(z_hi * 8 + to, me), device_id_type=MESH,
        )

    for r in range(1, 8):
        eight_copy(r).start()

    keep.wait()
    for r in (1, 3, 2):
        x_first(r).wait_recv()
    for r in (2, 1, 3):
        z_second(r).start()
    full = lined[...]
    for n in range(9):
        columns = slice(256 * n, 256 * n + 256)
        result = times(full, inv[n, 0], inv[n, 1]) + values[:, columns]
        for p in range(PLANES):
            grad_vmem[0, 0, p, :, columns] = result[ROWS * p : ROWS * p + C].astype(BF16)

    for k in (1, 3):
        z_copy(k).wait_recv()
        for r in (2, 1, 3):
            x_copy(k, r).start()

    for r in range(1, 8):
        eight_copy(r).wait()
    total = sums8[0]
    for b in range(1, 8):
        total = total + sums8[b]
    sums4[z_hi] = total

    def four_copy(r):
        to = (z_hi + r) % 4
        return pltpu.make_async_remote_copy(
            src_ref=sums4.at[z_hi], dst_ref=sums4.at[z_hi],
            send_sem=dp_send.at[5, r], recv_sem=dp_recv.at[5, r],
            device_id=(to * 8 + eight, me), device_id_type=MESH,
        )

    for r in range(1, 4):
        four_copy(r).start()
    z_copy(2).wait_recv()
    for r in (2, 1, 3):
        x_copy(2, r).start()
    order = (0, 1, 3, 2)
    for k in order:
        for r in range(1, 4):
            x_copy(k, r).wait_recv()
        if k != 0:
            z_second(k).wait_recv()
        core_copy(k).start()
    for r in range(1, 4):
        four_copy(r).wait()
    total = turn(sums4[0] + sums4[1] + sums4[2] + sums4[3], 20)
    sums_ref[0:C, :] = total
    square = lax.broadcasted_iota(jnp.int32, (C, 128), 0) == lane
    sums_ref[C : C + 1, :] = jnp.sum(jnp.where(square, total[:, C : C + 1], 0.0), axis=0, keepdims=True)
    for r in range(1, 4):
        z_copy(r).wait_send()
        x_first(r).wait_send()
        z_second(r).wait_send()
        for k in range(4):
            x_copy(k, r).wait_send()
    for k in order:
        core_copy(k).wait()


def results(out_from, grad_from, spec_from, sums, out_to, grad_to, spec_to, point_to, bias_to, sem):
    copies = []
    strips = spec_from.reshape(4, C, C, 2, 128)
    for j in range(4):
        for k in range(4):
            rows = pl.ds(5 * k, 5)
            copies.append(
                pltpu.make_async_copy(
                    strips.at[j, rows], spec_to.at[rows, :, :, 128 * j : 128 * j + 128], sem.at[4 * j + k]
                )
            )
    for p in range(PLANES):
        copies.append(pltpu.make_async_copy(out_from.at[0, 0, p], out_to.at[0, 0, p], sem.at[16 + p]))
        copies.append(pltpu.make_async_copy(grad_from.at[0, 0, p], grad_to.at[0, 0, p], sem.at[19 + p]))
    for copy in copies:
        copy.start()
    point_to[...] = sums[0:C, 0:C]
    bias_to[...] = sums[C : C + 1, 0:C]
    for copy in copies:
        copy.wait()


def on_device(wake_field, spec_weight, point_weight, bias_term, cotangent):
    forward, inverse, x_two, x_inverse, kz_weight = tables()
    weight = spec_weight.transpose(1, 2, 0, 3)
    anywhere = pl.BlockSpec(memory_space=pl.ANY)
    inside = pl.BlockSpec(memory_space=pltpu.VMEM)
    field = wake_field.shape
    output_field, grad_field, grad_spec, sums = pl.pallas_call(
        kernel,
        out_shape=(
            pltpu.VMEM(field, BF16),
            pltpu.VMEM(field, BF16),
            pltpu.VMEM((4, C, PAIRS, 128), F32),
            pltpu.VMEM((ROWS, 128), F32),
        ),
        in_specs=[anywhere] * 3 + [inside] * 3 + [anywhere] * 4,
        out_specs=(inside, inside, inside, inside),
        scratch_shapes=[
            pltpu.VMEM(field, BF16),
            pltpu.VMEM(field, BF16),
            pltpu.VMEM(weight.shape, BF16),
            pltpu.VMEM(forward.shape, BF16),
            pltpu.VMEM(inverse.shape, BF16),
            pltpu.VMEM(x_two.shape, BF16),
            pltpu.VMEM(x_inverse.shape, BF16),
            pltpu.VMEM((TALL, CELLS), F32),
            pltpu.VMEM((TALL, CELLS), F32),
            pltpu.VMEM((C, PAIRS, 512), F32),
            pltpu.VMEM((TALL, WIDE), F32),
            pltpu.VMEM((TALL, WIDE), F32),
            pltpu.VMEM((TALL, CELLS), F32),
            pltpu.VMEM((TALL, WIDE), F32),
            pltpu.VMEM((TALL, 512), F32),
            pltpu.VMEM((4, PAIRS, 128), F32),
            pltpu.VMEM((4, PAIRS, 128), F32),
            pltpu.VMEM((4, PAIRS, 128), F32),
            pltpu.VMEM((ROWS, 128), F32),
            pltpu.VMEM((4, SLABS, C, 128), F32),
            pltpu.VMEM((4, SLABS, C, 128), F32),
            pltpu.VMEM((16, PAIRS, 128), F32),
            pltpu.VMEM((16, 16, 128), F32),
            pltpu.VMEM((C, 16, 128), F32),
            pltpu.VMEM((10, 16, 128), F32),
            pltpu.VMEM((10, 16, 128), F32),
            pltpu.VMEM((8, C, 128), F32),
            pltpu.VMEM((4, C, 128), F32),
            pltpu.SemaphoreType.DMA((9,)),
            pltpu.SemaphoreType.DMA((2,)),
            pltpu.SemaphoreType.DMA((4, 16)),
            pltpu.SemaphoreType.DMA((4, 16)),
            pltpu.SemaphoreType.DMA((8, 16)),
            pltpu.SemaphoreType.DMA((8, 16)),
            pltpu.SemaphoreType.DMA((4, 4)),
            pltpu.SemaphoreType.DMA((4, 4)),
            pltpu.SemaphoreType.DMA((4,)),
            pltpu.SemaphoreType.DMA((4,)),
        ],
        compiler_params=pltpu.CompilerParams(
            collective_id=0, has_side_effects=True, vmem_limit_bytes=52 * 1024 * 1024
        ),
    )(wake_field, cotangent, weight, point_weight, bias_term[None], kz_weight, forward, inverse, x_two, x_inverse)
    output_field, grad_field, grad_spec, grad_point, grad_bias = pl.pallas_call(
        results,
        out_shape=(
            jax.ShapeDtypeStruct(field, BF16),
            jax.ShapeDtypeStruct(field, BF16),
            jax.ShapeDtypeStruct((C, C, 2, 512), F32),
            jax.ShapeDtypeStruct((C, C), F32),
            jax.ShapeDtypeStruct((1, C), F32),
        ),
        in_specs=[inside] * 4,
        out_specs=(anywhere, anywhere, anywhere, inside, inside),
        scratch_shapes=[pltpu.SemaphoreType.DMA((22,))],
    )(*[pltpu.with_memory_space_constraint(array, pltpu.VMEM) for array in (output_field, grad_field, grad_spec, sums)])
    return (
        output_field,
        grad_field,
        grad_spec.transpose(2, 0, 1, 3)[..., :MODES],
        grad_point,
        grad_bias.reshape(C),
    )


def solution(mesh):
    placed = (
        P("dp", None, "space", None, None),
        P(None, None, None, "space"),
        P(),
        P(),
        P("dp", None, "space", None, None),
    )
    return jax.shard_map(
        on_device,
        mesh=mesh,
        in_specs=placed,
        out_specs=(
            P("dp", None, "space", None, None),
            P("dp", None, "space", None, None),
            P(None, None, None, "space"),
            P(),
            P(),
        ),
        check_vma=False,
    )
```
